32 devices in a mesh: dp: 4 (over x, core), seq: 8 (over z, y).
Axes of the slice: x: 2, y: 2, z: 4, core: 2. Of those that a mesh axis runs over, the one named last changes fastest.
Arguments:
- x_long: bfloat16 [4, 4, 4096, 768], P('dp', None, 'seq')
- x_short: bfloat16 [4, 8, 1, 512, 768], P('dp', 'seq')
- item_start: int32 [4, 4], P('dp'), may hold values from 0 to 7
- short_lengths: int32 [4, 8, 1], P('dp', 'seq'), may hold values from 128 to 512, as said below
- w_query: bfloat16 [768, 768], replicated, may hold values from -0.375 to 0.375
- w_key: bfloat16 [768, 768], replicated, may hold values from -0.375 to 0.375
- w_value: bfloat16 [768, 768], replicated, may hold values from -0.21875 to 0.21875
- w_out: bfloat16 [768, 768], replicated, may hold values from -0.4375 to 0.4375
- conv_taps: float32 [33, 12], replicated, may hold values from -2 to 2
- ln1_gain: float32 [768], replicated, may hold values from 0.25 to 1.75
- ln1_bias: float32 [768], replicated, may hold values from -3 to 3
- w_up: bfloat16 [768, 3072], replicated, may hold values from -0.21875 to 0.21875
- up_bias: float32 [3072], replicated, may hold values from -3 to 3
- w_down: bfloat16 [3072, 768], replicated, may hold values from -0.109375 to 0.109375
- down_bias: float32 [768], replicated, may hold values from -3 to 3
- ln2_gain: float32 [768], replicated, may hold values from 0.25 to 1.75
- ln2_bias: float32 [768], replicated, may hold values from -3 to 3
- cot_long: bfloat16 [4, 4, 4096, 768], P('dp', None, 'seq'), may hold values from -6 to 6
- cot_short: bfloat16 [4, 8, 1, 512, 768], P('dp', 'seq'), may hold values from -6 to 6
Outputs:
- out_long: bfloat16 [4, 4, 4096, 768], P('dp', None, 'seq')
- out_short: bfloat16 [4, 8, 1, 512, 768], P('dp', 'seq')
- grad_long: bfloat16 [4, 4, 4096, 768], P('dp', None, 'seq')
- grad_short: bfloat16 [4, 8, 1, 512, 768], P('dp', 'seq')
- grad_w_query: float32 [768, 768], P('seq')
- grad_w_key: float32 [768, 768], P('seq')
- grad_w_value: float32 [768, 768], P('seq')
- grad_w_out: float32 [768, 768], P('seq')
- grad_conv: float32 [33, 12], replicated
- grad_ln1_gain: float32 [768], replicated
- grad_ln1_bias: float32 [768], replicated
- grad_w_up: float32 [768, 3072], P('seq')
- grad_up_bias: float32 [3072], replicated
- grad_w_down: float32 [3072, 768], P('seq')
- grad_down_bias: float32 [768], replicated
- grad_ln2_gain: float32 [768], replicated
- grad_ln2_bias: float32 [768], replicated
The draws below stay inside these ranges and needn't reach their ends.
Inputs may be any that keep to these rules, and one draw needn't show every extreme that they name: `short_lengths`: each short item's length is a multiple of 64, and some short item has length 512 in every draw.
All inputs are finite; a program needn't handle non-finite values.
Results may differ from the reference program's by a relative error of at most 0.02.
The reference program's roundings to bfloat16 on the way count: a program that leaves them out, or rounds other values in their place, can miss the bound.
Values may be sent and summed in bfloat16 or wider, within the bound.
No kernel may reach another device: no remote copies, remote signals or barrier semaphores. Data moves between devices by JAX's collectives and lax.ppermute only.
A program may use at most 448 MiB of HBM per device.

```python
import jax
import jax.numpy as jnp
from jax import lax

D = 768
H = 12
HD = 64
FF = 3072
LM = 64
NS_STEPS = 6
HALF = 16
TAPS = 33
LONG = 4096
SHORT = 512
LONGS = 4
SHORTS = 1
N_DP = 4
N_SEQ = 8


def draw_x_long(key, part):
    key = jax.random.fold_in(key, 11)
    rough_key, coarse_key = jax.random.split(key)
    seg_len = LONG // LM
    rough = jax.random.normal(rough_key, (N_DP, LONGS, LONG, D), jnp.float32)
    coarse = jax.random.normal(coarse_key, (N_DP, LONGS, LM, 1, D), jnp.float32)
    coarse = jnp.broadcast_to(coarse, (N_DP, LONGS, LM, seg_len, D)).reshape(N_DP, LONGS, LONG, D)
    return (0.7 * rough + 0.7 * coarse).astype(jnp.bfloat16)


def draw_x_short(key, part):
    key = jax.random.fold_in(key, 17)
    rough_key, coarse_key = jax.random.split(key)
    block_len = SHORT // LM
    rough = jax.random.normal(rough_key, (N_DP, N_SEQ, SHORTS, SHORT, D), jnp.float32)
    coarse = jax.random.normal(coarse_key, (N_DP, N_SEQ, SHORTS, LM, 1, D), jnp.float32)
    coarse = jnp.broadcast_to(coarse, (N_DP, N_SEQ, SHORTS, LM, block_len, D)).reshape(N_DP, N_SEQ, SHORTS, SHORT, D)
    return (0.7 * rough + 0.7 * coarse).astype(jnp.bfloat16)


def draw_short_lengths(key, part):
    key = jax.random.fold_in(key, 23)
    pick_key, place_key = jax.random.split(key)
    blocks = SHORT // LM
    lowest = max(1, blocks // 4)
    item_total = N_DP * N_SEQ * SHORTS
    multiples = jax.random.randint(pick_key, (item_total,), lowest, blocks + 1)
    chosen = jax.random.randint(place_key, (), 0, item_total)
    multiples = jnp.where(jnp.arange(item_total) == chosen, blocks, multiples)
    return (multiples * LM).astype(jnp.int32).reshape(N_DP, N_SEQ, SHORTS)


def with_ends(drawn, own_key, smallest, largest):
    spot = [jax.random.randint(jax.random.fold_in(own_key, axis), (), 0, length) for axis, length in enumerate(drawn.shape)]
    longest = drawn.shape.index(max(drawn.shape))
    next_to = spot[:longest] + [(spot[longest] + 1) % drawn.shape[longest]] + spot[longest + 1:]
    return drawn.at[tuple(spot)].set(smallest).at[tuple(next_to)].set(largest)


def levels(own_key, extent, pieces, low, largest):
    def one(dim, shards_of):
        heights = jax.random.uniform(jax.random.fold_in(jax.random.fold_in(own_key, 6), dim), (shards_of,), jnp.float32, low / len(pieces), largest / len(pieces))
        return jnp.repeat(jnp.exp(heights), extent[dim] // shards_of).reshape((-1,) + (1,) * (len(extent) - dim - 1))

    level = one(*pieces[0])
    for cut in pieces[1:]:
        level = level * one(*cut)
    return level


def gaussian(rng, dims, width, reach, pieces=(), held_as=jnp.bfloat16):
    level = levels(rng, dims, pieces, -0.22, 0.18) if pieces else 1.0
    array = jax.random.normal(rng, dims, jnp.float32) * width * level
    return jnp.minimum(jnp.maximum(array, -reach), reach).astype(held_as)


def setup_inputs(seed: int = 0) -> dict:
    arg_keys = jax.random.split(jax.random.key(seed), 20)
    x_long = draw_x_long(jax.random.fold_in(arg_keys[19], 71), 0)
    x_short = draw_x_short(jax.random.fold_in(arg_keys[19], 71), 0)
    item_start = with_ends(jax.random.randint(arg_keys[2], (N_DP, LONGS), 0, N_SEQ), jax.random.fold_in(arg_keys[2], 1), 0, N_SEQ - 1).astype(jnp.int32)
    short_lengths = draw_short_lengths(jax.random.fold_in(arg_keys[19], 71), 0)
    w_query = gaussian(arg_keys[4], (D, D), (D // 3) ** -0.5, 0.375)
    w_key = gaussian(arg_keys[5], (D, D), (D // 3) ** -0.5, 0.375)
    w_value = gaussian(arg_keys[6], (D, D), D ** -0.5, 0.21875)
    w_out = gaussian(arg_keys[7], (D, D), (D // 4) ** -0.5, 0.4375)
    conv_taps = gaussian(arg_keys[8], (TAPS, H), (max(1, TAPS // 4)) ** -0.5, 2.0, (), jnp.float32)
    ln1_gain = jnp.clip(1.0 + 0.15 * jax.random.normal(arg_keys[9], (D,), jnp.float32), 0.25, 1.75)
    ln1_bias = gaussian(arg_keys[10], (D,), 0.3, 3.0, (), jnp.float32)
    w_up = gaussian(arg_keys[11], (D, FF), D ** -0.5, 0.21875)
    up_bias = gaussian(arg_keys[12], (FF,), 0.5, 3.0, (), jnp.float32)
    w_down = gaussian(arg_keys[13], (FF, D), FF ** -0.5, 0.109375)
    down_bias = gaussian(arg_keys[14], (D,), 0.3, 3.0, (), jnp.float32)
    ln2_gain = jnp.clip(1.0 + 0.15 * jax.random.normal(arg_keys[15], (D,), jnp.float32), 0.25, 1.75)
    ln2_bias = gaussian(arg_keys[16], (D,), 0.3, 3.0, (), jnp.float32)
    cot_long = gaussian(arg_keys[17], (N_DP, LONGS, LONG, D), 1.0, 6.0, ((0, 4), (2, 8)))
    cot_short = gaussian(arg_keys[18], (N_DP, N_SEQ, SHORTS, SHORT, D), 1.0, 6.0, ((0, 4), (1, 8)))
    return {"x_long": x_long, "x_short": x_short, "item_start": item_start, "short_lengths": short_lengths, "w_query": w_query, "w_key": w_key, "w_value": w_value, "w_out": w_out, "conv_taps": conv_taps, "ln1_gain": ln1_gain, "ln1_bias": ln1_bias, "w_up": w_up, "up_bias": up_bias, "w_down": w_down, "down_bias": down_bias, "ln2_gain": ln2_gain, "ln2_bias": ln2_bias, "cot_long": cot_long, "cot_short": cot_short}


PRECISE = lax.Precision.HIGHEST
EPSILON = 1e-05
MASKED_SCORE = -1e+30

@jax.custom_vjp
def low(v):
    return lax.optimization_barrier(v.astype(jnp.bfloat16)).astype(jnp.float32)

@jax.custom_vjp
def low_back(v):
    return v

def low_keep(v):
    return (low(v), None)

def low_pass(kept, grad):
    return (grad,)

def back_keep(v):
    return (v, None)

def back_low(kept, grad):
    return (low(grad),)
low.defvjp(low_keep, low_pass)
low_back.defvjp(back_keep, back_low)

def matmul_high(left, right):
    return jnp.dot(left, right, precision=PRECISE, preferred_element_type=jnp.float32)

def layer_norm(values, gain, bias):
    center = values - lax.optimization_barrier(jnp.mean(values, axis=-1, keepdims=True))
    spread = lax.optimization_barrier(jnp.mean(center * center, axis=-1, keepdims=True))
    return center * lax.rsqrt(spread + EPSILON) * gain + bias

def newton_inverse(matrix):
    eye_mat = jnp.eye(matrix.shape[-1], dtype=matrix.dtype)
    col_most = lax.optimization_barrier(jnp.max(lax.optimization_barrier(jnp.sum(matrix, axis=-2)), axis=-1))[..., None, None]
    row_most = lax.optimization_barrier(jnp.max(lax.optimization_barrier(jnp.sum(matrix, axis=-1)), axis=-1))[..., None, None]
    approx = jnp.swapaxes(matrix, -1, -2) / (col_most * row_most)
    for rounds in range(NS_STEPS):
        product = jnp.einsum('...ij,...jk->...ik', matrix, approx, precision=PRECISE)
        nested = 7.0 * eye_mat - product
        nested = 15.0 * eye_mat - jnp.einsum('...ij,...jk->...ik', product, nested, precision=PRECISE)
        nested = 13.0 * eye_mat - jnp.einsum('...ij,...jk->...ik', product, nested, precision=PRECISE)
        approx = 0.25 * jnp.einsum('...ij,...jk->...ik', approx, nested, precision=PRECISE)
    return approx

def block_forward(params, tokens, member, counts, valid):
    w_query, w_key, w_value, w_out, conv_taps, ln1_gain, ln1_bias, w_up, up_bias, w_down, down_bias, ln2_gain, ln2_bias = params
    row_count = tokens.shape[0]
    score_scale = HD ** (-0.5)
    query = low_back(low(matmul_high(tokens, w_query)))
    key = low_back(low(matmul_high(tokens, w_key)))
    value = low_back(low(matmul_high(tokens, w_value)))
    lm_query = low(matmul_high(member, query) / counts[:, None])
    lm_key = low(matmul_high(member, key) / counts[:, None])
    q_heads = query.reshape(row_count, H, HD)
    k_heads = key.reshape(row_count, H, HD)
    v_heads = value.reshape(row_count, H, HD)
    lq_heads = lm_query.reshape(LM, H, HD)
    lk_heads = lm_key.reshape(LM, H, HD)
    scores_f = low_back(score_scale * jnp.einsum('nhe,lhe->hnl', q_heads, lk_heads, precision=PRECISE))
    probs_f = low(jax.nn.softmax(scores_f, axis=-1))
    scores_a = score_scale * jnp.einsum('mhe,lhe->hml', lq_heads, lk_heads, precision=PRECISE)
    probs_a = jax.nn.softmax(scores_a, axis=-1)
    scores_b = low_back(score_scale * jnp.einsum('lhe,nhe->hln', lq_heads, k_heads, precision=PRECISE))
    scores_b = jnp.where(valid[None, None, :] > 0, scores_b, MASKED_SCORE)
    probs_b = low(jax.nn.softmax(scores_b, axis=-1))
    mixed = low_back(jnp.einsum('hln,nhe->hle', probs_b, v_heads, precision=PRECISE))
    inverse = newton_inverse(probs_a)
    lm_out = low(jnp.einsum('hlm,hme->hle', inverse, mixed, precision=PRECISE))
    attended = jnp.einsum('hnl,hle->nhe', probs_f, lm_out, precision=PRECISE)
    masked_v = v_heads * valid[:, None, None]
    padded = jnp.pad(masked_v, ((HALF, HALF), (0, 0), (0, 0)))
    conv_sum = jnp.zeros((row_count, H, HD), jnp.float32)
    for offset in range(2 * HALF + 1):
        conv_sum = conv_sum + conv_taps[offset][None, :, None] * padded[offset:offset + row_count]
    context = low_back(low((attended + conv_sum).reshape(row_count, D)))
    attn_out = low_back(matmul_high(context, w_out))
    hidden = low(layer_norm(tokens + attn_out, ln1_gain, ln1_bias))
    pre_act = low_back(matmul_high(hidden, w_up) + up_bias)
    active = low(jax.nn.gelu(pre_act, approximate=False))
    branch = low_back(matmul_high(active, w_down) + down_bias)
    return layer_norm(hidden + branch, ln2_gain, ln2_bias)

def reference(x_long, x_short, item_start, short_lengths, w_query, w_key, w_value, w_out, conv_taps, ln1_gain, ln1_bias, w_up, up_bias, w_down, down_bias, ln2_gain, ln2_bias, cot_long, cot_short):
    params = tuple((weight.astype(jnp.float32) for weight in (w_query, w_key, w_value, w_out, conv_taps, ln1_gain, ln1_bias, w_up, up_bias, w_down, down_bias, ln2_gain, ln2_bias)))
    seg_len = LONG // LM
    long_member = (jnp.arange(LONG, dtype=jnp.int32)[None, :] // seg_len == jnp.arange(LM, dtype=jnp.int32)[:, None]).astype(jnp.float32)
    long_counts = jnp.full((LM,), float(seg_len), jnp.float32)
    long_valid = jnp.ones((LONG,), jnp.float32)
    shift_rows = item_start.reshape(-1).astype(jnp.int32) * (LONG // N_SEQ)
    long_flat = x_long.astype(jnp.float32).reshape(N_DP * LONGS, LONG, D)
    short_flat = x_short.astype(jnp.float32).reshape(N_DP * N_SEQ * SHORTS, SHORT, D)
    lengths = short_lengths.reshape(-1).astype(jnp.int32)

    def forward(params, long_in, short_in):
        block = jax.checkpoint(block_forward)

        def long_step(carry, item):
            tokens, shift = item
            ordered = jnp.roll(tokens, -shift, axis=0)
            result = block(params, ordered, long_member, long_counts, long_valid)
            return (carry, jnp.roll(result, shift, axis=0))

        def short_step(carry, item):
            tokens, length = item
            seg_short = length // LM
            positions = jnp.arange(SHORT, dtype=jnp.int32)
            valid = positions < length
            member = ((positions[None, :] // seg_short == jnp.arange(LM, dtype=jnp.int32)[:, None]) & valid[None, :]).astype(jnp.float32)
            counts = jnp.ones((LM,), jnp.float32) * seg_short.astype(jnp.float32)
            return (carry, block(params, tokens, member, counts, valid.astype(jnp.float32)))
        zero_carry = jnp.zeros((), jnp.float32)
        _, long_out = lax.scan(long_step, zero_carry, (long_in, shift_rows))
        _, short_out = lax.scan(short_step, zero_carry, (short_in, lengths))
        return (long_out, short_out)
    outputs, pullback = jax.vjp(forward, params, long_flat, short_flat)
    grad_params, grad_long_in, grad_short_in = pullback((cot_long.astype(jnp.float32).reshape(long_flat.shape), cot_short.astype(jnp.float32).reshape(short_flat.shape)))
    return (outputs[0].reshape(x_long.shape).astype(jnp.bfloat16), outputs[1].reshape(x_short.shape).astype(jnp.bfloat16), grad_long_in.reshape(x_long.shape).astype(jnp.bfloat16), grad_short_in.reshape(x_short.shape).astype(jnp.bfloat16), grad_params[0], grad_params[1], grad_params[2], grad_params[3], grad_params[4], grad_params[5], grad_params[6], grad_params[7], grad_params[8], grad_params[9], grad_params[10], grad_params[11], grad_params[12])
```

```python
import functools

import jax
import jax.numpy as jnp
from jax import lax
from jax.experimental import pallas as pl
from jax.experimental.pallas import tpu as pltpu
from jax.sharding import PartitionSpec as P

D = 768
H = 12
HD = 64
FF = 3072
LM = 64
NS_STEPS = 6
HALF = 16
TAPS = 33
LONG = 4096
GROUP = 256
EPSILON = 1e-05
MASKED_SCORE = -1e30
SCALE = 0.125
VMEM_BYTES = 63 * 1024 * 1024

f32 = jnp.float32
bf = jnp.bfloat16
sds = jax.ShapeDtypeStruct


def dot(a, b, ca, cb):
    return lax.dot_general(a, b, (((ca,), (cb,)), ((), ())), preferred_element_type=f32)


def split(v):
    hi = v.astype(bf)
    return hi, (v - hi.astype(f32)).astype(bf)


def mm(a, b, ca=1, cb=0):
    ah, al = split(a)
    bh, bl = split(b)
    return dot(ah, bh, ca, cb) + (dot(ah, bl, ca, cb) + dot(al, bh, ca, cb))


def iota(shape, dim):
    return lax.broadcasted_iota(jnp.int32, shape, dim)


def spread_heads(block):
    tiled = jnp.concatenate([block.astype(f32)] * 4, axis=0)
    same = (iota((GROUP, GROUP), 0) // HD) == (iota((GROUP, GROUP), 1) // HD)
    return jnp.where(same, tiled, 0.0).astype(bf)


def pick_heads(full):
    head = iota((LM, GROUP), 1) // HD
    out = full[:LM]
    for h in range(1, 4):
        out = jnp.where(head == h, full[h * LM : (h + 1) * LM], out)
    return out


def lanes_of(columns):
    n = columns[0].shape[0]
    lane = iota((n, 128), 1)
    wide = jnp.zeros((n, 128), f32)
    for k, col in enumerate(columns):
        wide = jnp.where(lane == k, col, wide)
    return wide.T[:8]


def three_parts(row):
    hi = row.astype(bf).astype(f32)
    mid = (row - hi).astype(bf).astype(f32)
    low = row - hi - mid
    r = iota((16, row.shape[1]), 0)
    return jnp.where(r == 0, hi, jnp.where(r == 1, mid, jnp.where(r == 2, low, 0.0))).astype(bf)


def from_parts(rows):
    v = rows.astype(f32)
    total = v[0:1] + v[1:2] + v[2:3]
    return jnp.broadcast_to(total, (8, total.shape[1])).T[:, 0:1]


def head_softmax(scores):
    rows = scores.shape[1]
    s3 = scores.reshape(4, LM, rows)
    e = jnp.exp(s3 - jnp.max(s3, axis=1, keepdims=True))
    return (e / jnp.sum(e, axis=1, keepdims=True)).reshape(GROUP, rows)


def params(vmem=VMEM_BYTES):
    return pltpu.CompilerParams(vmem_limit_bytes=vmem)


def cost(flops, nbytes, trans=0):
    return pl.CostEstimate(flops=int(flops), bytes_accessed=int(nbytes), transcendentals=int(trans))


SMEM_SPEC = pl.BlockSpec(memory_space=pltpu.SMEM)


def const_spec(shape):
    return pl.BlockSpec(shape, lambda i: tuple(0 for _ in shape), pipeline_mode=pl.Buffered(1))


def qkv_kernel(n_long, x_l, x_s, wq, wk, wv, q_l, k_l, v_l, q_s, k_s, v_s, w_t):
    i = pl.program_id(0)

    @pl.when(i == 0)
    def _():
        for j, w in enumerate((wq, wk, wv)):
            w_t[j] = w[...].T

    x = jnp.where(i < n_long, x_l[...], x_s[...])
    made = [dot(w_t[j], x, 1, 1).astype(bf) for j in range(3)]

    @pl.when(i < n_long)
    def _():
        for ref, v in zip((q_l, k_l, v_l), made):
            ref[...] = v

    @pl.when(i >= n_long)
    def _():
        for ref, v in zip((q_s, k_s, v_s), made):
            ref[...] = v


def qkv(x_l, x_s, wq, wk, wv, tile=512):
    nl, ns = x_l.shape[0] // tile, x_s.shape[0] // tile
    long_at = lambda i: jnp.minimum(i, nl - 1)
    short_at = lambda i: jnp.maximum(i - nl, 0)
    row = lambda f: pl.BlockSpec((tile, D), lambda i: (f(i), 0))
    col = lambda f: pl.BlockSpec((D, tile), lambda i: (0, f(i)))
    tl, ts = x_l.shape[0], x_s.shape[0]
    return pl.pallas_call(
        functools.partial(qkv_kernel, nl),
        grid=(nl + ns,),
        in_specs=[row(long_at), row(short_at)] + [const_spec((D, D))] * 3,
        out_specs=[col(long_at)] * 3 + [col(short_at)] * 3,
        out_shape=[sds((D, tl), bf)] * 3 + [sds((D, ts), bf)] * 3,
        scratch_shapes=[pltpu.VMEM((3, D, D), bf)],
        compiler_params=params(),
        cost_estimate=cost(6 * (tl + ts) * D * D, 8 * (tl + ts) * D),
        name="qkv",
    )(x_l, x_s, wq, wk, wv)


def short_member(length, rows):
    seg = length // LM
    lm = iota((LM, rows), 0)
    pos = iota((LM, rows), 1)
    return ((pos >= lm * seg) & (pos < (lm + 1) * seg)).astype(f32)


def short_marks_kernel(length, q, k, lq, lk):
    member = short_member(length[0], q.shape[1]).astype(bf)
    count = (length[0] // LM).astype(f32)
    lq[...] = (dot(member, q[...], 1, 1) / count).astype(bf)
    lk[...] = (dot(member, k[...], 1, 1) / count).astype(bf)


def short_marks(length, q, k):
    return pl.pallas_call(
        short_marks_kernel,
        in_specs=[SMEM_SPEC] + [pl.BlockSpec(memory_space=pltpu.VMEM)] * 2,
        out_shape=[sds((LM, D), bf)] * 2,
        compiler_params=params(),
        cost_estimate=cost(1e8, 2e6),
        name="short_marks",
    )(length, q, k)


def stats_kernel(masked, units, length, lq, k, v, msg):
    rows = k.shape[1]
    sums, stats = [], []
    for g in range(3):
        gs = slice(g * GROUP, (g + 1) * GROUP)
        scores = dot(spread_heads(lq[:, gs] * SCALE), k[gs, :], 1, 0)
        if masked:
            scores = jnp.where(iota((GROUP, rows), 1) < length[0], scores, MASKED_SCORE)
        most = jnp.max(scores, axis=1, keepdims=True)
        e = jnp.exp(scores - most)
        stats.append(lanes_of([most, jnp.sum(e, axis=1, keepdims=True)]))
        sums.append(pick_heads(dot(e.astype(bf), v[gs, :], 1, 1)))
    sums = jnp.concatenate(sums, axis=1)
    stats = jnp.concatenate(stats, axis=1)
    width = D // units
    for u in range(units):
        us = slice(u * width, (u + 1) * width)
        msg[u, :LM, :] = sums[:, us]
        msg[u, LM:, :] = stats[:, us]


def item_specs(rows):
    mark = pl.BlockSpec((LM, D), lambda i: (i, 0))
    tok = pl.BlockSpec((D, rows), lambda i: (0, i))
    return mark, tok


def stats(length, lq, k, v, items, units, masked):
    rows = k.shape[1] // items
    mark, tok = item_specs(rows)
    return pl.pallas_call(
        functools.partial(stats_kernel, masked, units),
        grid=(items,),
        in_specs=[SMEM_SPEC, mark, tok, tok],
        out_specs=pl.BlockSpec((units, LM + 8, D // units), lambda i: (i, 0, 0)),
        out_shape=sds((items * units, LM + 8, D // units), f32),
        compiler_params=params(),
        cost_estimate=cost(4 * items * rows * D * GROUP, 4 * items * rows * D, items * rows * D),
        name="stats",
    )(length, lq, k, v)


def eye():
    return jnp.where(iota((LM, LM), 0) == iota((LM, LM), 1), 1.0, 0.0).astype(f32)


def head_slices(count):
    return [slice(h * HD, (h + 1) * HD) for h in range(count)]


def mark_probs(q, k):
    s = SCALE * dot(q, k, 1, 1)
    e = jnp.exp(s - jnp.max(s, axis=-1, keepdims=True))
    return e / jnp.sum(e, axis=-1, keepdims=True)


def inverse_start(a):
    col = jnp.sum(a, axis=0, keepdims=True)
    row = jnp.sum(a, axis=1, keepdims=True)
    return col, row, jnp.max(col, axis=1, keepdims=True), jnp.max(row, axis=0, keepdims=True)


def inverse_steps(a_list, kept=None):
    ident = eye()
    z_list = []
    for a in a_list:
        _, _, cm, rm = inverse_start(a)
        z_list.append(a.T / (cm * rm))
    for _ in range(NS_STEPS):
        p_list = [mm(a, z) for a, z in zip(a_list, z_list)]
        t2 = [15.0 * ident - mm(p, 7.0 * ident - p) for p in p_list]
        t3 = [13.0 * ident - mm(p, t) for p, t in zip(p_list, t2)]
        if kept is not None:
            kept.append((z_list, p_list, t2, t3))
        z_list = [0.25 * mm(z, t) for z, t in zip(z_list, t3)]
    return z_list


def inverse_kernel(lq, lk, z_out):
    hs = head_slices(lq.shape[2] // HD)
    a_list = [mark_probs(lq[0, :, s], lk[0, :, s]) for s in hs]
    for s, z in zip(hs, inverse_steps(a_list)):
        z_out[0, :, s] = z


def inverse(lq, lk):
    units, _, width = lq.shape
    spec = pl.BlockSpec((1, LM, width), lambda i: (i, 0, 0))
    return pl.pallas_call(
        inverse_kernel,
        grid=(units,),
        in_specs=[spec, spec],
        out_specs=spec,
        out_shape=sds((units, LM, width), f32),
        compiler_params=params(),
        cost_estimate=cost(units * (width // HD) * 24 * 3 * 2 * 64**3 * 16, 1e6),
        name="inverse",
    )(lq, lk)


def combine_kernel(senders, msg, z, out, bv_out):
    width = z.shape[2]
    most = jnp.concatenate([msg[0, d, LM : LM + 1, :] for d in range(senders)], axis=0)
    part = jnp.concatenate([msg[0, d, LM + 1 : LM + 2, :] for d in range(senders)], axis=0)
    top = jnp.max(most, axis=0, keepdims=True)
    e = jnp.exp(most - top)
    total = jnp.sum(part * e, axis=0, keepdims=True)
    weight = e / total
    if senders < 8:
        weight = jnp.concatenate([weight] + [jnp.zeros((8 - senders, width), f32)], axis=0)
    weight = weight.T
    w_all = []
    for s in head_slices(width // HD):
        bv = jnp.zeros((LM, HD), f32)
        for d in range(senders):
            bv = bv + weight[s, d : d + 1] * msg[0, d, :LM, s]
        bv_out[0, :, s] = bv
        w_all.append(mm(z[0, :, s], bv))
    out[0, :LM, :] = jnp.concatenate(w_all, axis=1).astype(bf)
    out[0, LM:, :] = three_parts(top + jnp.log(total))


def combine(msg, z):
    units, senders, _, width = msg.shape
    spec = pl.BlockSpec((1, LM, width), lambda i: (i, 0, 0))
    return pl.pallas_call(
        functools.partial(combine_kernel, senders),
        grid=(units,),
        in_specs=[pl.BlockSpec((1, senders, LM + 8, width), lambda i: (i, 0, 0, 0)), spec],
        out_specs=[pl.BlockSpec((1, LM + 16, width), lambda i: (i, 0, 0)), spec],
        out_shape=[sds((units, LM + 16, width), bf), sds((units, LM, width), f32)],
        compiler_params=params(),
        cost_estimate=cost(1e7, 2e6),
        name="combine",
    )(msg, z)


def joined(ref, units, rows):
    return jnp.concatenate([ref[u, rows, :] for u in range(units)], axis=1)


def mix_kernel(units, lk, w, q, conv, out):
    w_all = joined(w, units, slice(0, LM))
    for g in range(3):
        gs = slice(g * GROUP, (g + 1) * GROUP)
        probs = head_softmax(dot(spread_heads(lk[:, gs] * SCALE), q[gs, :], 1, 0)).astype(bf)
        out[gs, :] = (dot(spread_heads(w_all[:, gs]), probs, 0, 0) + conv[gs, :]).astype(bf)


def unit_spec(units, rows, width):
    return pl.BlockSpec((units, rows, width), lambda i: (i, 0, 0))


def mix(lk, w, q, conv, items, units):
    rows = q.shape[1] // items
    mark, tok = item_specs(rows)
    return pl.pallas_call(
        functools.partial(mix_kernel, units),
        grid=(items,),
        in_specs=[mark, unit_spec(units, LM + 16, D // units), tok, tok],
        out_specs=tok,
        out_shape=sds(q.shape, bf),
        compiler_params=params(),
        cost_estimate=cost(4 * items * rows * D * GROUP, 8 * items * rows * D, items * rows * D),
        name="mix",
    )(lk, w, q, conv)


def windows(body, rim, items, rows, limit):
    out = []
    for j in range(items):
        own = body[:, j * rows : (j + 1) * rows]
        if limit is not None:
            own = jnp.where(iota(own.shape, 1) < limit, own.astype(f32), 0.0).astype(bf)
        wide = jnp.concatenate(
            [rim[:, 32 * j : 32 * j + HALF], own, rim[:, 32 * j + HALF : 32 * j + 2 * HALF]], axis=1
        )
        for t in range(rows // 128):
            out.append(wide[:, t * 128 : t * 128 + 128 + 2 * HALF])
    return jnp.concatenate(out, axis=0)


def band(row):
    wide = jnp.concatenate([row, jnp.zeros((1, 128), f32)], axis=1)
    rolled = pltpu.roll(jnp.broadcast_to(wide, (128, 256)), 0, 1, stride=1, stride_axis=0)
    return split(rolled[:, : 128 + 2 * HALF])


def unstack(stacked, out, items, rows, limit=None):
    k = 0
    for j in range(items):
        for t in range(rows // 128):
            v = stacked[k * HD : (k + 1) * HD]
            if limit is not None:
                v = jnp.where(iota(v.shape, 1) + t * 128 < limit, v, 0.0)
            out[:, j * rows + t * 128 : j * rows + (t + 1) * 128] = v
            k += 1


def conv_kernel(items, rows, masked, length, v, rim, taps, out):
    limit = length[0] if masked else None
    wins = windows(v[...], rim[...], items, rows, limit)
    hi, lo = band(taps[0, 0:1, :])
    unstack(dot(wins, hi, 1, 1) + dot(wins, lo, 1, 1), out, items, rows)


def conv(length, v, rim, taps, items, masked):
    rows = v.shape[1] // items
    tok = pl.BlockSpec((HD, items * rows), lambda h: (h, 0))
    return pl.pallas_call(
        functools.partial(conv_kernel, items, rows, masked),
        grid=(H,),
        in_specs=[
            SMEM_SPEC,
            tok,
            pl.BlockSpec((HD, rim.shape[1]), lambda h: (h, 0)),
            pl.BlockSpec((1, 8, 128), lambda h: (h, 0, 0)),
        ],
        out_specs=tok,
        out_shape=sds(v.shape, f32),
        compiler_params=params(),
        cost_estimate=cost(4 * 512 * v.size, 6 * v.size),
        name="conv",
    )(length, v, rim, taps)


def conv_back_kernel(items, rows, masked, length, v, rim, up, up_rim, taps, out, tap_grad):
    limit = length[0] if masked else None
    wins = windows(v[...], rim[...], items, rows, limit)
    up_wins = windows(up[...], up_rim[...], items, rows, None)
    hi, lo = band(taps[0, 1:2, :])
    unstack(dot(up_wins, hi, 1, 1) + dot(up_wins, lo, 1, 1), out, items, rows, limit)
    ups = jnp.concatenate(
        [up[:, t * 128 : (t + 1) * 128] for t in range(items * rows // 128)], axis=0
    )
    gram = dot(ups, wins, 0, 0)
    flip = (iota((128, 128), 0) + iota((128, 128), 1) == 127).astype(f32).astype(bf)
    hi, lo = split(gram)
    gram = dot(flip, hi, 1, 0) + dot(flip, lo, 1, 0)
    gram = jnp.concatenate([gram, jnp.zeros((128, 256 - gram.shape[1]), f32)], axis=1)
    skewed = pltpu.roll(gram, 129, 1, stride=1, stride_axis=0)
    tap_grad[0] = jnp.broadcast_to(jnp.sum(skewed, axis=0, keepdims=True)[:, :128], (8, 128))


def conv_back(length, v, rim, up, up_rim, taps, items, masked):
    rows = v.shape[1] // items
    tok = pl.BlockSpec((HD, items * rows), lambda h: (h, 0))
    rim_spec = pl.BlockSpec((HD, rim.shape[1]), lambda h: (h, 0))
    tap_spec = pl.BlockSpec((1, 8, 128), lambda h: (h, 0, 0))
    return pl.pallas_call(
        functools.partial(conv_back_kernel, items, rows, masked),
        grid=(H,),
        in_specs=[SMEM_SPEC, tok, rim_spec, tok, rim_spec, tap_spec],
        out_specs=[tok, tap_spec],
        out_shape=[sds(v.shape, f32), sds((H, 8, 128), f32)],
        compiler_params=params(),
        cost_estimate=cost(6 * 512 * v.size, 8 * v.size),
        name="conv_back",
    )(length, v, rim, up, up_rim, taps)


def fold_rows(v):
    return jnp.sum(v.reshape(v.shape[0] // 8, 8, v.shape[1]), axis=0)


def gelu_parts(x):
    e = jnp.exp(x * x * (-0.5))
    t = pl.reciprocal(1.0 + jnp.abs(x) * (0.3275911 * 0.7071067811865476), approx=False)
    poly = t * (
        0.127414796 + t * (-0.142248368 + t * (0.7107068705 + t * (-0.7265760135 + t * 0.5307027145)))
    )
    tail = poly * e
    phi = jnp.where(x >= 0, 1.0 - tail, tail)
    return x * phi, phi + x * e * 0.3989422804014327


def put_bf16(pairs, stage, sem):
    pend = []
    for acc, dst in pairs:
        for c in range(0, acc.shape[1], D):
            slot = len(pend) % 2
            if len(pend) >= 2:
                pend[-2].wait()
            stage[slot] = acc[:, c : c + D].astype(bf)
            pend.append(pltpu.make_async_copy(stage.at[slot], dst.at[:, c : c + D], sem.at[slot]))
            pend[-1].start()
    pend[-2].wait()
    pend[-1].wait()


def dense_kernel(n_long, chunk, x_l, x_s, o_l, o_s, c_l, c_s, w_out, w_up, w_down, g1, b1, bu, bd, g2, b2,
                 out_l, out_s, dr_l, dr_s, do_l, do_s, gup, gdn, gout, small, small_up,
                 acc_up, acc_dn, acc_out, act, dact, accs, accu, stage, sem):
    i = pl.program_id(0)
    last = pl.num_programs(0) - 1
    is_long = i < n_long

    @pl.when(i == 0)
    def _():
        for ref in (acc_up, acc_dn, acc_out, accs, accu):
            ref[...] = jnp.zeros_like(ref)

    x = jnp.where(is_long, x_l[...], x_s[...]).astype(f32)
    o_t = jnp.where(is_long, o_l[...], o_s[...])
    r1 = x + dot(o_t, w_out[...], 0, 0)
    cen = r1 - jnp.mean(r1, axis=-1, keepdims=True)
    rstd1 = lax.rsqrt(jnp.mean(cen * cen, axis=-1, keepdims=True) + EPSILON)
    xh1 = cen * rstd1
    h1 = (xh1 * g1[...] + b1[...]).astype(bf)
    r2 = h1.astype(f32) + bd[...]
    for c in range(FF // chunk):
        cs = slice(c * chunk, (c + 1) * chunk)
        a, dg = gelu_parts(dot(h1, w_up[:, cs], 1, 0) + bu[:, cs])
        a = a.astype(bf)
        act[:, cs] = a
        dact[:, cs] = dg
        r2 = r2 + dot(a, w_down[cs, :], 1, 0)
    cen2 = r2 - jnp.mean(r2, axis=-1, keepdims=True)
    rstd2 = lax.rsqrt(jnp.mean(cen2 * cen2, axis=-1, keepdims=True) + EPSILON)
    xh2 = cen2 * rstd2
    out = (xh2 * g2[...] + b2[...]).astype(bf)
    g = jnp.where(is_long, c_l[...], c_s[...]).astype(f32)
    dxh = g * g2[...]
    dr2 = rstd2 * (
        dxh - jnp.mean(dxh, axis=-1, keepdims=True) - xh2 * jnp.mean(dxh * xh2, axis=-1, keepdims=True)
    )
    dz2 = dr2.astype(bf)
    accs[4] += fold_rows(g * xh2)
    accs[5] += fold_rows(g)
    accs[2] += fold_rows(dz2.astype(f32))
    dz2_t = dz2.T
    h1_t = h1.T
    dh1 = dr2
    for c in range(FF // chunk):
        cs = slice(c * chunk, (c + 1) * chunk)
        dp1 = (dot(dz2, w_down[cs, :], 1, 1) * dact[:, cs]).astype(bf)
        accu[:, cs] += fold_rows(dp1.astype(f32))
        dh1 = dh1 + dot(dp1, w_up[:, cs], 1, 1)
        acc_up[:, cs] += dot(h1_t, dp1, 1, 0)
        acc_dn[:, cs] += dot(dz2_t, act[:, cs], 1, 0)
    accs[0] += fold_rows(dh1 * xh1)
    accs[1] += fold_rows(dh1)
    dx = dh1 * g1[...]
    dr1 = rstd1 * (
        dx - jnp.mean(dx, axis=-1, keepdims=True) - xh1 * jnp.mean(dx * xh1, axis=-1, keepdims=True)
    )
    da1 = dr1.astype(bf)
    acc_out[...] += dot(o_t, da1, 1, 0)
    do_t = dot(w_out[...], da1, 1, 1).astype(bf)

    @pl.when(is_long)
    def _():
        out_l[...] = out
        dr_l[...] = dr1
        do_l[...] = do_t

    @pl.when(jnp.logical_not(is_long))
    def _():
        out_s[...] = out
        dr_s[...] = dr1
        do_s[...] = do_t

    @pl.when(i == last)
    def _():
        put_bf16(((acc_up, gup), (acc_dn, gdn), (acc_out, gout)), stage, sem)
        small[...] = jnp.sum(accs[...], axis=1)
        small_up[...] = jnp.sum(accu[...], axis=0, keepdims=True)


def dense(x_l, x_s, o_l, o_s, c_l, c_s, w_out, w_up, w_down, g1, b1, bu, bd, g2, b2, tile=256, chunk=768):
    nl, ns = x_l.shape[0] // tile, x_s.shape[0] // tile
    long_at = lambda i: jnp.minimum(i, nl - 1)
    short_at = lambda i: jnp.maximum(i - nl, 0)
    row = lambda f: pl.BlockSpec((tile, D), lambda i: (f(i), 0))
    col = lambda f: pl.BlockSpec((D, tile), lambda i: (0, f(i)))
    anywhere = pl.BlockSpec(memory_space=pl.ANY)
    tl, ts = x_l.shape[0], x_s.shape[0]
    vec = const_spec((1, D))
    return pl.pallas_call(
        functools.partial(dense_kernel, nl, chunk),
        grid=(nl + ns,),
        in_specs=[row(long_at), row(short_at), col(long_at), col(short_at), row(long_at), row(short_at)]
        + [const_spec((D, D)), const_spec((D, FF)), const_spec((FF, D))]
        + [vec, vec, const_spec((1, FF)), vec, vec, vec],
        out_specs=[row(long_at), row(short_at), row(long_at), row(short_at), col(long_at), col(short_at)]
        + [anywhere] * 3
        + [const_spec((6, D)), const_spec((1, FF))],
        out_shape=[sds((tl, D), bf), sds((ts, D), bf), sds((tl, D), f32), sds((ts, D), f32)]
        + [sds((D, tl), bf), sds((D, ts), bf), sds((D, FF), bf), sds((D, FF), bf), sds((D, D), bf)]
        + [sds((6, D), f32), sds((1, FF), f32)],
        scratch_shapes=[
            pltpu.VMEM((D, FF), f32),
            pltpu.VMEM((D, FF), f32),
            pltpu.VMEM((D, D), f32),
            pltpu.VMEM((tile, FF), bf),
            pltpu.VMEM((tile, FF), f32),
            pltpu.VMEM((6, 8, D), f32),
            pltpu.VMEM((8, FF), f32),
            pltpu.VMEM((2, D, D), bf),
            pltpu.SemaphoreType.DMA((2,)),
        ],
        compiler_params=params(),
        cost_estimate=cost(2 * (tl + ts) * (3 * D * D + 6 * D * FF), 60e6, (tl + ts) * FF),
        name="dense",
    )(x_l, x_s, o_l, o_s, c_l, c_s, w_out, w_up, w_down, g1, b1, bu, bd, g2, b2)


def back_f_kernel(units, lk, w, q, up, dw_out, dlk_out, dsf_out):
    w_all = joined(w, units, slice(0, LM))
    dws = []
    for g in range(3):
        gs = slice(g * GROUP, (g + 1) * GROUP)
        q_g, up_g = q[gs, :], up[gs, :]
        rows = q_g.shape[1]
        probs = head_softmax(dot(spread_heads(lk[:, gs] * SCALE), q_g, 1, 0))
        dws.append(pick_heads(dot(probs.astype(bf), up_g, 1, 1)))
        dprobs = dot(spread_heads(w_all[:, gs]), up_g, 1, 0)
        weighted = jnp.sum((probs * dprobs).reshape(4, LM, rows), axis=1, keepdims=True)
        dsf = probs * (dprobs.reshape(4, LM, rows) - weighted).reshape(GROUP, rows)
        dsf = dsf.astype(bf)
        dsf_out[gs, :] = dsf
        dlk_out[:, gs] = SCALE * pick_heads(dot(dsf, q_g, 1, 1))
    dws = jnp.concatenate(dws, axis=1)
    width = D // units
    for u in range(units):
        dw_out[u] = dws[:, u * width : (u + 1) * width]


def back_f(lk, w, q, up, items, units):
    rows = q.shape[1] // items
    mark, tok = item_specs(rows)
    width = D // units
    return pl.pallas_call(
        functools.partial(back_f_kernel, units),
        grid=(items,),
        in_specs=[mark, unit_spec(units, LM + 16, width), tok, tok],
        out_specs=[unit_spec(units, LM, width), mark, tok],
        out_shape=[sds((items * units, LM, width), f32), sds((items * LM, D), f32), sds(q.shape, bf)],
        compiler_params=params(),
        cost_estimate=cost(8 * items * rows * D * GROUP, 6 * items * rows * D, items * rows * D),
        name="back_f",
    )(lk, w, q, up)


def back_mix_kernel(senders, dw_in, z, bv, out, dw_out):
    width = z.shape[2]
    dw = dw_in[0, 0]
    for d in range(1, senders):
        dw = dw + dw_in[0, d]
    dw_out[0] = dw
    dbvs, dots = [], []
    for s in head_slices(width // HD):
        dbv = mm(z[0, :, s], dw[:, s], 0, 0).astype(bf)
        dots.append(jnp.sum(dbv.astype(f32) * bv[0, :, s], axis=1, keepdims=True))
        dbvs.append(dbv)
    out[0, :LM, :] = jnp.concatenate(dbvs, axis=1)
    out[0, LM:, :] = three_parts(lanes_of([jnp.concatenate(dots, axis=0)])[:1])


def back_mix(dw, z, bv):
    units, senders, _, width = dw.shape
    spec = pl.BlockSpec((1, LM, width), lambda i: (i, 0, 0))
    return pl.pallas_call(
        functools.partial(back_mix_kernel, senders),
        grid=(units,),
        in_specs=[pl.BlockSpec((1, senders, LM, width), lambda i: (i, 0, 0, 0)), spec, spec],
        out_specs=[pl.BlockSpec((1, LM + 16, width), lambda i: (i, 0, 0)), spec],
        out_shape=[sds((units, LM + 16, width), bf), sds((units, LM, width), f32)],
        compiler_params=params(),
        cost_estimate=cost(1e7, 2e6),
        name="back_mix",
    )(dw, z, bv)


def back_inverse_kernel(lq, lk, dw, bv, dlq_out, dlk_out):
    hs = head_slices(lq.shape[2] // HD)
    a_list = [mark_probs(lq[0, :, s], lk[0, :, s]) for s in hs]
    kept = []
    inverse_steps(a_list, kept)
    ident = eye()
    dz = [mm(dw[0, :, s], bv[0, :, s], 1, 1) for s in hs]
    da = [jnp.zeros((LM, LM), f32) for _ in hs]
    for z, p, t2, t3 in reversed(kept):
        dt3 = [0.25 * mm(zz, d, 0, 0) for zz, d in zip(z, dz)]
        dz = [0.25 * mm(d, t, 1, 1) for d, t in zip(dz, t3)]
        dp = [-mm(d, t, 1, 1) for d, t in zip(dt3, t2)]
        dt2 = [-mm(pp, d, 0, 0) for pp, d in zip(p, dt3)]
        dp = [x - mm(d, 7.0 * ident - pp, 1, 1) for x, d, pp in zip(dp, dt2, p)]
        dp = [x + mm(pp, d, 0, 0) for x, pp, d in zip(dp, p, dt2)]
        da = [x + mm(d, zz, 1, 1) for x, d, zz in zip(da, dp, z)]
        dz = [x + mm(a, d, 0, 0) for x, a, d in zip(dz, a_list, dp)]
    for s, a, g, d in zip(hs, a_list, da, dz):
        col, row, cm, rm = inverse_start(a)
        norm = cm * rm
        g = g + d.T / norm
        dnorm = -jnp.sum(jnp.sum(d.T * a, axis=1, keepdims=True), axis=0, keepdims=True) / (norm * norm)
        at_col = (col == cm).astype(f32)
        at_row = (row == rm).astype(f32)
        g = g + dnorm * rm * at_col / jnp.sum(at_col, axis=1, keepdims=True)
        g = g + dnorm * cm * at_row / jnp.sum(at_row, axis=0, keepdims=True)
        ds = a * (g - jnp.sum(a * g, axis=1, keepdims=True))
        dlq_out[0, :, s] = SCALE * mm(ds, lk[0, :, s].astype(f32))
        dlk_out[0, :, s] = SCALE * mm(ds, lq[0, :, s].astype(f32), 0, 0)


def back_inverse(lq, lk, dw, bv):
    units, _, width = lq.shape
    spec = pl.BlockSpec((1, LM, width), lambda i: (i, 0, 0))
    return pl.pallas_call(
        back_inverse_kernel,
        grid=(units,),
        in_specs=[spec] * 4,
        out_specs=[spec] * 2,
        out_shape=[sds((units, LM, width), f32)] * 2,
        compiler_params=params(),
        cost_estimate=cost(units * (width // HD) * 72 * 3 * 2 * 64**3 * 16, 2e6),
        name="back_inverse",
    )(lq, lk, dw, bv)


def back_b_kernel(masked, units, length, lq, w, dbv, k, v, dconv, dsb_out, dv_out, dlq_out):
    rows = k.shape[1]
    level = from_parts(joined(w, units, slice(LM, LM + 16)))
    dots = from_parts(joined(dbv, units, slice(LM, LM + 16)))
    dbv_all = joined(dbv, units, slice(0, LM))
    for g in range(3):
        gs = slice(g * GROUP, (g + 1) * GROUP)
        scores = dot(spread_heads(lq[:, gs] * SCALE), k[gs, :], 1, 0)
        if masked:
            scores = jnp.where(iota((GROUP, rows), 1) < length[0], scores, MASKED_SCORE)
        probs = jnp.exp(scores - level[gs])
        wide = spread_heads(dbv_all[:, gs])
        dsb = (probs * (dot(wide, v[gs, :], 1, 0) - dots[gs])).astype(bf)
        dsb_out[gs, :] = dsb
        dv_out[gs, :] = (dot(wide, probs.astype(bf), 0, 0) + dconv[gs, :]).astype(bf)
        dlq_out[:, gs] = SCALE * pick_heads(dot(dsb, k[gs, :], 1, 1))


def back_b(length, lq, w, dbv, k, v, dconv, items, units, masked):
    rows = k.shape[1] // items
    mark, tok = item_specs(rows)
    unit = unit_spec(units, LM + 16, D // units)
    return pl.pallas_call(
        functools.partial(back_b_kernel, masked, units),
        grid=(items,),
        in_specs=[SMEM_SPEC, mark, unit, unit, tok, tok, tok],
        out_specs=[tok, tok, mark],
        out_shape=[sds(k.shape, bf), sds(k.shape, bf), sds((items * LM, D), f32)],
        compiler_params=params(),
        cost_estimate=cost(10 * items * rows * D * GROUP, 12 * items * rows * D, items * rows * D),
        name="back_b",
    )(length, lq, w, dbv, k, v, dconv)


def final_part(member, x, dr, lq, lk, dsf, dsb, dv, sq, sk, wq, wk, wv, acc):
    member2 = jnp.concatenate([member, member], axis=0)
    x_t = x[...].T
    made = []
    for marks, scores, sums in ((lk, dsf, sq), (lq, dsb, sk)):
        hi, lo = split(sums[...])
        back = dot(jnp.concatenate([hi, lo], axis=0), member2, 0, 0)
        parts = []
        for g in range(3):
            gs = slice(g * GROUP, (g + 1) * GROUP)
            part = dot(spread_heads(marks[:, gs] * SCALE), scores[gs, :], 0, 0) + back[gs]
            parts.append(part.astype(bf).T)
        made.append(jnp.concatenate(parts, axis=1))
    made.append(dv[...].T)
    total = dr[...]
    for j, (grad, w) in enumerate(zip(made, (wq, wk, wv))):
        total = total + dot(grad, w[...], 1, 1)
        acc[j] += dot(x_t, grad, 1, 0)
    return total.astype(bf)


def final_kernel(n_long, length, x_l, dr_l, lq_l, lk_l, dsf_l, dsb_l, dv_l, sq_l, sk_l,
                 x_s, dr_s, lq_s, lk_s, dsf_s, dsb_s, dv_s, sq_s, sk_s, wq, wk, wv,
                 out_l, out_s, gq, gk, gv, acc, stage, sem):
    i = pl.program_id(0)

    @pl.when(i == 0)
    def _():
        acc[...] = jnp.zeros_like(acc)

    @pl.when(i < n_long)
    def _():
        count, rows = sq_l.shape[0], x_l.shape[0]
        member = (iota((count, rows), 1) // (LONG // LM) == iota((count, rows), 0)).astype(f32).astype(bf)
        out_l[...] = final_part(member, x_l, dr_l, lq_l, lk_l, dsf_l, dsb_l, dv_l, sq_l, sk_l, wq, wk, wv, acc)

    @pl.when(i >= n_long)
    def _():
        member = short_member(length[0], x_s.shape[0]).astype(bf)
        out_s[...] = final_part(member, x_s, dr_s, lq_s, lk_s, dsf_s, dsb_s, dv_s, sq_s, sk_s, wq, wk, wv, acc)
        put_bf16(((acc.at[0], gq), (acc.at[1], gk), (acc.at[2], gv)), stage, sem)


def final(length, long_args, short_args, weights, items):
    x_l, x_s = long_args[0], short_args[0]
    tl, ts = x_l.shape[0], x_s.shape[0]
    rows = tl // items
    marks_l = long_args[7].shape[0] // items
    at = lambda i: jnp.minimum(i, items - 1)

    def specs(n, r, marks, f):
        row = pl.BlockSpec((r, D), lambda i: (f(i), 0))
        mark = pl.BlockSpec((LM, D), lambda i: (f(i), 0))
        tok = pl.BlockSpec((D, r), lambda i: (0, f(i)))
        own = pl.BlockSpec((marks, D), lambda i: (f(i), 0))
        return [row, row, mark, mark, tok, tok, tok, own, own]

    anywhere = pl.BlockSpec(memory_space=pl.ANY)
    return pl.pallas_call(
        functools.partial(final_kernel, items),
        grid=(items + 1,),
        in_specs=[SMEM_SPEC]
        + specs(items, rows, marks_l, at)
        + specs(1, ts, LM, lambda i: 0)
        + [const_spec((D, D))] * 3,
        out_specs=[
            pl.BlockSpec((rows, D), lambda i: (at(i), 0)),
            pl.BlockSpec((ts, D), lambda i: (0, 0)),
        ]
        + [anywhere] * 3,
        out_shape=[sds((tl, D), bf), sds((ts, D), bf)] + [sds((D, D), bf)] * 3,
        scratch_shapes=[
            pltpu.VMEM((3, D, D), f32),
            pltpu.VMEM((2, D, D), bf),
            pltpu.SemaphoreType.DMA((2,)),
        ],
        compiler_params=params(),
        cost_estimate=cost(12 * (tl + ts) * D * D, 20 * (tl + ts) * D),
        name="final",
    )(length, *long_args, *short_args, *weights)


def swap(values, axis, bit):
    count = lax.axis_size(axis)
    return lax.ppermute(values, axis, [(i, i ^ bit) for i in range(count)])


def side(axis, bit):
    return (lax.axis_index(axis) // bit) % 2


def halve(values, dim, axis, bit):
    mine = side(axis, bit)
    keep = lax.dynamic_index_in_dim(values, mine, dim, keepdims=False)
    send = lax.dynamic_index_in_dim(values, 1 - mine, dim, keepdims=False)
    return keep.astype(f32) + swap(send.astype(bf), axis, bit).astype(f32)


def join(values, dim, axis, bit):
    mine = side(axis, bit)
    other = swap(values, axis, bit)
    return jnp.where(
        mine == 0,
        jnp.concatenate([values, other], axis=dim),
        jnp.concatenate([other, values], axis=dim),
    )


def is_small_mesh():
    return lax.axis_size("dp") == 4 and lax.axis_size("seq") == 8


def reduce_rows(grad, order):
    n = grad.shape[1]
    if not is_small_mesh():
        own = lax.psum_scatter(grad, "seq", scatter_dimension=0, tiled=True)
        return lax.psum(own.astype(f32), "dp")
    v = grad.reshape(2, 2, 2, 2, 48, n)
    v = halve(v, 3, "dp", 1).astype(bf)
    dims = ["z1", "z0", "y"]
    for step in order:
        if step == "x":
            v = halve(v.reshape(v.shape[:-1] + (2, n // 2)), v.ndim - 1, "dp", 2)
        else:
            dim = dims.index(step)
            dims.pop(dim)
            v = halve(v, dim, "seq", {"y": 1, "z0": 2, "z1": 4}[step])
        v = v.astype(bf)
    v = join(v, 1, "dp", 2)
    return join(v, 0, "dp", 1).astype(f32)


def reduce_columns(grad, order):
    if not is_small_mesh():
        own = lax.psum_scatter(grad, "seq", scatter_dimension=1, tiled=True)
        return lax.psum(own.astype(f32), "dp").T
    v = halve(grad.reshape(2, D // 2, FF), 0, "dp", 1).astype(bf)
    v = v.reshape(D // 2, 2, 2, 2, FF // 8)
    dims = ["z1", "z0", "y"]
    for step in order:
        if step == "x":
            v = halve(v.reshape((2, D // 4) + v.shape[1:]), 0, "dp", 2)
        else:
            dim = dims.index(step)
            dims.pop(dim)
            v = halve(v, dim + 1, "seq", {"y": 1, "z0": 2, "z1": 4}[step])
        v = v.astype(bf)
    v = join(v, 0, "dp", 2)
    return join(v, 0, "dp", 1).astype(f32).T


def sum_everywhere(values):
    if not is_small_mesh():
        return lax.psum(values, ("dp", "seq"))
    for axis, bit in (("dp", 1), ("dp", 2), ("seq", 1), ("seq", 2), ("seq", 4)):
        values = values + swap(values, axis, bit)
    return values


def gather(values):
    return lax.all_gather(values, "seq", axis=0)


def exchange(values):
    return lax.all_to_all(values, "seq", 0, 0, tiled=True)


def neighbours(first, last):
    count = lax.axis_size("seq")
    right = lax.ppermute(first, "seq", [((i + 1) % count, i) for i in range(count)])
    left = lax.ppermute(last, "seq", [(i, (i + 1) % count) for i in range(count)])
    return left, right


def pad_units(values, count):
    have = values.shape[0]
    if have == count:
        return values
    return jnp.concatenate([values, jnp.zeros((count - have,) + values.shape[1:], values.dtype)], axis=0)


def body(x_long, x_short, item_start, short_lengths, w_query, w_key, w_value, w_out, conv_taps, ln1_gain, ln1_bias,
         w_up, up_bias, w_down, down_bias, ln2_gain, ln2_bias, cot_long, cot_short):
    _, items, rows, _ = x_long.shape
    short_rows = x_short.shape[3]
    seg = LONG // LM
    own_marks = rows // seg
    n_seq = lax.axis_size("seq")
    me = lax.axis_index("seq")
    heads_each = next(h for h in (1, 2, 3, 4, 6, 12) if H % h == 0 and items * H // h <= n_seq and (h * HD) % 128 == 0)
    units = H // heads_each
    width = heads_each * HD
    owners = items * units

    x_l = x_long.reshape(items * rows, D)
    x_s = x_short.reshape(short_rows, D)
    length = short_lengths.reshape(1)
    no_length = jnp.zeros((1,), jnp.int32)

    x_mean = jnp.sum(x_long[0].reshape(items, own_marks, seg, D).astype(f32), axis=2) * (1.0 / seg)
    means = gather(x_mean)
    means = means.transpose(1, 0, 2, 3).reshape(items * LM, D)
    mean_hi, mean_lo = split(means)

    def marks_of(w):
        return (
            jnp.dot(mean_hi, w, preferred_element_type=f32) + jnp.dot(mean_lo, w, preferred_element_type=f32)
        ).astype(bf)

    lq_l, lk_l = marks_of(w_query), marks_of(w_key)

    place = (me - item_start[0]) % n_seq
    open_left = (place > 0)[:, None, None]
    open_right = (place < n_seq - 1)[:, None, None]

    def rims(left, right):
        return jnp.concatenate(
            [jnp.where(open_left, left, jnp.zeros_like(left)), jnp.where(open_right, right, jnp.zeros_like(right))], axis=1
        ).reshape(items * 2 * HALF, D)

    x_rim = rims(*neighbours(x_long[0, :, :HALF], x_long[0, :, rows - HALF :]))
    v_rim = jnp.einsum("ke,nk->en", w_value, x_rim, preferred_element_type=f32).astype(bf)
    no_rim = jnp.zeros((D, 2 * HALF), bf)

    tap_rows = jnp.stack([conv_taps.T, conv_taps[::-1].T], axis=1)
    tap_rows = jnp.pad(tap_rows, ((0, 0), (0, 6), (0, 128 - TAPS)))

    q_l, k_l, v_l, q_s, k_s, v_s = qkv(x_l, x_s, w_query, w_key, w_value)
    lq_s, lk_s = short_marks(length, q_s, k_s)

    msg_l = stats(no_length, lq_l, k_l, v_l, items, units, False)
    msg_s = stats(length, lq_s, k_s, v_s, 1, units, True)
    got_l = exchange(pad_units(msg_l, n_seq))

    mine = jnp.minimum(me, owners - 1)

    def my_unit(marks):
        return lax.dynamic_slice(
            marks, ((mine // units) * LM, (mine % units) * width), (LM, width)
        )

    def unit_rows(marks):
        return marks.reshape(LM, units, width).transpose(1, 0, 2)

    lq_u = jnp.concatenate([my_unit(lq_l)[None], unit_rows(lq_s)], axis=0)
    lk_u = jnp.concatenate([my_unit(lk_l)[None], unit_rows(lk_s)], axis=0)
    z_u = inverse(lq_u, lk_u)

    c_l = conv(no_length, v_l, v_rim, tap_rows, items, False)
    c_s = conv(length, v_s, no_rim, tap_rows, 1, True)

    w_own, bv_own = combine(got_l[None], z_u[:1])
    w_s, bv_s = combine(msg_s[:, None], z_u[1:])
    w_l = gather(w_own[0])

    o_l = mix(lk_l, w_l[:owners], q_l, c_l, items, units)
    o_s = mix(lk_s, w_s, q_s, c_s, 1, units)

    vec = lambda v: v.reshape(1, -1)
    out_l, out_s, dr_l, dr_s, do_l, do_s, g_up, g_dn, g_out, small, small_up = dense(
        x_l, x_s, o_l, o_s, cot_long.reshape(items * rows, D), cot_short.reshape(short_rows, D), w_out, w_up, w_down,
        vec(ln1_gain), vec(ln1_bias), vec(up_bias), vec(down_bias), vec(ln2_gain), vec(ln2_bias),
    )

    do_items = do_l.reshape(D, items, rows)
    do_rim = rims(
        *neighbours(do_items[:, :, :HALF].transpose(1, 2, 0), do_items[:, :, rows - HALF :].transpose(1, 2, 0))
    ).T
    dw_l, dlk_part, dsf_l = back_f(lk_l, w_l[:owners], q_l, do_l, items, units)
    dw_s, dlk_part_s, dsf_s = back_f(lk_s, w_s, q_s, do_s, 1, units)
    got_dw = exchange(pad_units(dw_l, n_seq))

    dc_l, tap_l = conv_back(no_length, v_l, v_rim, do_l, do_rim, tap_rows, items, False)
    dc_s, tap_s = conv_back(length, v_s, no_rim, do_s, no_rim, tap_rows, 1, True)

    dbv_own, dw_own = back_mix(got_dw[None], z_u[:1], bv_own)
    dbv_s, dw_sum_s = back_mix(dw_s[:, None], z_u[1:], bv_s)
    dbv_l = gather(dbv_own[0])

    dlq_u, dlk_u = back_inverse(
        lq_u, lk_u, jnp.concatenate([dw_own, dw_sum_s], axis=0), jnp.concatenate([bv_own, bv_s], axis=0)
    )
    dsb_l, dv_l, dlq_part = back_b(no_length, lq_l, w_l[:owners], dbv_l[:owners], k_l, v_l, dc_l, items, units, False)
    dsb_s, dv_s, dlq_part_s = back_b(length, lq_s, w_s, dbv_s, k_s, v_s, dc_s, 1, units, True)

    owned = (jnp.arange(owners) == me).astype(f32).reshape(items, units, 1, 1)

    def with_own(part, own):
        return part.reshape(items, LM, D) + (owned * own[None, None]).transpose(0, 2, 1, 3).reshape(items, LM, D)

    dl = jnp.stack([with_own(dlq_part, dlq_u[0]), with_own(dlk_part, dlk_u[0])]).astype(bf)
    dl = dl.reshape(2 * items, n_seq, own_marks, D).transpose(1, 0, 2, 3)
    dl = jnp.sum(exchange(dl).astype(f32), axis=0) * (1.0 / seg)
    dl = jnp.pad(dl.reshape(2, items, own_marks, D), ((0, 0), (0, 0), (0, 16 - own_marks), (0, 0)))
    dl = dl.reshape(2, items * 16, D)

    count = (length[0] // LM).astype(f32)
    from_units = lambda u: u.transpose(1, 0, 2).reshape(LM, D)
    sq_s = (dlq_part_s + from_units(dlq_u[1:])) / count
    sk_s = (dlk_part_s + from_units(dlk_u[1:])) / count

    grad_l, grad_s, g_q, g_k, g_v = final(
        length,
        (x_l, dr_l, lq_l, lk_l, dsf_l, dsb_l, dv_l, dl[0], dl[1]),
        (x_s, dr_s, lq_s, lk_s, dsf_s, dsb_s, dv_s, sq_s, sk_s),
        (w_query, w_key, w_value),
        items,
    )

    packed = jnp.concatenate(
        [small.reshape(-1), small_up.reshape(-1), (tap_l + tap_s)[:, 0, :].reshape(-1)]
    ).reshape(-1, 128)
    packed = sum_everywhere(packed).reshape(-1)
    small = packed[: 6 * D].reshape(6, D)
    small_up = packed[6 * D : 6 * D + FF]
    taps_g = packed[6 * D + FF :].reshape(H, 128)[:, :TAPS].T

    up_g = reduce_rows(g_up, ("x", "y", "z0", "z1"))
    down_g = reduce_columns(g_dn, ("y", "z0", "x", "z1"))
    out_g = reduce_rows(g_out, ("z0", "x", "y", "z1"))
    q_g = reduce_rows(g_q, ("x", "y", "z0", "z1"))
    k_g = reduce_rows(g_k, ("y", "z0", "x", "z1"))
    v_g = reduce_rows(g_v, ("z0", "x", "y", "z1"))
    return (
        out_l.reshape(x_long.shape),
        out_s.reshape(x_short.shape),
        grad_l.reshape(x_long.shape),
        grad_s.reshape(x_short.shape),
        q_g,
        k_g,
        v_g,
        out_g,
        taps_g,
        small[0],
        small[1],
        up_g,
        small_up,
        down_g,
        small[2],
        small[4],
        small[5],
    )


def solution(mesh):
    tokens = P("dp", None, "seq", None)
    shorts = P("dp", "seq", None, None, None)
    rows = P("seq", None)
    return jax.shard_map(
        body,
        mesh=mesh,
        in_specs=(tokens, shorts, P("dp", None), P("dp", "seq", None)) + (P(),) * 13 + (tokens, shorts),
        out_specs=(tokens, shorts, tokens, shorts, rows, rows, rows, rows, P(), P(), P(), rows, P(), rows, P(), P(), P()),
        check_vma=False,
    )
```

```python
import functools

import jax
import jax.numpy as jnp
from jax import lax
from jax.experimental import pallas as pl
from jax.experimental.pallas import tpu as pltpu
from jax.sharding import PartitionSpec as P

D = 768
H = 12
HD = 64
FF = 3072
LM = 64
NS_STEPS = 6
HALF = 16
TAPS = 33
LONG = 4096
GROUP = 256
EPSILON = 1e-05
MASKED_SCORE = -1e30
SCALE = 0.125
VMEM_BYTES = 63 * 1024 * 1024

f32 = jnp.float32
bf = jnp.bfloat16
sds = jax.ShapeDtypeStruct


def dot(a, b, ca, cb):
    return lax.dot_general(a, b, (((ca,), (cb,)), ((), ())), preferred_element_type=f32)


def split(v):
    hi = v.astype(bf)
    return hi, (v - hi.astype(f32)).astype(bf)


def mm(a, b, ca=1, cb=0):
    ah, al = split(a)
    bh, bl = split(b)
    return dot(ah, bh, ca, cb) + (dot(ah, bl, ca, cb) + dot(al, bh, ca, cb))


def iota(shape, dim):
    return lax.broadcasted_iota(jnp.int32, shape, dim)


def spread_heads(block):
    tiled = jnp.concatenate([block.astype(f32)] * 4, axis=0)
    same = (iota((GROUP, GROUP), 0) // HD) == (iota((GROUP, GROUP), 1) // HD)
    return jnp.where(same, tiled, 0.0).astype(bf)


def pick_heads(full):
    head = iota((LM, GROUP), 1) // HD
    out = full[:LM]
    for h in range(1, 4):
        out = jnp.where(head == h, full[h * LM : (h + 1) * LM], out)
    return out


def lanes_of(columns):
    n = columns[0].shape[0]
    lane = iota((n, 128), 1)
    wide = jnp.zeros((n, 128), f32)
    for k, col in enumerate(columns):
        wide = jnp.where(lane == k, col, wide)
    return wide.T[:8]


def three_parts(row):
    hi = row.astype(bf).astype(f32)
    mid = (row - hi).astype(bf).astype(f32)
    low = row - hi - mid
    r = iota((16, row.shape[1]), 0)
    return jnp.where(r == 0, hi, jnp.where(r == 1, mid, jnp.where(r == 2, low, 0.0))).astype(bf)


def from_parts(rows):
    v = rows.astype(f32)
    total = v[0:1] + v[1:2] + v[2:3]
    return jnp.broadcast_to(total, (8, total.shape[1])).T[:, 0:1]


def head_softmax(scores):
    rows = scores.shape[1]
    s3 = scores.reshape(4, LM, rows)
    e = jnp.exp(s3 - jnp.max(s3, axis=1, keepdims=True))
    return (e / jnp.sum(e, axis=1, keepdims=True)).reshape(GROUP, rows)


def params(vmem=VMEM_BYTES):
    return pltpu.CompilerParams(vmem_limit_bytes=vmem)


def cost(flops, nbytes, trans=0):
    return pl.CostEstimate(flops=int(flops), bytes_accessed=int(nbytes), transcendentals=int(trans))


SMEM_SPEC = pl.BlockSpec(memory_space=pltpu.SMEM)
ANY_SPEC = pl.BlockSpec(memory_space=pl.ANY)


def after(kernel, count, deps):
    return lambda *refs: kernel(*refs[:count], *refs[count + len(deps) :])


def const_spec(shape):
    return pl.BlockSpec(shape, lambda i: tuple(0 for _ in shape), pipeline_mode=pl.Buffered(1))


def short_member(length, rows):
    seg = length // LM
    lm = iota((LM, rows), 0)
    pos = iota((LM, rows), 1)
    return ((pos >= lm * seg) & (pos < (lm + 1) * seg)).astype(f32)


def qkv_kernel(n_long, length, x_l, x_s, wq, wk, wv, q_l, k_l, v_l, q_s, k_s, v_s, lq, lk, w_t):
    i = pl.program_id(0)

    @pl.when(i == 0)
    def _():
        for j, w in enumerate((wq, wk, wv)):
            w_t[j] = w[...].T

    x = jnp.where(i < n_long, x_l[...], x_s[...])
    made = [dot(w_t[j], x, 1, 1).astype(bf) for j in range(3)]

    @pl.when(i < n_long)
    def _():
        for ref, v in zip((q_l, k_l, v_l), made):
            ref[...] = v

    @pl.when(i >= n_long)
    def _():
        for ref, v in zip((q_s, k_s, v_s), made):
            ref[...] = v
        member = short_member(length[0], made[0].shape[1]).astype(bf)
        count = (length[0] // LM).astype(f32)
        lq[...] = (dot(member, made[0], 1, 1) / count).astype(bf)
        lk[...] = (dot(member, made[1], 1, 1) / count).astype(bf)


def qkv(length, x_l, x_s, wq, wk, wv):
    tile = x_s.shape[0]
    nl = x_l.shape[0] // tile
    long_at = lambda i: jnp.minimum(i, nl - 1)
    row = lambda f: pl.BlockSpec((tile, D), lambda i: (f(i), 0))
    col = lambda f: pl.BlockSpec((D, tile), lambda i: (0, f(i)))
    first = lambda i: 0
    tl, ts = x_l.shape[0], x_s.shape[0]
    return pl.pallas_call(
        functools.partial(qkv_kernel, nl),
        grid=(nl + 1,),
        in_specs=[SMEM_SPEC, row(long_at), row(first)] + [const_spec((D, D))] * 3,
        out_specs=[col(long_at)] * 3 + [col(first)] * 3 + [pl.BlockSpec((LM, D), lambda i: (0, 0))] * 2,
        out_shape=[sds((D, tl), bf)] * 3 + [sds((D, ts), bf)] * 3 + [sds((LM, D), bf)] * 2,
        scratch_shapes=[pltpu.VMEM((3, D, D), bf)],
        compiler_params=params(),
        cost_estimate=cost(6 * (tl + ts) * D * D, 8 * (tl + ts) * D),
        name="qkv",
    )(length, x_l, x_s, wq, wk, wv)


def mark_scores(lq_g, k_g, limit):
    scores = dot(spread_heads(lq_g * SCALE), k_g, 1, 0)
    if limit is not None:
        scores = jnp.where(iota(scores.shape, 1) < limit, scores, MASKED_SCORE)
    return scores


def group_slices():
    return [slice(g * GROUP, (g + 1) * GROUP) for g in range(3)]


def stats_kernel(units, lq, k, v, msg):
    sums, stats = [], []
    for gs in group_slices():
        scores = mark_scores(lq[:, gs], k[gs, :], None)
        most = jnp.max(scores, axis=1, keepdims=True)
        e = jnp.exp(scores - most)
        stats.append(lanes_of([most, jnp.sum(e, axis=1, keepdims=True)]))
        sums.append(pick_heads(dot(e.astype(bf), v[gs, :], 1, 1)))
    sums = jnp.concatenate(sums, axis=1)
    stats = jnp.concatenate(stats, axis=1)
    width = D // units
    for u in range(units):
        us = slice(u * width, (u + 1) * width)
        msg[u, :LM, :] = sums[:, us]
        msg[u, LM:, :] = stats[:, us]


def item_specs(rows):
    mark = pl.BlockSpec((LM, D), lambda i: (i, 0))
    tok = pl.BlockSpec((D, rows), lambda i: (0, i))
    return mark, tok


def stats(lq, k, v, items, units):
    rows = k.shape[1] // items
    mark, tok = item_specs(rows)
    return pl.pallas_call(
        functools.partial(stats_kernel, units),
        grid=(items,),
        in_specs=[mark, tok, tok],
        out_specs=pl.BlockSpec((units, LM + 8, D // units), lambda i: (i, 0, 0)),
        out_shape=sds((items * units, LM + 8, D // units), f32),
        compiler_params=params(),
        cost_estimate=cost(4 * items * rows * D * GROUP, 4 * items * rows * D, items * rows * D),
        name="stats",
    )(lq, k, v)


def eye():
    return jnp.where(iota((LM, LM), 0) == iota((LM, LM), 1), 1.0, 0.0).astype(f32)


def head_slices(count):
    return [slice(h * HD, (h + 1) * HD) for h in range(count)]


def mark_probs(q, k):
    s = SCALE * dot(q, k, 1, 1)
    e = jnp.exp(s - jnp.max(s, axis=-1, keepdims=True))
    return e / jnp.sum(e, axis=-1, keepdims=True)


def inverse_start(a):
    col = jnp.sum(a, axis=0, keepdims=True)
    row = jnp.sum(a, axis=1, keepdims=True)
    return col, row, jnp.max(col, axis=1, keepdims=True), jnp.max(row, axis=0, keepdims=True)


def inverse_steps(a_list, kept=None):
    ident = eye()
    z_list = []
    for a in a_list:
        _, _, cm, rm = inverse_start(a)
        z_list.append(a.T / (cm * rm))
    for _ in range(NS_STEPS):
        p_list = [mm(a, z) for a, z in zip(a_list, z_list)]
        t2 = [15.0 * ident - mm(p, 7.0 * ident - p) for p in p_list]
        t3 = [13.0 * ident - mm(p, t) for p, t in zip(p_list, t2)]
        if kept is not None:
            kept.append((z_list, p_list, t2, t3))
        z_list = [0.25 * mm(z, t) for z, t in zip(z_list, t3)]
    return z_list


def own_slices(*refs):
    return [(k, s) for k, ref in enumerate(refs) for s in head_slices(ref.shape[1] // HD)]


def inverse_kernel(at, lq_l, lk_l, lq_s, lk_s, z_l, z_s):
    qs, ks, zs = (lq_l, lq_s), (lk_l, lk_s), (z_l, z_s)
    heads = own_slices(lq_l, lq_s)
    a_list = [mark_probs(qs[n][:, s], ks[n][:, s]) for n, s in heads]
    for (n, s), z in zip(heads, inverse_steps(a_list)):
        zs[n][:, s] = z


def whole(shape):
    return pl.BlockSpec(shape, lambda i, at: tuple(0 for _ in shape))


def inverse(at, lq_l, lk_l, lq_s, lk_s, width):
    own = pl.BlockSpec((LM, width), lambda i, at: (at[0], at[1]))
    return pl.pallas_call(
        inverse_kernel,
        grid_spec=pltpu.PrefetchScalarGridSpec(
            num_scalar_prefetch=1,
            grid=(1,),
            in_specs=[own, own, whole((LM, D)), whole((LM, D))],
            out_specs=[whole((LM, width)), whole((LM, D))],
        ),
        out_shape=[sds((LM, width), f32), sds((LM, D), f32)],
        compiler_params=params(),
        cost_estimate=cost((width + D) // HD * 24 * 3 * 2 * 64**3 * 20, 1e6),
        name="inverse",
    )(at, lq_l, lk_l, lq_s, lk_s)


def combine_kernel(senders, msg, z, out, bv_out):
    width = z.shape[1]
    most = jnp.concatenate([msg[d, LM : LM + 1, :] for d in range(senders)], axis=0)
    part = jnp.concatenate([msg[d, LM + 1 : LM + 2, :] for d in range(senders)], axis=0)
    top = jnp.max(most, axis=0, keepdims=True)
    e = jnp.exp(most - top)
    total = jnp.sum(part * e, axis=0, keepdims=True)
    weight = (e / total).T
    w_all = []
    for s in head_slices(width // HD):
        bv = jnp.zeros((LM, HD), f32)
        for d in range(senders):
            bv = bv + weight[s, d : d + 1] * msg[d, :LM, s]
        bv_out[:, s] = bv
        w_all.append(mm(z[:, s], bv))
    out[:LM, :] = jnp.concatenate(w_all, axis=1).astype(bf)
    out[LM:, :] = three_parts(top + jnp.log(total))


VMEM_SPEC = pl.BlockSpec(memory_space=pltpu.VMEM)


def combine(msg, z):
    senders, _, width = msg.shape
    return pl.pallas_call(
        functools.partial(combine_kernel, senders),
        in_specs=[VMEM_SPEC] * 2,
        out_specs=[VMEM_SPEC] * 2,
        out_shape=[sds((LM + 16, width), bf), sds((LM, width), f32)],
        compiler_params=params(),
        cost_estimate=cost(1e8, 4e6),
        name="combine",
    )(msg, z)


def joined(ref, units, rows):
    return jnp.concatenate([ref[u, rows, :] for u in range(units)], axis=1)


def mark_mix(lk_g, w_g, q_g, conv_g):
    probs = head_softmax(dot(spread_heads(lk_g * SCALE), q_g, 1, 0)).astype(bf)
    return (dot(spread_heads(w_g), probs, 0, 0) + conv_g).astype(bf)


def mix_kernel(units, lk, w, q, conv, out):
    w_all = joined(w, units, slice(0, LM))
    for gs in group_slices():
        out[gs, :] = mark_mix(lk[:, gs], w_all[:, gs], q[gs, :], conv[gs, :])


def short_kernel(length, q, k, v, lq, lk, z, conv, out, w_out, bv_out):
    for gs in group_slices():
        scores = mark_scores(lq[:, gs], k[gs, :], length[0])
        e = jnp.exp(scores - jnp.max(scores, axis=1, keepdims=True))
        probs = e / jnp.sum(e, axis=1, keepdims=True)
        bv = pick_heads(dot(probs.astype(bf), v[gs, :], 1, 1))
        bv_out[:, gs] = bv
        z_g = z[:, gs]
        w = jnp.concatenate([mm(z_g[:, s], bv[:, s]) for s in head_slices(4)], axis=1).astype(bf)
        w_out[:, gs] = w
        out[gs, :] = mark_mix(lk[:, gs], w, q[gs, :], conv[gs, :])


def short_attend(length, q, k, v, lq, lk, z, conv):
    return pl.pallas_call(
        short_kernel,
        in_specs=[SMEM_SPEC] + [VMEM_SPEC] * 7,
        out_specs=[VMEM_SPEC] * 3,
        out_shape=[sds(q.shape, bf), sds((LM, D), bf), sds((LM, D), f32)],
        compiler_params=params(),
        cost_estimate=cost(4 * q.size * GROUP * 2, 10 * q.size, 2 * q.size),
        name="short_attend",
    )(length, q, k, v, lq, lk, z, conv)


def unit_spec(units, rows, width):
    return pl.BlockSpec((units, rows, width), lambda i: (i, 0, 0))


def mix(lk, w, q, conv, items, units):
    rows = q.shape[1] // items
    mark, tok = item_specs(rows)
    return pl.pallas_call(
        functools.partial(mix_kernel, units),
        grid=(items,),
        in_specs=[mark, unit_spec(units, LM + 16, D // units), tok, tok],
        out_specs=tok,
        out_shape=sds(q.shape, bf),
        compiler_params=params(),
        cost_estimate=cost(4 * items * rows * D * GROUP, 8 * items * rows * D, items * rows * D),
        name="mix",
    )(lk, w, q, conv)


def windows(body, rim, items, rows, limit):
    out = []
    for j in range(items):
        own = body[:, j * rows : (j + 1) * rows]
        if limit is not None:
            own = jnp.where(iota(own.shape, 1) < limit, own.astype(f32), 0.0).astype(bf)
        wide = jnp.concatenate(
            [rim[:, 32 * j : 32 * j + HALF], own, rim[:, 32 * j + HALF : 32 * j + 2 * HALF]], axis=1
        )
        for t in range(rows // 128):
            out.append(wide[:, t * 128 : t * 128 + 128 + 2 * HALF])
    return jnp.concatenate(out, axis=0)


def band(row):
    wide = jnp.concatenate([row, jnp.zeros((1, 128), f32)], axis=1)
    rolled = pltpu.roll(jnp.broadcast_to(wide, (128, 256)), 0, 1, stride=1, stride_axis=0)
    return split(rolled[:, : 128 + 2 * HALF])


HEAD_STEP = 3


def unstack(stacked, out, at, items, rows, limit=None):
    k = 0
    for j in range(items):
        for t in range(rows // 128):
            v = stacked[k * HD : (k + 1) * HD]
            if limit is not None:
                v = jnp.where(iota(v.shape, 1) + t * 128 < limit, v, 0.0)
            out[at, j * rows + t * 128 : j * rows + (t + 1) * 128] = v
            k += 1


def both_windows(v_l, v_s, rim, at, items, limit):
    no_rim = jnp.zeros((HD, 2 * HALF), bf)
    rows, short_rows = v_l.shape[1] // items, v_s.shape[1]
    return jnp.concatenate(
        [
            windows(v_l[at, :], rim[at, :], items, rows, None),
            windows(v_s[at, :], no_rim, 1, short_rows, limit),
        ],
        axis=0,
    )


def banded(wins, row, out_l, out_s, at, items, limit):
    hi, lo = band(row)
    made = dot(wins, hi, 1, 1) + dot(wins, lo, 1, 1)
    cut = HD * out_l.shape[1] // 128
    unstack(made[:cut], out_l, at, items, out_l.shape[1] // items)
    unstack(made[cut:], out_s, at, 1, out_s.shape[1], limit)


def conv_kernel(items, length, v_l, v_s, rim, taps, out_l, out_s):
    for h in range(HEAD_STEP):
        at = slice(h * HD, (h + 1) * HD)
        wins = both_windows(v_l, v_s, rim, at, items, length[0])
        banded(wins, taps[h, 0:1, :], out_l, out_s, at, items, None)


def conv_specs(v_l, v_s, rim):
    n = HEAD_STEP * HD
    spec = lambda a: pl.BlockSpec((n, a.shape[1]), lambda h: (h, 0))
    return spec(v_l), spec(v_s), spec(rim), pl.BlockSpec((HEAD_STEP, 8, 128), lambda h: (h, 0, 0))


def conv(length, v_l, v_s, rim, taps, items):
    tok_l, tok_s, rims, tap = conv_specs(v_l, v_s, rim)
    return pl.pallas_call(
        functools.partial(conv_kernel, items),
        grid=(H // HEAD_STEP,),
        in_specs=[SMEM_SPEC, tok_l, tok_s, rims, tap],
        out_specs=[tok_l, tok_s],
        out_shape=[sds(v_l.shape, f32), sds(v_s.shape, f32)],
        compiler_params=params(),
        cost_estimate=cost(4 * 512 * v_l.size, 8 * v_l.size),
        name="conv",
    )(length, v_l, v_s, rim, taps)


def conv_back_kernel(items, length, v_l, v_s, rim, up_l, up_s, up_rim, taps, out_l, out_s, tap_grad):
    flip = (iota((128, 128), 0) + iota((128, 128), 1) == 127).astype(f32).astype(bf)
    for h in range(HEAD_STEP):
        at = slice(h * HD, (h + 1) * HD)
        wins = both_windows(v_l, v_s, rim, at, items, length[0])
        up_wins = both_windows(up_l, up_s, up_rim, at, items, None)
        banded(up_wins, taps[h, 1:2, :], out_l, out_s, at, items, length[0])
        ups = [up_l[at, t * 128 : (t + 1) * 128] for t in range(up_l.shape[1] // 128)]
        ups += [up_s[at, t * 128 : (t + 1) * 128] for t in range(up_s.shape[1] // 128)]
        gram = dot(jnp.concatenate(ups, axis=0), wins, 0, 0)
        hi, lo = split(gram)
        gram = dot(flip, hi, 1, 0) + dot(flip, lo, 1, 0)
        gram = jnp.concatenate([gram, jnp.zeros((128, 256 - gram.shape[1]), f32)], axis=1)
        skewed = pltpu.roll(gram, 129, 1, stride=1, stride_axis=0)
        tap_grad[h] = jnp.broadcast_to(jnp.sum(skewed, axis=0, keepdims=True)[:, :128], (8, 128))


def conv_back(length, v_l, v_s, rim, up_l, up_s, up_rim, taps, items, deps=()):
    tok_l, tok_s, rims, tap = conv_specs(v_l, v_s, rim)
    return pl.pallas_call(
        after(functools.partial(conv_back_kernel, items), 8, deps),
        grid=(H // HEAD_STEP,),
        in_specs=[SMEM_SPEC, tok_l, tok_s, rims, tok_l, tok_s, rims, tap] + [ANY_SPEC] * len(deps),
        out_specs=[tok_l, tok_s, tap],
        out_shape=[sds(v_l.shape, f32), sds(v_s.shape, f32), sds((H, 8, 128), f32)],
        compiler_params=params(),
        cost_estimate=cost(6 * 512 * v_l.size, 12 * v_l.size),
        name="conv_back",
    )(length, v_l, v_s, rim, up_l, up_s, up_rim, taps, *deps)


def fold_rows(v):
    return jnp.sum(v.reshape(v.shape[0] // 8, 8, v.shape[1]), axis=0)


def gelu_parts(x):
    e = jnp.exp(x * x * (-0.5))
    t = pl.reciprocal(1.0 + jnp.abs(x) * (0.3275911 * 0.7071067811865476), approx=False)
    poly = t * (
        0.127414796 + t * (-0.142248368 + t * (0.7107068705 + t * (-0.7265760135 + t * 0.5307027145)))
    )
    tail = poly * e
    phi = jnp.where(x >= 0, 1.0 - tail, tail)
    return x * phi, phi + x * e * 0.3989422804014327


def put_bf16(jobs, stage, sem):
    pend = []
    for k, (load, copies) in enumerate(jobs):
        slot = k % 2
        if k >= 2:
            for cp in pend[k - 2]:
                cp.wait()
        stage[slot] = load().astype(bf)
        pend.append(copies(stage.at[slot], sem.at[slot]))
    for group in pend[-2:]:
        for cp in group:
            cp.wait()


def to_side(src, keep, send, keeps, sem):
    copy = pltpu.make_async_copy(src, keep, sem)

    @pl.when(keeps)
    def _():
        copy.start()

    @pl.when(jnp.logical_not(keeps))
    def _():
        pltpu.make_async_copy(src, send, sem).start()

    return [copy]


def column_jobs(acc, keep, send, core):
    n = acc.shape[1] // D
    jobs = []
    for c in range(n):
        half, at = c // (n // 2), (c % (n // 2)) * D
        jobs.append((
            lambda c=c: acc[:, c * D : (c + 1) * D],
            lambda src, sem, half=half, at=at: to_side(
                src, keep.at[:, at : at + D], send.at[:, at : at + D], core == half, sem
            ),
        ))
    return jobs


def row_jobs(acc, keep, send, core):
    half = D // 2

    def copies(src, sem, c):
        out = []
        for ref, which in ((keep, core), (send, 1 - core)):
            start = pl.multiple_of(which * half, half)
            out.append(pltpu.make_async_copy(src.at[pl.ds(start, half), :], ref.at[:, c * D : (c + 1) * D], sem))
            out[-1].start()
        return out

    return [
        (lambda c=c: acc[:, c * D : (c + 1) * D], lambda src, sem, c=c: copies(src, sem, c))
        for c in range(acc.shape[1] // D)
    ]


def plain_job(acc, dst):
    def copies(src, sem):
        copy = pltpu.make_async_copy(src, dst, sem)
        copy.start()
        return [copy]

    return (lambda: acc[...], copies)


def dense_kernel(n_long, chunk, core, x_l, x_s, o_l, o_s, c_l, c_s, w_out, w_up, w_down, g1, b1, bu, bd, g2, b2,
                 out_l, out_s, dr_l, dr_s, do_l, do_s, up_keep, up_send, dn_keep, dn_send, gout, small, small_up,
                 acc_up, acc_dn, acc_out, act, dact, accs, accu, stage, sem):
    i = pl.program_id(0)
    last = pl.num_programs(0) - 1
    is_long = i < n_long

    @pl.when(i == 0)
    def _():
        for ref in (acc_up, acc_dn, acc_out, accs, accu):
            ref[...] = jnp.zeros_like(ref)

    x = jnp.where(is_long, x_l[...], x_s[...]).astype(f32)
    o_t = jnp.where(is_long, o_l[...], o_s[...])
    r1 = x + dot(o_t, w_out[...], 0, 0)
    cen = r1 - jnp.mean(r1, axis=-1, keepdims=True)
    rstd1 = lax.rsqrt(jnp.mean(cen * cen, axis=-1, keepdims=True) + EPSILON)
    xh1 = cen * rstd1
    h1 = (xh1 * g1[...] + b1[...]).astype(bf)
    r2 = h1.astype(f32) + bd[...]
    for c in range(FF // chunk):
        cs = slice(c * chunk, (c + 1) * chunk)
        a, dg = gelu_parts(dot(h1, w_up[:, cs], 1, 0) + bu[:, cs])
        a = a.astype(bf)
        act[:, cs] = a
        dact[:, cs] = dg
        r2 = r2 + dot(a, w_down[cs, :], 1, 0)
    cen2 = r2 - jnp.mean(r2, axis=-1, keepdims=True)
    rstd2 = lax.rsqrt(jnp.mean(cen2 * cen2, axis=-1, keepdims=True) + EPSILON)
    xh2 = cen2 * rstd2
    out = (xh2 * g2[...] + b2[...]).astype(bf)
    g = jnp.where(is_long, c_l[...], c_s[...]).astype(f32)
    dxh = g * g2[...]
    dr2 = rstd2 * (
        dxh - jnp.mean(dxh, axis=-1, keepdims=True) - xh2 * jnp.mean(dxh * xh2, axis=-1, keepdims=True)
    )
    dz2 = dr2.astype(bf)
    accs[4] += fold_rows(g * xh2)
    accs[5] += fold_rows(g)
    accs[2] += fold_rows(dz2.astype(f32))
    dz2_t = dz2.T
    h1_t = h1.T
    dh1 = dr2
    for c in range(FF // chunk):
        cs = slice(c * chunk, (c + 1) * chunk)
        dp1 = (dot(dz2, w_down[cs, :], 1, 1) * dact[:, cs]).astype(bf)
        accu[:, cs] += fold_rows(dp1.astype(f32))
        dh1 = dh1 + dot(dp1, w_up[:, cs], 1, 1)
        acc_up[:, cs] += dot(h1_t, dp1, 1, 0)
        acc_dn[:, cs] += dot(dz2_t, act[:, cs], 1, 0)
    accs[0] += fold_rows(dh1 * xh1)
    accs[1] += fold_rows(dh1)
    dx = dh1 * g1[...]
    dr1 = rstd1 * (
        dx - jnp.mean(dx, axis=-1, keepdims=True) - xh1 * jnp.mean(dx * xh1, axis=-1, keepdims=True)
    )
    da1 = dr1.astype(bf)
    acc_out[...] += dot(o_t, da1, 1, 0)
    do_t = dot(w_out[...], da1, 1, 1).astype(bf)

    @pl.when(is_long)
    def _():
        out_l[...] = out
        dr_l[...] = dr1
        do_l[...] = do_t

    @pl.when(jnp.logical_not(is_long))
    def _():
        out_s[...] = out
        dr_s[...] = dr1
        do_s[...] = do_t

    @pl.when(i == last)
    def _():
        jobs = column_jobs(acc_up, up_keep, up_send, core[0])
        jobs += row_jobs(acc_dn, dn_keep, dn_send, core[0])
        put_bf16(jobs + [plain_job(acc_out, gout)], stage, sem)
        small[...] = jnp.sum(accs[...], axis=1)
        small_up[...] = jnp.sum(accu[...], axis=0, keepdims=True)


def dense(core, x_l, x_s, o_l, o_s, c_l, c_s, w_out, w_up, w_down, g1, b1, bu, bd, g2, b2, tile=256, chunk=768):
    nl, ns = x_l.shape[0] // tile, x_s.shape[0] // tile
    long_at = lambda i: jnp.minimum(i, nl - 1)
    short_at = lambda i: jnp.maximum(i - nl, 0)
    row = lambda f: pl.BlockSpec((tile, D), lambda i: (f(i), 0))
    col = lambda f: pl.BlockSpec((D, tile), lambda i: (0, f(i)))
    anywhere = pl.BlockSpec(memory_space=pl.ANY)
    tl, ts = x_l.shape[0], x_s.shape[0]
    vec = const_spec((1, D))
    return pl.pallas_call(
        functools.partial(dense_kernel, nl, chunk),
        grid=(nl + ns,),
        in_specs=[SMEM_SPEC, row(long_at), row(short_at), col(long_at), col(short_at), row(long_at), row(short_at)]
        + [const_spec((D, D)), const_spec((D, FF)), const_spec((FF, D))]
        + [vec, vec, const_spec((1, FF)), vec, vec, vec],
        out_specs=[row(long_at), row(short_at), row(long_at), row(short_at), col(long_at), col(short_at)]
        + [anywhere] * 5
        + [const_spec((6, D)), const_spec((1, FF))],
        out_shape=[sds((tl, D), bf), sds((ts, D), bf), sds((tl, D), f32), sds((ts, D), f32)]
        + [sds((D, tl), bf), sds((D, ts), bf), sds((D, FF // 2), bf), sds((D, FF // 2), bf)]
        + [sds((D // 2, FF), bf), sds((D // 2, FF), bf), sds((D, D), bf)]
        + [sds((6, D), f32), sds((1, FF), f32)],
        scratch_shapes=[
            pltpu.VMEM((D, FF), f32),
            pltpu.VMEM((D, FF), f32),
            pltpu.VMEM((D, D), f32),
            pltpu.VMEM((tile, FF), bf),
            pltpu.VMEM((tile, FF), f32),
            pltpu.VMEM((6, 8, D), f32),
            pltpu.VMEM((8, FF), f32),
            pltpu.VMEM((2, D, D), bf),
            pltpu.SemaphoreType.DMA((2,)),
        ],
        compiler_params=params(),
        cost_estimate=cost(2 * (tl + ts) * (3 * D * D + 6 * D * FF), 60e6, (tl + ts) * FF),
        name="dense",
    )(core, x_l, x_s, o_l, o_s, c_l, c_s, w_out, w_up, w_down, g1, b1, bu, bd, g2, b2)


def back_f_group(lk_g, w_g, q_g, up_g):
    rows = q_g.shape[1]
    probs = head_softmax(dot(spread_heads(lk_g * SCALE), q_g, 1, 0))
    dw = pick_heads(dot(probs.astype(bf), up_g, 1, 1))
    dprobs = dot(spread_heads(w_g), up_g, 1, 0)
    weighted = jnp.sum((probs * dprobs).reshape(4, LM, rows), axis=1, keepdims=True)
    dsf = (probs * (dprobs.reshape(4, LM, rows) - weighted).reshape(GROUP, rows)).astype(bf)
    return dw, dsf, SCALE * pick_heads(dot(dsf, q_g, 1, 1))


def back_f_kernel(units, lk, w, q, up, dw_out, dlk_out, dsf_out, edges):
    w_all = joined(w, units, slice(0, LM))
    rows = q.shape[1]
    edges[0] = jnp.concatenate([up[:, :HALF], up[:, rows - HALF :]], axis=1).T
    dws = []
    for gs in group_slices():
        dw, dsf_out[gs, :], dlk_out[:, gs] = back_f_group(lk[:, gs], w_all[:, gs], q[gs, :], up[gs, :])
        dws.append(dw)
    dws = jnp.concatenate(dws, axis=1)
    width = D // units
    for u in range(units):
        dw_out[u] = dws[:, u * width : (u + 1) * width]


def back_f(lk, w, q, up, items, units):
    rows = q.shape[1] // items
    mark, tok = item_specs(rows)
    width = D // units
    return pl.pallas_call(
        functools.partial(back_f_kernel, units),
        grid=(items,),
        in_specs=[mark, unit_spec(units, LM + 16, width), tok, tok],
        out_specs=[unit_spec(units, LM, width), mark, tok, pl.BlockSpec((1, 2 * HALF, D), lambda i: (i, 0, 0))],
        out_shape=[
            sds((items * units, LM, width), f32),
            sds((items * LM, D), f32),
            sds(q.shape, bf),
            sds((items, 2 * HALF, D), bf),
        ],
        compiler_params=params(),
        cost_estimate=cost(8 * items * rows * D * GROUP, 6 * items * rows * D, items * rows * D),
        name="back_f",
    )(lk, w, q, up)


def back_mix_kernel(senders, dw_in, z, bv, out, dw_out):
    width = z.shape[1]
    dw = dw_in[0]
    for d in range(1, senders):
        dw = dw + dw_in[d]
    dw_out[...] = dw
    dbvs, dots = [], []
    for s in head_slices(width // HD):
        dbv = mm(z[:, s], dw[:, s], 0, 0).astype(bf)
        dots.append(jnp.sum(dbv.astype(f32) * bv[:, s], axis=1, keepdims=True))
        dbvs.append(dbv)
    out[:LM, :] = jnp.concatenate(dbvs, axis=1)
    out[LM:, :] = three_parts(lanes_of([jnp.concatenate(dots, axis=0)])[:1])


def back_mix(dw, z, bv, deps=()):
    senders, _, width = dw.shape
    return pl.pallas_call(
        after(functools.partial(back_mix_kernel, senders), 3, deps),
        in_specs=[VMEM_SPEC] * 3 + [ANY_SPEC] * len(deps),
        out_specs=[VMEM_SPEC] * 2,
        out_shape=[sds((LM + 16, width), bf), sds((LM, width), f32)],
        compiler_params=params(),
        cost_estimate=cost(1e8, 4e6),
        name="back_mix",
    )(dw, z, bv, *deps)


def back_inverse_kernel(at, lq_l, lk_l, lq_s, lk_s, dw_l, bv_l, dw_s, bv_s, dlq_l, dlk_l, dlq_s, dlk_s):
    qs, ks, dws, bvs = (lq_l, lq_s), (lk_l, lk_s), (dw_l, dw_s), (bv_l, bv_s)
    heads = own_slices(lq_l, lq_s)
    a_list = [mark_probs(qs[n][:, s], ks[n][:, s]) for n, s in heads]
    kept = []
    inverse_steps(a_list, kept)
    ident = eye()
    dz = [mm(dws[n][:, s], bvs[n][:, s], 1, 1) for n, s in heads]
    da = [jnp.zeros((LM, LM), f32) for _ in heads]
    for z, p, t2, t3 in reversed(kept):
        dt3 = [0.25 * mm(zz, d, 0, 0) for zz, d in zip(z, dz)]
        dz = [0.25 * mm(d, t, 1, 1) for d, t in zip(dz, t3)]
        dp = [-mm(d, t, 1, 1) for d, t in zip(dt3, t2)]
        dt2 = [-mm(pp, d, 0, 0) for pp, d in zip(p, dt3)]
        dp = [x - mm(d, 7.0 * ident - pp, 1, 1) for x, d, pp in zip(dp, dt2, p)]
        dp = [x + mm(pp, d, 0, 0) for x, pp, d in zip(dp, p, dt2)]
        da = [x + mm(d, zz, 1, 1) for x, d, zz in zip(da, dp, z)]
        dz = [x + mm(a, d, 0, 0) for x, a, d in zip(dz, a_list, dp)]
    for (n, s), a, g, d in zip(heads, a_list, da, dz):
        col, row, cm, rm = inverse_start(a)
        norm = cm * rm
        g = g + d.T / norm
        dnorm = -jnp.sum(jnp.sum(d.T * a, axis=1, keepdims=True), axis=0, keepdims=True) / (norm * norm)
        at_col = (col == cm).astype(f32)
        at_row = (row == rm).astype(f32)
        g = g + dnorm * rm * at_col / jnp.sum(at_col, axis=1, keepdims=True)
        g = g + dnorm * cm * at_row / jnp.sum(at_row, axis=0, keepdims=True)
        ds = a * (g - jnp.sum(a * g, axis=1, keepdims=True))
        (dlq_l, dlq_s)[n][:, s] = SCALE * mm(ds, ks[n][:, s].astype(f32))
        (dlk_l, dlk_s)[n][:, s] = SCALE * mm(ds, qs[n][:, s].astype(f32), 0, 0)


def back_inverse(at, lq_l, lk_l, lq_s, lk_s, dw_l, bv_l, dw_s, bv_s, deps=()):
    width = dw_l.shape[1]
    own = pl.BlockSpec((LM, width), lambda i, at: (at[0], at[1]))
    one, all_heads = whole((LM, width)), whole((LM, D))
    return pl.pallas_call(
        after(back_inverse_kernel, 9, deps),
        grid_spec=pltpu.PrefetchScalarGridSpec(
            num_scalar_prefetch=1,
            grid=(1,),
            in_specs=[own, own, all_heads, all_heads, one, one, all_heads, all_heads] + [ANY_SPEC] * len(deps),
            out_specs=[one, one, all_heads, all_heads],
        ),
        out_shape=[sds((LM, width), f32)] * 2 + [sds((LM, D), f32)] * 2,
        compiler_params=params(),
        cost_estimate=cost((width + D) // HD * 72 * 3 * 2 * 64**3 * 20, 2e6),
        name="back_inverse",
    )(at, lq_l, lk_l, lq_s, lk_s, dw_l, bv_l, dw_s, bv_s, *deps)


def back_b_group(lq_g, k_g, v_g, dbv_g, dots, dconv_g, probs):
    wide = spread_heads(dbv_g)
    dsb = (probs * (dot(wide, v_g, 1, 0) - dots)).astype(bf)
    dv = (dot(wide, probs.astype(bf), 0, 0) + dconv_g).astype(bf)
    return dsb, dv, SCALE * pick_heads(dot(dsb, k_g, 1, 1))


def back_b_kernel(units, lq, w, dbv, k, v, dconv, x, gv_in, dsb_out, dv_out, dlq_out, gv_out, acc):
    i = pl.program_id(0)

    @pl.when(i == 0)
    def _():
        acc[...] = gv_in[...]

    level = from_parts(joined(w, units, slice(LM, LM + 16)))
    dots = from_parts(joined(dbv, units, slice(LM, LM + 16)))
    dbv_all = joined(dbv, units, slice(0, LM))
    for gs in group_slices():
        probs = jnp.exp(mark_scores(lq[:, gs], k[gs, :], None) - level[gs])
        dsb_out[gs, :], dv, dlq_out[:, gs] = back_b_group(
            lq[:, gs], k[gs, :], v[gs, :], dbv_all[:, gs], dots[gs], dconv[gs, :], probs
        )
        dv_out[gs, :] = dv
        acc[gs, :] += dot(dv, x[...], 1, 0)

    @pl.when(i == pl.num_programs(0) - 1)
    def _():
        gv_out[...] = acc[...].astype(bf)


def back_b(lq, w, dbv, k, v, dconv, x, gv, items, units, deps=()):
    rows = k.shape[1] // items
    mark, tok = item_specs(rows)
    unit = unit_spec(units, LM + 16, D // units)
    square = const_spec((D, D))
    return pl.pallas_call(
        after(functools.partial(back_b_kernel, units), 8, deps),
        grid=(items,),
        in_specs=[mark, unit, unit, tok, tok, tok, pl.BlockSpec((rows, D), lambda i: (i, 0)), square]
        + [ANY_SPEC] * len(deps),
        out_specs=[tok, tok, mark, square],
        out_shape=[sds(k.shape, bf), sds(k.shape, bf), sds((items * LM, D), f32), sds((D, D), bf)],
        scratch_shapes=[pltpu.VMEM((D, D), f32)],
        compiler_params=params(),
        cost_estimate=cost(14 * items * rows * D * GROUP, 14 * items * rows * D, items * rows * D),
        name="back_b",
    )(lq, w, dbv, k, v, dconv, x, gv, *deps)


def short_back_kernel(length, q, k, v, lq, lk, z, w, bv, up, dconv, x, dsf_out, dsb_out, dv_out, dlq_out, dlk_out, dw_out, gv_out):
    for gs in group_slices():
        dw, dsf_out[gs, :], dlk_out[:, gs] = back_f_group(lk[:, gs], w[:, gs], q[gs, :], up[gs, :])
        dw_out[:, gs] = dw
        z_g, bv_g = z[:, gs], bv[:, gs]
        dbvs = [mm(z_g[:, s], dw[:, s], 0, 0).astype(bf) for s in head_slices(4)]
        dots = jnp.concatenate(
            [jnp.sum(d.astype(f32) * bv_g[:, s], axis=1, keepdims=True) for d, s in zip(dbvs, head_slices(4))], axis=0
        )
        scores = mark_scores(lq[:, gs], k[gs, :], length[0])
        e = jnp.exp(scores - jnp.max(scores, axis=1, keepdims=True))
        probs = e / jnp.sum(e, axis=1, keepdims=True)
        dsb_out[gs, :], dv, dlq_out[:, gs] = back_b_group(
            lq[:, gs], k[gs, :], v[gs, :], jnp.concatenate(dbvs, axis=1), dots, dconv[gs, :], probs
        )
        dv_out[gs, :] = dv
        gv_out[gs, :] = dot(dv, x[...], 1, 0)


def short_back(length, q, k, v, lq, lk, z, w, bv, up, dconv, x, deps=()):
    mark = sds((LM, D), f32)
    return pl.pallas_call(
        after(short_back_kernel, 12, deps),
        in_specs=[SMEM_SPEC] + [VMEM_SPEC] * 11 + [ANY_SPEC] * len(deps),
        out_specs=[VMEM_SPEC] * 7,
        out_shape=[sds(q.shape, bf)] * 3 + [mark] * 3 + [sds((D, D), f32)],
        compiler_params=params(),
        cost_estimate=cost(24 * q.size * GROUP, 20 * q.size, 2 * q.size),
        name="short_back",
    )(length, q, k, v, lq, lk, z, w, bv, up, dconv, x, *deps)


def score_part(member, x, lq, lk, dsf, dsb, sq, sk, dq_out, dk_out, acc):
    member2 = jnp.concatenate([member, member], axis=0)
    for n, (marks, scores, sums, out) in enumerate(((lk, dsf, sq, dq_out), (lq, dsb, sk, dk_out))):
        hi, lo = split(sums)
        back = dot(jnp.concatenate([hi, lo], axis=0), member2, 0, 0)
        for gs in group_slices():
            part = (dot(spread_heads(marks[:, gs] * SCALE), scores[gs, :], 0, 0) + back[gs]).astype(bf)
            out[gs, :] = part
            acc[n, gs, :] += dot(part, x[...], 1, 0)


def score_grads_kernel(n_long, length, core, x_l, lq_l, lk_l, dsf_l, dsb_l, sq_l, sk_l,
                       x_s, lq_s, lk_s, dsf_s, dsb_s, sq_s, sk_s, sq_own, sk_own,
                       dq_l, dk_l, dq_s, dk_s, keep, send, acc, stage, sem):
    i = pl.program_id(0)

    @pl.when(i == 0)
    def _():
        acc[...] = jnp.zeros_like(acc)
        member = short_member(length[0], x_s.shape[0]).astype(bf)
        count = (length[0] // LM).astype(f32)
        sq, sk = (sq_s[...] + sq_own[...]) / count, (sk_s[...] + sk_own[...]) / count
        score_part(member, x_s, lq_s, lk_s, dsf_s, dsb_s, sq, sk, dq_s, dk_s, acc)

    @pl.when(i > 0)
    def _():
        count, rows = sq_l.shape[0], x_l.shape[0]
        member = (iota((count, rows), 1) // (LONG // LM) == iota((count, rows), 0)).astype(f32).astype(bf)
        score_part(member, x_l, lq_l, lk_l, dsf_l, dsb_l, sq_l[...], sk_l[...], dq_l, dk_l, acc)

    @pl.when(i == n_long)
    def _():
        jobs = [
            (lambda: acc[0], lambda src, sem: to_side(src, keep, send, core[0] == 0, sem)),
            (lambda: acc[1], lambda src, sem: to_side(src, keep, send, core[0] == 1, sem)),
        ]
        put_bf16(jobs, stage, sem)


def score_grads(length, core, long_args, short_args, items, deps=()):
    x_l, x_s = long_args[0], short_args[0]
    tl, ts = x_l.shape[0], x_s.shape[0]
    rows = tl // items
    marks_l = long_args[5].shape[0] // items
    at = lambda i: jnp.maximum(i - 1, 0)
    first = lambda i: 0

    def specs(r, marks, f):
        row = pl.BlockSpec((r, D), lambda i: (f(i), 0))
        mark = pl.BlockSpec((LM, D), lambda i: (f(i), 0))
        tok = pl.BlockSpec((D, r), lambda i: (0, f(i)))
        own = pl.BlockSpec((marks, D), lambda i: (f(i), 0))
        return [row, mark, mark, tok, tok, own, own]

    long_out = pl.BlockSpec((D, rows), lambda i: (0, at(i)))
    short_out = pl.BlockSpec((D, ts), lambda i: (0, 0))
    return pl.pallas_call(
        after(functools.partial(score_grads_kernel, items), 18, deps),
        grid=(items + 1,),
        in_specs=[SMEM_SPEC, SMEM_SPEC]
        + specs(rows, marks_l, at)
        + specs(ts, LM, first)
        + [const_spec((LM, D))] * 2
        + [ANY_SPEC] * len(deps),
        out_specs=[long_out] * 2 + [short_out] * 2 + [ANY_SPEC] * 2,
        out_shape=[sds((D, tl), bf)] * 2 + [sds((D, ts), bf)] * 2 + [sds((D, D), bf)] * 2,
        scratch_shapes=[
            pltpu.VMEM((2, D, D), f32),
            pltpu.VMEM((2, D, D), bf),
            pltpu.SemaphoreType.DMA((2,)),
        ],
        compiler_params=params(),
        cost_estimate=cost(6 * (tl + ts) * D * D, 20 * (tl + ts) * D),
        name="score_grads",
    )(length, core, *long_args, *short_args, *deps)


def input_grad_kernel(n_long, dr_l, dq_l, dk_l, dv_l, dr_s, dq_s, dk_s, dv_s, wq, wk, wv, out_l, out_s):
    i = pl.program_id(0)
    is_long = i < n_long
    total = jnp.where(is_long, dr_l[...], dr_s[...])
    for long_ref, short_ref, w in ((dq_l, dq_s, wq), (dk_l, dk_s, wk), (dv_l, dv_s, wv)):
        grad = jnp.where(is_long, long_ref[...], short_ref[...])
        total = total + dot(grad, w[...], 0, 1)
    total = total.astype(bf)

    @pl.when(is_long)
    def _():
        out_l[...] = total

    @pl.when(jnp.logical_not(is_long))
    def _():
        out_s[...] = total


def input_grad(long_args, short_args, weights, deps=()):
    tl, ts = long_args[0].shape[0], short_args[0].shape[0]
    nl = tl // ts
    at = lambda i: jnp.minimum(i, nl - 1)
    row = lambda f: pl.BlockSpec((ts, D), lambda i: (f(i), 0))
    col = lambda f: pl.BlockSpec((D, ts), lambda i: (0, f(i)))
    first = lambda i: 0
    return pl.pallas_call(
        after(functools.partial(input_grad_kernel, nl), 11, deps),
        grid=(nl + 1,),
        in_specs=[row(at)] + [col(at)] * 3 + [row(first)] + [col(first)] * 3 + [const_spec((D, D))] * 3
        + [ANY_SPEC] * len(deps),
        out_specs=[row(at), row(first)],
        out_shape=[sds((tl, D), bf), sds((ts, D), bf)],
        compiler_params=params(),
        cost_estimate=cost(6 * (tl + ts) * D * D, 12 * (tl + ts) * D),
        name="input_grad",
    )(*long_args, *short_args, *weights, *deps)


def swap(values, axis, bit):
    count = lax.axis_size(axis)
    return lax.ppermute(values, axis, [(i, i ^ bit) for i in range(count)])


def side(axis, bit):
    return (lax.axis_index(axis) // bit) % 2


def exchange(values):
    return lax.all_to_all(values, "seq", 0, 0, tiled=True)


def gather(values):
    return exchange(jnp.broadcast_to(values[None], (lax.axis_size("seq"),) + values.shape))


def tied(values, dep):
    return lax.optimization_barrier(tuple(values) + (dep,))[:-1]


def is_small_mesh():
    return lax.axis_size("dp") == 4 and lax.axis_size("seq") == 8


def pair_sum(keep, send, axis, bit):
    return keep.astype(f32) + swap(send, axis, bit).astype(f32)


class Reduction:
    def __init__(self, keep, send, dim):
        self.dim, self.other = dim, 1 - dim
        self.core, self.x = side("dp", 1), side("dp", 2)
        v = pair_sum(keep, send, "dp", 1)
        if not is_small_mesh():
            self.theirs = v.astype(bf)
            return
        half = v.shape[self.other] // 2
        self.mine = lax.dynamic_slice_in_dim(v, self.x * half, half, self.other).astype(bf)
        self.theirs = lax.dynamic_slice_in_dim(v, (1 - self.x) * half, half, self.other).astype(bf)

    def wait_for(self, dep):
        if is_small_mesh():
            (self.mine,) = tied((self.mine,), dep)

    def over_x(self):
        if not is_small_mesh():
            self.value = self.theirs
            return self.value
        n_seq = lax.axis_size("seq")
        v = pair_sum(self.mine, self.theirs, "dp", 2).astype(bf)
        if self.dim == 0:
            v = v.reshape(n_seq, v.shape[0] // n_seq, v.shape[1])
        else:
            v = v.reshape(v.shape[0], n_seq, v.shape[1] // n_seq).transpose(1, 0, 2)
        self.value = v
        return v

    def over_seq(self):
        if not is_small_mesh():
            self.own = lax.psum_scatter(self.value, "seq", scatter_dimension=self.dim, tiled=True)
        else:
            self.own = jnp.sum(exchange(self.value).astype(f32), axis=0).astype(bf)
        return self.own

    def both(self):
        if not is_small_mesh():
            place = (jnp.arange(2) == self.core).astype(f32)[:, None, None]
            shares = lax.psum(self.own.astype(f32)[None] * place, "dp")
            return shares[0], shares[1]
        got = swap(self.own, "dp", 2)
        v = jnp.where(
            self.x == 0,
            jnp.concatenate([self.own, got], axis=self.other),
            jnp.concatenate([got, self.own], axis=self.other),
        )
        got = swap(v, "dp", 1)
        first = self.core == 0
        return jnp.where(first, v, got).astype(f32), jnp.where(first, got, v).astype(f32)


class Halving(Reduction):
    def __init__(self, keep, send, dim, order):
        if not is_small_mesh():
            super().__init__(keep, send, dim)
            return
        self.dim, self.other = dim, 1 - dim
        self.core, self.x = side("dp", 1), side("dp", 2)
        v = pair_sum(keep, send, "dp", 1)
        rows, n = v.shape
        if dim == 0:
            v = v.reshape(2, 2, 2, rows // 8, n)
        else:
            v = v.reshape(rows, 8, n // 8).transpose(1, 0, 2).reshape(2, 2, 2, rows, n // 8)
        self.left = ["z1", "z0", "y"]
        self.order = list(order)
        self.split(v)

    def split(self, v):
        step = self.order[0]
        if step == "x":
            dim = v.ndim - 1 if self.dim == 0 else v.ndim - 2
            bit = self.x
            size = v.shape[dim] // 2
        else:
            dim = self.left.index(step)
            self.left.pop(dim)
            bit = side("seq", {"y": 1, "z0": 2, "z1": 4}[step])
            size = 1
        take = lambda at: lax.dynamic_slice_in_dim(v, at * size, size, dim).astype(bf)
        self.mine, self.theirs = take(bit), take(1 - bit)
        if step != "x":
            self.mine, self.theirs = (lax.squeeze(u, (dim,)) for u in (self.mine, self.theirs))

    def step(self):
        if not is_small_mesh():
            self.value = self.theirs
            return self.theirs
        axis, bit = {"x": ("dp", 2), "y": ("seq", 1), "z0": ("seq", 2), "z1": ("seq", 4)}[self.order.pop(0)]
        v = pair_sum(self.mine, self.theirs, axis, bit)
        if self.order:
            self.split(v)
            return self.theirs
        self.own = v.astype(bf)
        return self.own

    def last(self):
        if not is_small_mesh():
            self.step()
            return self.over_seq()
        return self.step()


def hold(value, dep):
    return tied((value,), dep)[0]


class SumStages:
    def __init__(self, values):
        self.values = values
        self.steps = [("dp", 1), ("seq", 4), ("seq", 2), ("seq", 1), ("dp", 2)]

    def step(self, dep):
        if is_small_mesh():
            axis, bit = self.steps.pop(0)
            held = hold(self.values, dep)
            self.values = held + swap(held, axis, bit)
        elif len(self.steps) == 5:
            self.steps.pop(0)
            self.values = lax.psum(self.values, ("dp", "seq"))
        return self.values


def neighbours(first, last):
    count = lax.axis_size("seq")
    right = lax.ppermute(first, "seq", [((i + 1) % count, i) for i in range(count)])
    left = lax.ppermute(last, "seq", [(i, (i + 1) % count) for i in range(count)])
    return left, right


def pad_units(values, count):
    have = values.shape[0]
    if have == count:
        return values
    return jnp.concatenate([values, jnp.zeros((count - have,) + values.shape[1:], values.dtype)], axis=0)


def body(x_long, x_short, item_start, short_lengths, w_query, w_key, w_value, w_out, conv_taps, ln1_gain, ln1_bias,
         w_up, up_bias, w_down, down_bias, ln2_gain, ln2_bias, cot_long, cot_short):
    _, items, rows, _ = x_long.shape
    short_rows = x_short.shape[3]
    seg = LONG // LM
    own_marks = rows // seg
    n_seq = lax.axis_size("seq")
    me = lax.axis_index("seq")
    heads_each = next(h for h in (2, 4, 6, 12) if H % h == 0 and items * H // h <= n_seq)
    units = H // heads_each
    width = heads_each * HD
    owners = items * units

    x_l = x_long.reshape(items * rows, D)
    x_s = x_short.reshape(short_rows, D)
    length = short_lengths.reshape(1)
    core = side("dp", 1).astype(jnp.int32).reshape(1)
    mine = jnp.minimum(me, owners - 1).astype(jnp.int32)
    at = jnp.stack([mine // units, mine % units])

    x_mean = jnp.sum(x_long[0].reshape(items, own_marks, seg, D).astype(f32), axis=2) * (1.0 / seg)
    means = gather(x_mean.reshape(items * own_marks, D))
    means = means.reshape(n_seq, items, own_marks, D).transpose(1, 0, 2, 3).reshape(items * LM, D)
    mean_hi, mean_lo = split(means)

    def marks_of(w):
        return (
            jnp.dot(mean_hi, w, preferred_element_type=f32) + jnp.dot(mean_lo, w, preferred_element_type=f32)
        ).astype(bf)

    place = (me - item_start[0]) % n_seq
    open_left = (place > 0)[:, None, None]
    open_right = (place < n_seq - 1)[:, None, None]

    def rims(left, right):
        return jnp.concatenate(
            [jnp.where(open_left, left, jnp.zeros_like(left)), jnp.where(open_right, right, jnp.zeros_like(right))], axis=1
        ).reshape(items * 2 * HALF, D)

    x_rim = rims(*neighbours(x_long[0, :, :HALF], x_long[0, :, rows - HALF :]))
    v_rim = jnp.einsum("ke,nk->en", w_value, x_rim, preferred_element_type=f32).astype(bf)

    tap_rows = jnp.stack([conv_taps.T, conv_taps[::-1].T], axis=1)
    tap_rows = jnp.pad(tap_rows, ((0, 0), (0, 6), (0, 128 - TAPS)))

    q_l, k_l, v_l, q_s, k_s, v_s, lq_s, lk_s = qkv(length, x_l, x_s, w_query, w_key, w_value)
    c_l, c_s = conv(length, v_l, v_s, v_rim, tap_rows, items)
    lq_l, lk_l = marks_of(w_query), marks_of(w_key)

    msg_l = stats(lq_l, k_l, v_l, items, units)
    got_l = exchange(pad_units(msg_l, n_seq))
    z_own, z_s = inverse(at, lq_l, lk_l, lq_s, lk_s, width)
    w_own, bv_own = combine(got_l, z_own)
    w_l = gather(w_own)[:owners]
    o_s, w_s, bv_s = short_attend(length, q_s, k_s, v_s, lq_s, lk_s, z_s, c_s)
    o_l = mix(lk_l, w_l, q_l, c_l, items, units)

    vec = lambda v: v.reshape(1, -1)
    out_l, out_s, dr_l, dr_s, do_l, do_s, up_keep, up_send, dn_keep, dn_send, g_out, small, small_up = dense(
        core, x_l, x_s, o_l, o_s, cot_long.reshape(items * rows, D), cot_short.reshape(short_rows, D), w_out, w_up,
        w_down, vec(ln1_gain), vec(ln1_bias), vec(up_bias), vec(down_bias), vec(ln2_gain), vec(ln2_bias),
    )

    dw_l, dlk_part, dsf_l, edges = back_f(lk_l, w_l, q_l, do_l, items, units)
    got_dw = exchange(pad_units(dw_l, n_seq))
    up_keep, dn_keep = tied((up_keep, dn_keep), edges)
    up = Halving(up_keep, up_send, 0, ("x", "y", "z0", "z1"))
    down = Halving(dn_keep, dn_send, 1, ("y", "x", "z0", "z1"))
    do_rim = rims(*tied(neighbours(edges[:, :HALF], edges[:, HALF:]) + (up.theirs,), down.theirs)[:2]).T

    dc_l, dc_s, tap_g = conv_back(
        length, v_l, v_s, v_rim, do_l, do_s, do_rim, tap_rows, items, (up.theirs, down.theirs)
    )
    dsf_s, dsb_s, dv_s, dlq_s, dlk_s, dw_s, gv_s = short_back(
        length, q_s, k_s, v_s, lq_s, lk_s, z_s, w_s, bv_s, do_s, dc_s, x_s
    )
    packed = jnp.concatenate([small.reshape(-1), small_up.reshape(-1), tap_g[:, 0, :].reshape(-1)]).reshape(-1, 128)
    packed = SumStages(packed)
    dbv_own, dw_own = back_mix(got_dw, z_own, bv_own, (dv_s,))
    dbv_l = gather(dbv_own)[:owners]
    dlq_own, dlk_own, dlq_own_s, dlk_own_s = back_inverse(
        at, lq_l, lk_l, lq_s, lk_s, dw_own, bv_own, dw_s, bv_s, (up.step(), down.step())
    )
    dsb_l, dv_l, dlq_part, g_v = back_b(
        lq_l, w_l, dbv_l, k_l, v_l, dc_l, x_l, gv_s, items, units, (up.step(), down.step(), packed.step(dw_own))
    )

    owned = (jnp.arange(owners) == me).astype(f32).reshape(items, units, 1, 1)

    def with_own(part, own):
        return part.reshape(items, LM, D) + (owned * own[None, None]).transpose(0, 2, 1, 3).reshape(items, LM, D)

    dl = jnp.stack([with_own(dlq_part, dlq_own), with_own(dlk_part, dlk_own)]).astype(bf)
    dl = dl.reshape(2 * items, n_seq, own_marks, D).transpose(1, 0, 2, 3)
    dl = jnp.sum(exchange(dl).astype(f32), axis=0) * (1.0 / seg)
    dl = jnp.pad(dl.reshape(2, items, own_marks, D), ((0, 0), (0, 0), (0, 16 - own_marks), (0, 0)))
    dl = dl.reshape(2, items * 16, D)

    g_v = g_v.T
    is_first = core[0] == 0
    value_out = Reduction(jnp.where(is_first, g_v, g_out), jnp.where(is_first, g_out, g_v), 0)

    dq_l, dk_l, dq_s, dk_s, qk_keep, qk_send = score_grads(
        length,
        core,
        (x_l, lq_l, lk_l, dsf_l, dsb_l, dl[0], dl[1]),
        (x_s, lq_s, lk_s, dsf_s, dsb_s, dlq_s, dlk_s, dlq_own_s, dlk_own_s),
        items,
        (up.step(), down.step(), packed.step(dlq_part), value_out.theirs),
    )
    query_key = Reduction(qk_keep, qk_send, 1)
    grad_l, grad_s = input_grad(
        (dr_l, dq_l, dk_l, dv_l),
        (dr_s, dq_s, dk_s, dv_s),
        (w_query, w_key, w_value),
        (query_key.theirs, value_out.over_x()),
    )
    query_key.wait_for(grad_l)
    up.last()
    down.last()
    query_key.over_x()
    ready = query_key.value
    up.own, down.own = hold(up.own, ready), hold(down.own, ready)
    packed.step(grad_l)
    packed.step(ready)
    value_out.over_seq()
    query_key.over_seq()
    up_a, up_b = up.both()
    down_a, down_b = down.both()
    v_a, v_b = value_out.both()
    q_g, k_g = query_key.both()

    packed = packed.step(ready).reshape(-1)
    small = packed[: 6 * D].reshape(6, D)
    small_up = packed[6 * D : 6 * D + FF]
    taps_g = packed[6 * D + FF :].reshape(H, 128)[:, :TAPS].T

    return (
        out_l.reshape(x_long.shape),
        out_s.reshape(x_short.shape),
        grad_l.reshape(x_long.shape),
        grad_s.reshape(x_short.shape),
        q_g.T,
        k_g.T,
        v_a,
        v_b,
        taps_g,
        small[0],
        small[1],
        jnp.concatenate([up_a, up_b], axis=1),
        small_up,
        jnp.concatenate([down_a, down_b], axis=0).T,
        small[2],
        small[4],
        small[5],
    )


def solution(mesh):
    tokens = P("dp", None, "seq", None)
    shorts = P("dp", "seq", None, None, None)
    rows = P("seq", None)
    return jax.shard_map(
        body,
        mesh=mesh,
        in_specs=(tokens, shorts, P("dp", None), P("dp", "seq", None)) + (P(),) * 13 + (tokens, shorts),
        out_specs=(tokens, shorts, tokens, shorts, rows, rows, rows, rows, P(), P(), P(), rows, P(), rows, P(), P(), P()),
        check_vma=False,
    )
```

```python
import functools

import jax
import jax.numpy as jnp
from jax import lax
from jax.experimental import pallas as pl
from jax.experimental.pallas import tpu as pltpu
from jax.sharding import PartitionSpec as P

D = 768
H = 12
HD = 64
FF = 3072
LM = 64
NS_STEPS = 6
HALF = 16
TAPS = 33
LONG = 4096
GROUP = 256
EPSILON = 1e-05
MASKED_SCORE = -1e30
SCALE = 0.125
VMEM_BYTES = 63 * 1024 * 1024

f32 = jnp.float32
bf = jnp.bfloat16
sds = jax.ShapeDtypeStruct


def dot(a, b, ca, cb):
    return lax.dot_general(a, b, (((ca,), (cb,)), ((), ())), preferred_element_type=f32)


def split(v):
    hi = v.astype(bf)
    return hi, (v - hi.astype(f32)).astype(bf)


def mm(a, b, ca=1, cb=0):
    ah, al = split(a)
    bh, bl = split(b)
    return dot(ah, bh, ca, cb) + (dot(ah, bl, ca, cb) + dot(al, bh, ca, cb))


def iota(shape, dim):
    return lax.broadcasted_iota(jnp.int32, shape, dim)


def spread_heads(block):
    tiled = jnp.concatenate([block.astype(f32)] * 4, axis=0)
    same = (iota((GROUP, GROUP), 0) // HD) == (iota((GROUP, GROUP), 1) // HD)
    return jnp.where(same, tiled, 0.0).astype(bf)


def pick_heads(full):
    head = iota((LM, GROUP), 1) // HD
    out = full[:LM]
    for h in range(1, 4):
        out = jnp.where(head == h, full[h * LM : (h + 1) * LM], out)
    return out


def lanes_of(columns):
    n = columns[0].shape[0]
    lane = iota((n, 128), 1)
    wide = jnp.zeros((n, 128), f32)
    for k, col in enumerate(columns):
        wide = jnp.where(lane == k, col, wide)
    return wide.T[:8]


def three_parts(row):
    hi = row.astype(bf).astype(f32)
    mid = (row - hi).astype(bf).astype(f32)
    low = row - hi - mid
    r = iota((16, row.shape[1]), 0)
    return jnp.where(r == 0, hi, jnp.where(r == 1, mid, jnp.where(r == 2, low, 0.0))).astype(bf)


def from_parts(rows):
    v = rows.astype(f32)
    total = v[0:1] + v[1:2] + v[2:3]
    return jnp.broadcast_to(total, (8, total.shape[1])).T[:, 0:1]


def head_softmax(scores):
    rows = scores.shape[1]
    s3 = scores.reshape(4, LM, rows)
    e = jnp.exp(s3 - jnp.max(s3, axis=1, keepdims=True))
    return (e / jnp.sum(e, axis=1, keepdims=True)).reshape(GROUP, rows)


def params(vmem=VMEM_BYTES):
    return pltpu.CompilerParams(vmem_limit_bytes=vmem)


def cost(flops, nbytes, trans=0):
    return pl.CostEstimate(flops=int(flops), bytes_accessed=int(nbytes), transcendentals=int(trans))


SMEM_SPEC = pl.BlockSpec(memory_space=pltpu.SMEM)
ANY_SPEC = pl.BlockSpec(memory_space=pl.ANY)


def after(kernel, count, deps):
    return lambda *refs: kernel(*refs[:count], *refs[count + len(deps) :])


def const_spec(shape):
    return pl.BlockSpec(shape, lambda i: tuple(0 for _ in shape), pipeline_mode=pl.Buffered(1))


def short_member(length, rows):
    seg = length // LM
    lm = iota((LM, rows), 0)
    pos = iota((LM, rows), 1)
    return ((pos >= lm * seg) & (pos < (lm + 1) * seg)).astype(f32)


def qkv_kernel(n_long, length, x_l, x_s, wq, wk, wv, q_l, k_l, v_l, q_s, k_s, v_s, lq, lk, w_t):
    i = pl.program_id(0)

    @pl.when(i == 0)
    def _():
        for j, w in enumerate((wq, wk, wv)):
            w_t[j * D : (j + 1) * D, :] = w[...].T

    x = jnp.where(i < n_long, x_l[...], x_s[...])
    made = dot(w_t[...], x, 1, 1).astype(bf)
    made = [made[j * D : (j + 1) * D] for j in range(3)]

    @pl.when(i < n_long)
    def _():
        for ref, v in zip((q_l, k_l, v_l), made):
            ref[...] = v

    @pl.when(i >= n_long)
    def _():
        for ref, v in zip((q_s, k_s, v_s), made):
            ref[...] = v
        member = short_member(length[0], made[0].shape[1]).astype(bf)
        count = (length[0] // LM).astype(f32)
        lq[...] = (dot(member, made[0], 1, 1) / count).astype(bf)
        lk[...] = (dot(member, made[1], 1, 1) / count).astype(bf)


def qkv(length, x_l, x_s, wq, wk, wv):
    tile = x_s.shape[0]
    nl = x_l.shape[0] // tile
    long_at = lambda i: jnp.minimum(i, nl - 1)
    row = lambda f: pl.BlockSpec((tile, D), lambda i: (f(i), 0))
    col = lambda f: pl.BlockSpec((D, tile), lambda i: (0, f(i)))
    first = lambda i: 0
    tl, ts = x_l.shape[0], x_s.shape[0]
    return pl.pallas_call(
        functools.partial(qkv_kernel, nl),
        grid=(nl + 1,),
        in_specs=[SMEM_SPEC, row(long_at), row(first)] + [const_spec((D, D))] * 3,
        out_specs=[col(long_at)] * 3 + [col(first)] * 3 + [pl.BlockSpec((LM, D), lambda i: (0, 0))] * 2,
        out_shape=[sds((D, tl), bf)] * 3 + [sds((D, ts), bf)] * 3 + [sds((LM, D), bf)] * 2,
        scratch_shapes=[pltpu.VMEM((3 * D, D), bf)],
        compiler_params=params(),
        cost_estimate=cost(6 * (tl + ts) * D * D, 8 * (tl + ts) * D),
        name="qkv",
    )(length, x_l, x_s, wq, wk, wv)


def mark_scores(lq_g, k_g, limit):
    scores = dot(spread_heads(lq_g * SCALE), k_g, 1, 0)
    if limit is not None:
        scores = jnp.where(iota(scores.shape, 1) < limit, scores, MASKED_SCORE)
    return scores


def group_slices():
    return [slice(g * GROUP, (g + 1) * GROUP) for g in range(3)]


def stats_kernel(units, lq, k, v, msg):
    sums, stats = [], []
    for gs in group_slices():
        scores = mark_scores(lq[:, gs], k[gs, :], None)
        most = jnp.max(scores, axis=1, keepdims=True)
        e = jnp.exp(scores - most)
        stats.append(lanes_of([most, jnp.sum(e, axis=1, keepdims=True)]))
        sums.append(pick_heads(dot(e.astype(bf), v[gs, :], 1, 1)))
    sums = jnp.concatenate(sums, axis=1)
    stats = jnp.concatenate(stats, axis=1)
    width = D // units
    for u in range(units):
        us = slice(u * width, (u + 1) * width)
        msg[u, :LM, :] = sums[:, us]
        msg[u, LM:, :] = stats[:, us]


def item_specs(rows):
    mark = pl.BlockSpec((LM, D), lambda i: (i, 0))
    tok = pl.BlockSpec((D, rows), lambda i: (0, i))
    return mark, tok


def stats(lq, k, v, items, units):
    rows = k.shape[1] // items
    mark, tok = item_specs(rows)
    return pl.pallas_call(
        functools.partial(stats_kernel, units),
        grid=(items,),
        in_specs=[mark, tok, tok],
        out_specs=pl.BlockSpec((units, LM + 8, D // units), lambda i: (i, 0, 0)),
        out_shape=sds((items * units, LM + 8, D // units), f32),
        compiler_params=params(),
        cost_estimate=cost(4 * items * rows * D * GROUP, 4 * items * rows * D, items * rows * D),
        name="stats",
    )(lq, k, v)


def eye():
    return jnp.where(iota((LM, LM), 0) == iota((LM, LM), 1), 1.0, 0.0).astype(f32)


def head_slices(count):
    return [slice(h * HD, (h + 1) * HD) for h in range(count)]


def mark_probs(q, k):
    s = SCALE * dot(q, k, 1, 1)
    e = jnp.exp(s - jnp.max(s, axis=-1, keepdims=True))
    return e / jnp.sum(e, axis=-1, keepdims=True)


def inverse_start(a):
    col = jnp.sum(a, axis=0, keepdims=True)
    row = jnp.sum(a, axis=1, keepdims=True)
    return col, row, jnp.max(col, axis=1, keepdims=True), jnp.max(row, axis=0, keepdims=True)


def inverse_steps(a_list, kept=None):
    ident = eye()
    z_list = []
    for a in a_list:
        _, _, cm, rm = inverse_start(a)
        z_list.append(a.T / (cm * rm))
    for _ in range(NS_STEPS):
        p_list = [mm(a, z) for a, z in zip(a_list, z_list)]
        t2 = [15.0 * ident - mm(p, 7.0 * ident - p) for p in p_list]
        t3 = [13.0 * ident - mm(p, t) for p, t in zip(p_list, t2)]
        if kept is not None:
            kept.append((z_list, p_list, t2, t3))
        z_list = [0.25 * mm(z, t) for z, t in zip(z_list, t3)]
    return z_list


def own_slices(*refs):
    return [(k, s) for k, ref in enumerate(refs) for s in head_slices(ref.shape[1] // HD)]


def inverse_kernel(at, lq_l, lk_l, lq_s, lk_s, z_l, z_s):
    qs, ks, zs = (lq_l, lq_s), (lk_l, lk_s), (z_l, z_s)
    heads = own_slices(lq_l, lq_s)
    a_list = [mark_probs(qs[n][:, s], ks[n][:, s]) for n, s in heads]
    for (n, s), z in zip(heads, inverse_steps(a_list)):
        zs[n][:, s] = z


def whole(shape):
    return pl.BlockSpec(shape, lambda i, at: tuple(0 for _ in shape))


def inverse(at, lq_l, lk_l, lq_s, lk_s, width):
    own = pl.BlockSpec((LM, width), lambda i, at: (at[0], at[1]))
    return pl.pallas_call(
        inverse_kernel,
        grid_spec=pltpu.PrefetchScalarGridSpec(
            num_scalar_prefetch=1,
            grid=(1,),
            in_specs=[own, own, whole((LM, D)), whole((LM, D))],
            out_specs=[whole((LM, width)), whole((LM, D))],
        ),
        out_shape=[sds((LM, width), f32), sds((LM, D), f32)],
        compiler_params=params(),
        cost_estimate=cost((width + D) // HD * 24 * 3 * 2 * 64**3 * 20, 1e6),
        name="inverse",
    )(at, lq_l, lk_l, lq_s, lk_s)


def put_all(out, marks, parts):
    for d in range(out.shape[0]):
        out[d, :LM, :] = marks
        out[d, LM:, :] = parts


def combine_kernel(senders, msg, z, out, bv_out):
    width = z.shape[1]
    most = jnp.concatenate([msg[d, LM : LM + 1, :] for d in range(senders)], axis=0)
    part = jnp.concatenate([msg[d, LM + 1 : LM + 2, :] for d in range(senders)], axis=0)
    top = jnp.max(most, axis=0, keepdims=True)
    e = jnp.exp(most - top)
    total = jnp.sum(part * e, axis=0, keepdims=True)
    weight = (e / total).T
    w_all = []
    for s in head_slices(width // HD):
        bv = jnp.zeros((LM, HD), f32)
        for d in range(senders):
            bv = bv + weight[s, d : d + 1] * msg[d, :LM, s]
        bv_out[:, s] = bv
        w_all.append(mm(z[:, s], bv))
    put_all(out, jnp.concatenate(w_all, axis=1).astype(bf), three_parts(top + jnp.log(total)))


VMEM_SPEC = pl.BlockSpec(memory_space=pltpu.VMEM)


def combine(msg, z):
    senders, _, width = msg.shape
    return pl.pallas_call(
        functools.partial(combine_kernel, senders),
        in_specs=[VMEM_SPEC] * 2,
        out_specs=[VMEM_SPEC] * 2,
        out_shape=[sds((senders, LM + 16, width), bf), sds((LM, width), f32)],
        compiler_params=params(),
        cost_estimate=cost(1e8, 4e6),
        name="combine",
    )(msg, z)


def joined(ref, units, rows):
    return jnp.concatenate([ref[u, rows, :] for u in range(units)], axis=1)


def mark_mix(lk_g, w_g, q_g, conv_g):
    probs = head_softmax(dot(spread_heads(lk_g * SCALE), q_g, 1, 0)).astype(bf)
    return (dot(spread_heads(w_g), probs, 0, 0) + conv_g).astype(bf)


def mix_kernel(units, lk, w, q, conv, out):
    w_all = joined(w, units, slice(0, LM))
    for gs in group_slices():
        out[gs, :] = mark_mix(lk[:, gs], w_all[:, gs], q[gs, :], conv[gs, :])


def short_kernel(length, q, k, v, lq, lk, z, conv, out, w_out, bv_out):
    for gs in group_slices():
        scores = mark_scores(lq[:, gs], k[gs, :], length[0])
        e = jnp.exp(scores - jnp.max(scores, axis=1, keepdims=True))
        probs = e / jnp.sum(e, axis=1, keepdims=True)
        bv = pick_heads(dot(probs.astype(bf), v[gs, :], 1, 1))
        bv_out[:, gs] = bv
        z_g = z[:, gs]
        w = jnp.concatenate([mm(z_g[:, s], bv[:, s]) for s in head_slices(4)], axis=1).astype(bf)
        w_out[:, gs] = w
        out[gs, :] = mark_mix(lk[:, gs], w, q[gs, :], conv[gs, :])


def short_attend(length, q, k, v, lq, lk, z, conv):
    return pl.pallas_call(
        short_kernel,
        in_specs=[SMEM_SPEC] + [VMEM_SPEC] * 7,
        out_specs=[VMEM_SPEC] * 3,
        out_shape=[sds(q.shape, bf), sds((LM, D), bf), sds((LM, D), f32)],
        compiler_params=params(),
        cost_estimate=cost(4 * q.size * GROUP * 2, 10 * q.size, 2 * q.size),
        name="short_attend",
    )(length, q, k, v, lq, lk, z, conv)


def unit_spec(units, rows, width):
    return pl.BlockSpec((units, rows, width), lambda i: (i, 0, 0))


def mix(lk, w, q, conv, items, units):
    rows = q.shape[1] // items
    mark, tok = item_specs(rows)
    return pl.pallas_call(
        functools.partial(mix_kernel, units),
        grid=(items,),
        in_specs=[mark, unit_spec(units, LM + 16, D // units), tok, tok],
        out_specs=tok,
        out_shape=sds(q.shape, bf),
        compiler_params=params(),
        cost_estimate=cost(4 * items * rows * D * GROUP, 8 * items * rows * D, items * rows * D),
        name="mix",
    )(lk, w, q, conv)


def windows(body, rim, items, rows, limit):
    out = []
    for j in range(items):
        own = body[:, j * rows : (j + 1) * rows]
        if limit is not None:
            own = jnp.where(iota(own.shape, 1) < limit, own.astype(f32), 0.0).astype(bf)
        wide = jnp.concatenate(
            [rim[:, 32 * j : 32 * j + HALF], own, rim[:, 32 * j + HALF : 32 * j + 2 * HALF]], axis=1
        )
        for t in range(rows // 128):
            out.append(wide[:, t * 128 : t * 128 + 128 + 2 * HALF])
    return jnp.concatenate(out, axis=0)


def band(row):
    wide = jnp.concatenate([row, jnp.zeros((1, 128), f32)], axis=1)
    rolled = pltpu.roll(jnp.broadcast_to(wide, (128, 256)), 0, 1, stride=1, stride_axis=0)
    return split(rolled[:, : 128 + 2 * HALF])


HEAD_STEP = 3


def unstack(stacked, out, at, items, rows, limit=None):
    k = 0
    for j in range(items):
        for t in range(rows // 128):
            v = stacked[k * HD : (k + 1) * HD]
            if limit is not None:
                v = jnp.where(iota(v.shape, 1) + t * 128 < limit, v, 0.0)
            out[at, j * rows + t * 128 : j * rows + (t + 1) * 128] = v
            k += 1


def both_windows(v_l, v_s, rim, at, items, limit):
    no_rim = jnp.zeros((HD, 2 * HALF), bf)
    rows, short_rows = v_l.shape[1] // items, v_s.shape[1]
    return jnp.concatenate(
        [
            windows(v_l[at, :], rim[at, :], items, rows, None),
            windows(v_s[at, :], no_rim, 1, short_rows, limit),
        ],
        axis=0,
    )


def banded(wins, row, out_l, out_s, at, items, limit):
    hi, lo = band(row)
    made = dot(wins, hi, 1, 1) + dot(wins, lo, 1, 1)
    cut = HD * out_l.shape[1] // 128
    unstack(made[:cut], out_l, at, items, out_l.shape[1] // items)
    unstack(made[cut:], out_s, at, 1, out_s.shape[1], limit)


def conv_kernel(items, length, v_l, v_s, rim, taps, out_l, out_s):
    for h in range(HEAD_STEP):
        at = slice(h * HD, (h + 1) * HD)
        wins = both_windows(v_l, v_s, rim, at, items, length[0])
        banded(wins, taps[h, 0:1, :], out_l, out_s, at, items, None)


def conv_specs(v_l, v_s, rim):
    n = HEAD_STEP * HD
    spec = lambda a: pl.BlockSpec((n, a.shape[1]), lambda h: (h, 0))
    return spec(v_l), spec(v_s), spec(rim), pl.BlockSpec((HEAD_STEP, 8, 128), lambda h: (h, 0, 0))


def conv(length, v_l, v_s, rim, taps, items):
    tok_l, tok_s, rims, tap = conv_specs(v_l, v_s, rim)
    return pl.pallas_call(
        functools.partial(conv_kernel, items),
        grid=(H // HEAD_STEP,),
        in_specs=[SMEM_SPEC, tok_l, tok_s, rims, tap],
        out_specs=[tok_l, tok_s],
        out_shape=[sds(v_l.shape, f32), sds(v_s.shape, f32)],
        compiler_params=params(),
        cost_estimate=cost(4 * 512 * v_l.size, 8 * v_l.size),
        name="conv",
    )(length, v_l, v_s, rim, taps)


def conv_back_kernel(items, length, v_l, v_s, rim, up_l, up_s, up_rim, taps, out_l, out_s, tap_grad):
    flip = (iota((128, 128), 0) + iota((128, 128), 1) == 127).astype(f32).astype(bf)
    for h in range(HEAD_STEP):
        at = slice(h * HD, (h + 1) * HD)
        wins = both_windows(v_l, v_s, rim, at, items, length[0])
        up_wins = both_windows(up_l, up_s, up_rim, at, items, None)
        banded(up_wins, taps[h, 1:2, :], out_l, out_s, at, items, length[0])
        ups = [up_l[at, t * 128 : (t + 1) * 128] for t in range(up_l.shape[1] // 128)]
        ups += [up_s[at, t * 128 : (t + 1) * 128] for t in range(up_s.shape[1] // 128)]
        gram = dot(jnp.concatenate(ups, axis=0), wins, 0, 0)
        hi, lo = split(gram)
        gram = dot(flip, hi, 1, 0) + dot(flip, lo, 1, 0)
        gram = jnp.concatenate([gram, jnp.zeros((128, 256 - gram.shape[1]), f32)], axis=1)
        skewed = pltpu.roll(gram, 129, 1, stride=1, stride_axis=0)
        tap_grad[h] = jnp.broadcast_to(jnp.sum(skewed, axis=0, keepdims=True)[:, :128], (8, 128))


def conv_back(length, v_l, v_s, rim, up_l, up_s, up_rim, taps, items, deps=()):
    tok_l, tok_s, rims, tap = conv_specs(v_l, v_s, rim)
    return pl.pallas_call(
        after(functools.partial(conv_back_kernel, items), 8, deps),
        grid=(H // HEAD_STEP,),
        in_specs=[SMEM_SPEC, tok_l, tok_s, rims, tok_l, tok_s, rims, tap] + [ANY_SPEC] * len(deps),
        out_specs=[tok_l, tok_s, tap],
        out_shape=[sds(v_l.shape, f32), sds(v_s.shape, f32), sds((H, 8, 128), f32)],
        compiler_params=params(),
        cost_estimate=cost(6 * 512 * v_l.size, 12 * v_l.size),
        name="conv_back",
    )(length, v_l, v_s, rim, up_l, up_s, up_rim, taps, *deps)


def fold_rows(v):
    return jnp.sum(v.reshape(v.shape[0] // 8, 8, v.shape[1]), axis=0)


def gelu_parts(x):
    e = jnp.exp(x * x * (-0.5))
    t = pl.reciprocal(1.0 + jnp.abs(x) * (0.3275911 * 0.7071067811865476), approx=False)
    poly = t * (
        0.127414796 + t * (-0.142248368 + t * (0.7107068705 + t * (-0.7265760135 + t * 0.5307027145)))
    )
    tail = poly * e
    phi = jnp.where(x >= 0, 1.0 - tail, tail)
    return x * phi, phi + x * e * 0.3989422804014327


def put_bf16(jobs, stage, sem):
    pend = []
    for k, (load, copies) in enumerate(jobs):
        slot = k % 2
        if k >= 2:
            for cp in pend[k - 2]:
                cp.wait()
        stage[slot] = load().astype(bf)
        pend.append(copies(stage.at[slot], sem.at[slot]))
    for group in pend[-2:]:
        for cp in group:
            cp.wait()


def to_side(src, keep, send, keeps, sem):
    copy = pltpu.make_async_copy(src, keep, sem)

    @pl.when(keeps)
    def _():
        copy.start()

    @pl.when(jnp.logical_not(keeps))
    def _():
        pltpu.make_async_copy(src, send, sem).start()

    return [copy]


def plain_job(acc, dst):
    def copies(src, sem):
        copy = pltpu.make_async_copy(src, dst, sem)
        copy.start()
        return [copy]

    return (lambda: acc[...], copies)


def dense_kernel(n_long, tile, chunk, core, x_l, x_s, o_l, o_s, c_l, c_s, w_out, w_up, w_down, vecs, bu,
                 out_l, out_s, dr_l, dr_s, do_l, do_s, up_keep, up_send, dn_keep, dn_send, gout, small, small_up,
                 acc_up, acc_dn, acc_out, act, dact, accs, accu, x_b, o_b, c_b, out_b, dr_b, do_b,
                 in_sem, out_sem, end_sem):
    i = pl.program_id(0)
    last = pl.num_programs(0) - 1
    slot = lax.rem(i, 2)
    g1, b1, bd, g2, b2 = (vecs.at[k : k + 1] for k in range(5))

    def at(step):
        return pl.ds(pl.multiple_of(step * tile, tile), tile)

    def in_copies(step, to, refs):
        x, o, c = refs
        return [
            pltpu.make_async_copy(x.at[at(step), :], x_b.at[to], in_sem.at[0, to]),
            pltpu.make_async_copy(o.at[:, at(step)], o_b.at[to], in_sem.at[1, to]),
            pltpu.make_async_copy(c.at[at(step), :], c_b.at[to], in_sem.at[2, to]),
        ]

    def fetch(step, to):
        @pl.when(step < n_long)
        def _():
            for cp in in_copies(step, to, (x_l, o_l, c_l)):
                cp.start()

        @pl.when(step >= n_long)
        def _():
            for cp in in_copies(step - n_long, to, (x_s, o_s, c_s)):
                cp.start()

    def out_copies(step, refs):
        out, dr, do = refs
        return [
            pltpu.make_async_copy(out_b, out.at[at(step), :], out_sem.at[0]),
            pltpu.make_async_copy(dr_b, dr.at[at(step), :], out_sem.at[1]),
            pltpu.make_async_copy(do_b, do.at[:, at(step)], out_sem.at[2]),
        ]

    @pl.when(i == 0)
    def _():
        fetch(i, slot)
        for ref in (acc_up, acc_dn, acc_out, accs, accu):
            ref[...] = jnp.zeros_like(ref)

    @pl.when(i < last)
    def _():
        fetch(i + 1, 1 - slot)

    for cp in in_copies(0, slot, (x_s, o_s, c_s)):
        cp.wait()

    o_t = o_b[slot]
    r1 = x_b[slot].astype(f32) + dot(o_t, w_out[...], 0, 0)
    cen = r1 - jnp.mean(r1, axis=-1, keepdims=True)
    rstd1 = lax.rsqrt(jnp.mean(cen * cen, axis=-1, keepdims=True) + EPSILON)
    xh1 = cen * rstd1
    h1 = (xh1 * g1[...] + b1[...]).astype(bf)
    r2 = h1.astype(f32) + bd[...]
    for c in range(FF // chunk):
        cs = slice(c * chunk, (c + 1) * chunk)
        a, dg = gelu_parts(dot(h1, w_up[:, cs], 1, 0) + bu[:, cs])
        a = a.astype(bf)
        act[:, cs] = a
        dact[:, cs] = dg.astype(dact.dtype)
        r2 = r2 + dot(a, w_down[cs, :], 1, 0)
    cen2 = r2 - jnp.mean(r2, axis=-1, keepdims=True)
    rstd2 = lax.rsqrt(jnp.mean(cen2 * cen2, axis=-1, keepdims=True) + EPSILON)
    xh2 = cen2 * rstd2

    @pl.when(i > 0)
    def _():
        for cp in out_copies(0, (out_s, dr_s, do_s)):
            cp.wait()

    out_b[...] = (xh2 * g2[...] + b2[...]).astype(bf)
    g = c_b[slot].astype(f32)
    dxh = g * g2[...]
    dr2 = rstd2 * (
        dxh - jnp.mean(dxh, axis=-1, keepdims=True) - xh2 * jnp.mean(dxh * xh2, axis=-1, keepdims=True)
    )
    dz2 = dr2.astype(bf)
    accs[4] += fold_rows(g * xh2)
    accs[5] += fold_rows(g)
    accs[2] += fold_rows(dz2.astype(f32))
    dz2_t = dz2.T
    h1_t = h1.T
    dh1 = dr2
    for c in range(FF // chunk):
        cs = slice(c * chunk, (c + 1) * chunk)
        dp1 = (dot(dz2, w_down[cs, :], 1, 1) * dact[:, cs].astype(f32)).astype(bf)
        accu[:, cs] += fold_rows(dp1.astype(f32))
        dh1 = dh1 + dot(dp1, w_up[:, cs], 1, 1)
        acc_up[:, cs] += dot(h1_t, dp1, 1, 0)
        acc_dn[:, cs] += dot(dz2_t, act[:, cs], 1, 0)
    accs[0] += fold_rows(dh1 * xh1)
    accs[1] += fold_rows(dh1)
    dx = dh1 * g1[...]
    dr1 = rstd1 * (
        dx - jnp.mean(dx, axis=-1, keepdims=True) - xh1 * jnp.mean(dx * xh1, axis=-1, keepdims=True)
    )
    da1 = dr1.astype(bf)
    dr_b[...] = dr1
    acc_out[...] += dot(o_t, da1, 1, 0)
    do_b[...] = dot(w_out[...], da1, 1, 1).astype(bf)

    @pl.when(i < n_long)
    def _():
        for cp in out_copies(i, (out_l, dr_l, do_l)):
            cp.start()

    @pl.when(i >= n_long)
    def _():
        for cp in out_copies(i - n_long, (out_s, dr_s, do_s)):
            cp.start()

    @pl.when(i == last)
    def _():
        slots = tile // 128
        half = FF // 2
        pend = []

        def put(rows, copies):
            k = len(pend)
            if k >= slots:
                for cp in pend[k - slots]:
                    cp.wait()
            part = act.at[(k % slots) * 128 : (k % slots + 1) * 128]
            part[:, : rows.shape[1]] = rows.astype(bf)
            pend.append(copies(part, end_sem.at[k % slots]))

        def up_copies(part, sem, r):
            out = []
            for ref, which in ((up_keep, core[0]), (up_send, 1 - core[0])):
                start = pl.multiple_of(which * half, half)
                out.append(pltpu.make_async_copy(part.at[:, pl.ds(start, half)], ref.at[r : r + 128, :], sem))
                out[-1].start()
            return out

        for r in range(0, D, 128):
            put(acc_up[r : r + 128, :], lambda part, sem, r=r: up_copies(part, sem, r))
        for r in range(0, D, 128):
            into = r % (D // 2)
            put(
                acc_dn[r : r + 128, :],
                lambda part, sem, r=r, into=into: to_side(
                    part, dn_keep.at[into : into + 128, :], dn_send.at[into : into + 128, :], core[0] == r // (D // 2), sem
                ),
            )
        for r in range(0, D, 128):
            put(acc_out[r : r + 128, :], lambda part, sem, r=r: started(part.at[:, :D], gout.at[r : r + 128, :], sem))
        small[...] = jnp.sum(accs[...], axis=1)
        small_up[...] = jnp.sum(accu[...], axis=0, keepdims=True)
        for group in pend[-slots:]:
            for cp in group:
                cp.wait()
        for cp in out_copies(0, (out_s, dr_s, do_s)):
            cp.wait()


def started(src, dst, sem):
    copy = pltpu.make_async_copy(src, dst, sem)
    copy.start()
    return [copy]


def dense(core, x_l, x_s, o_l, o_s, c_l, c_s, w_out, w_up, w_down, vecs, bu, tile=512, chunk=1536):
    nl, ns = x_l.shape[0] // tile, x_s.shape[0] // tile
    tl, ts = x_l.shape[0], x_s.shape[0]
    return pl.pallas_call(
        functools.partial(dense_kernel, nl, tile, chunk),
        grid=(nl + ns,),
        in_specs=[SMEM_SPEC]
        + [ANY_SPEC] * 6
        + [const_spec((D, D)), const_spec((D, FF)), const_spec((FF, D))]
        + [const_spec((8, D)), const_spec((1, FF))],
        out_specs=[ANY_SPEC] * 11 + [const_spec((6, D)), const_spec((1, FF))],
        out_shape=[sds((tl, D), bf), sds((ts, D), bf), sds((tl, D), f32), sds((ts, D), f32)]
        + [sds((D, tl), bf), sds((D, ts), bf), sds((D, FF // 2), bf), sds((D, FF // 2), bf)]
        + [sds((D // 2, FF), bf), sds((D // 2, FF), bf), sds((D, D), bf)]
        + [sds((6, D), f32), sds((1, FF), f32)],
        scratch_shapes=[
            pltpu.VMEM((D, FF), f32),
            pltpu.VMEM((D, FF), f32),
            pltpu.VMEM((D, D), f32),
            pltpu.VMEM((tile, FF), bf),
            pltpu.VMEM((tile, FF), f32),
            pltpu.VMEM((6, 8, D), f32),
            pltpu.VMEM((8, FF), f32),
            pltpu.VMEM((2, tile, D), bf),
            pltpu.VMEM((2, D, tile), bf),
            pltpu.VMEM((2, tile, D), bf),
            pltpu.VMEM((tile, D), bf),
            pltpu.VMEM((tile, D), f32),
            pltpu.VMEM((D, tile), bf),
            pltpu.SemaphoreType.DMA((3, 2)),
            pltpu.SemaphoreType.DMA((3,)),
            pltpu.SemaphoreType.DMA((tile // 128,)),
        ],
        compiler_params=params(),
        cost_estimate=cost(2 * (tl + ts) * (3 * D * D + 6 * D * FF), 60e6, (tl + ts) * FF),
        name="dense",
    )(core, x_l, x_s, o_l, o_s, c_l, c_s, w_out, w_up, w_down, vecs, bu)


def back_f_group(lk_g, w_g, q_g, up_g):
    rows = q_g.shape[1]
    probs = head_softmax(dot(spread_heads(lk_g * SCALE), q_g, 1, 0))
    dw = pick_heads(dot(probs.astype(bf), up_g, 1, 1))
    dprobs = dot(spread_heads(w_g), up_g, 1, 0)
    weighted = jnp.sum((probs * dprobs).reshape(4, LM, rows), axis=1, keepdims=True)
    dsf = (probs * (dprobs.reshape(4, LM, rows) - weighted).reshape(GROUP, rows)).astype(bf)
    return dw, dsf, SCALE * pick_heads(dot(dsf, q_g, 1, 1))


def back_f_kernel(units, lk, w, q, up, dw_out, dlk_out, dsf_out, edges):
    w_all = joined(w, units, slice(0, LM))
    rows = q.shape[1]
    edges[0] = jnp.concatenate([up[:, :HALF], up[:, rows - HALF :]], axis=1).T
    dws = []
    for gs in group_slices():
        dw, dsf_out[gs, :], dlk_out[:, gs] = back_f_group(lk[:, gs], w_all[:, gs], q[gs, :], up[gs, :])
        dws.append(dw)
    dws = jnp.concatenate(dws, axis=1)
    width = D // units
    for u in range(units):
        dw_out[u] = dws[:, u * width : (u + 1) * width]


def back_f(lk, w, q, up, items, units):
    rows = q.shape[1] // items
    mark, tok = item_specs(rows)
    width = D // units
    return pl.pallas_call(
        functools.partial(back_f_kernel, units),
        grid=(items,),
        in_specs=[mark, unit_spec(units, LM + 16, width), tok, tok],
        out_specs=[unit_spec(units, LM, width), mark, tok, pl.BlockSpec((1, 2 * HALF, D), lambda i: (i, 0, 0))],
        out_shape=[
            sds((items * units, LM, width), f32),
            sds((items * LM, D), f32),
            sds(q.shape, bf),
            sds((items, 2 * HALF, D), bf),
        ],
        compiler_params=params(),
        cost_estimate=cost(8 * items * rows * D * GROUP, 6 * items * rows * D, items * rows * D),
        name="back_f",
    )(lk, w, q, up)


def back_mix_kernel(senders, dw_in, z, bv, out, dw_out):
    width = z.shape[1]
    dw = dw_in[0]
    for d in range(1, senders):
        dw = dw + dw_in[d]
    dw_out[...] = dw
    dbvs, dots = [], []
    for s in head_slices(width // HD):
        dbv = mm(z[:, s], dw[:, s], 0, 0).astype(bf)
        dots.append(jnp.sum(dbv.astype(f32) * bv[:, s], axis=1, keepdims=True))
        dbvs.append(dbv)
    put_all(out, jnp.concatenate(dbvs, axis=1), three_parts(lanes_of([jnp.concatenate(dots, axis=0)])[:1]))


def back_mix(dw, z, bv, deps=()):
    senders, _, width = dw.shape
    return pl.pallas_call(
        after(functools.partial(back_mix_kernel, senders), 3, deps),
        in_specs=[VMEM_SPEC] * 3 + [ANY_SPEC] * len(deps),
        out_specs=[VMEM_SPEC] * 2,
        out_shape=[sds((senders, LM + 16, width), bf), sds((LM, width), f32)],
        compiler_params=params(),
        cost_estimate=cost(1e8, 4e6),
        name="back_mix",
    )(dw, z, bv, *deps)


def back_inverse_kernel(at, lq_l, lk_l, lq_s, lk_s, dw_l, bv_l, dw_s, bv_s, dlq_l, dlk_l, dlq_s, dlk_s):
    qs, ks, dws, bvs = (lq_l, lq_s), (lk_l, lk_s), (dw_l, dw_s), (bv_l, bv_s)
    heads = own_slices(lq_l, lq_s)
    a_list = [mark_probs(qs[n][:, s], ks[n][:, s]) for n, s in heads]
    kept = []
    inverse_steps(a_list, kept)
    ident = eye()
    dz = [mm(dws[n][:, s], bvs[n][:, s], 1, 1) for n, s in heads]
    da = [jnp.zeros((LM, LM), f32) for _ in heads]
    for z, p, t2, t3 in reversed(kept):
        dt3 = [0.25 * mm(zz, d, 0, 0) for zz, d in zip(z, dz)]
        dz = [0.25 * mm(d, t, 1, 1) for d, t in zip(dz, t3)]
        dp = [-mm(d, t, 1, 1) for d, t in zip(dt3, t2)]
        dt2 = [-mm(pp, d, 0, 0) for pp, d in zip(p, dt3)]
        dp = [x - mm(d, 7.0 * ident - pp, 1, 1) for x, d, pp in zip(dp, dt2, p)]
        dp = [x + mm(pp, d, 0, 0) for x, pp, d in zip(dp, p, dt2)]
        da = [x + mm(d, zz, 1, 1) for x, d, zz in zip(da, dp, z)]
        dz = [x + mm(a, d, 0, 0) for x, a, d in zip(dz, a_list, dp)]
    for (n, s), a, g, d in zip(heads, a_list, da, dz):
        col, row, cm, rm = inverse_start(a)
        norm = cm * rm
        g = g + d.T / norm
        dnorm = -jnp.sum(jnp.sum(d.T * a, axis=1, keepdims=True), axis=0, keepdims=True) / (norm * norm)
        at_col = (col == cm).astype(f32)
        at_row = (row == rm).astype(f32)
        g = g + dnorm * rm * at_col / jnp.sum(at_col, axis=1, keepdims=True)
        g = g + dnorm * cm * at_row / jnp.sum(at_row, axis=0, keepdims=True)
        ds = a * (g - jnp.sum(a * g, axis=1, keepdims=True))
        (dlq_l, dlq_s)[n][:, s] = SCALE * mm(ds, ks[n][:, s].astype(f32))
        (dlk_l, dlk_s)[n][:, s] = SCALE * mm(ds, qs[n][:, s].astype(f32), 0, 0)


def back_inverse(at, lq_l, lk_l, lq_s, lk_s, dw_l, bv_l, dw_s, bv_s, deps=()):
    width = dw_l.shape[1]
    own = pl.BlockSpec((LM, width), lambda i, at: (at[0], at[1]))
    one, all_heads = whole((LM, width)), whole((LM, D))
    return pl.pallas_call(
        after(back_inverse_kernel, 9, deps),
        grid_spec=pltpu.PrefetchScalarGridSpec(
            num_scalar_prefetch=1,
            grid=(1,),
            in_specs=[own, own, all_heads, all_heads, one, one, all_heads, all_heads] + [ANY_SPEC] * len(deps),
            out_specs=[one, one, all_heads, all_heads],
        ),
        out_shape=[sds((LM, width), f32)] * 2 + [sds((LM, D), f32)] * 2,
        compiler_params=params(),
        cost_estimate=cost((width + D) // HD * 72 * 3 * 2 * 64**3 * 20, 2e6),
        name="back_inverse",
    )(at, lq_l, lk_l, lq_s, lk_s, dw_l, bv_l, dw_s, bv_s, *deps)


def back_b_group(k_g, v_g, wide, dots, probs):
    dsb = (probs * (dot(wide, v_g, 1, 0) - dots)).astype(bf)
    return dsb, SCALE * pick_heads(dot(dsb, k_g, 1, 1))


def back_b_kernel(units, lq, w, dbv, k, v, dsb_out, probs_out, dlq_out):
    level = from_parts(joined(w, units, slice(LM, LM + 16)))
    dots = from_parts(joined(dbv, units, slice(LM, LM + 16)))
    dbv_all = joined(dbv, units, slice(0, LM))
    for gs in group_slices():
        probs = jnp.exp(mark_scores(lq[:, gs], k[gs, :], None) - level[gs])
        probs_out[gs, :] = probs.astype(bf)
        dsb_out[gs, :], dlq_out[:, gs] = back_b_group(
            k[gs, :], v[gs, :], spread_heads(dbv_all[:, gs]), dots[gs], probs
        )


def back_b(lq, w, dbv, k, v, items, units, deps=()):
    rows = k.shape[1] // items
    mark, tok = item_specs(rows)
    unit = unit_spec(units, LM + 16, D // units)
    return pl.pallas_call(
        after(functools.partial(back_b_kernel, units), 5, deps),
        grid=(items,),
        in_specs=[mark, unit, unit, tok, tok] + [ANY_SPEC] * len(deps),
        out_specs=[tok, tok, mark],
        out_shape=[sds(k.shape, bf), sds(k.shape, bf), sds((items * LM, D), f32)],
        compiler_params=params(),
        cost_estimate=cost(8 * items * rows * D * GROUP, 10 * items * rows * D, items * rows * D),
        name="back_b",
    )(lq, w, dbv, k, v, *deps)


def back_v_kernel(units, dbv, probs, dconv, x, gv_in, dv_out, gv_out, acc):
    i = pl.program_id(0)

    @pl.when(i == 0)
    def _():
        acc[...] = gv_in[...]

    dbv_all = joined(dbv, units, slice(0, LM))
    for gs in group_slices():
        dv_out[gs, :] = (dot(spread_heads(dbv_all[:, gs]), probs[gs, :], 0, 0) + dconv[gs, :]).astype(bf)
    acc[...] += dot(dv_out[...], x[...], 1, 0)

    @pl.when(i == pl.num_programs(0) - 1)
    def _():
        gv_out[...] = acc[...].T.astype(bf)


def back_v(dbv, probs, dconv, x, gv, items, units, deps=()):
    rows = probs.shape[1] // items
    _, tok = item_specs(rows)
    square = const_spec((D, D))
    return pl.pallas_call(
        after(functools.partial(back_v_kernel, units), 5, deps),
        grid=(items,),
        in_specs=[unit_spec(units, LM + 16, D // units), tok, tok, pl.BlockSpec((rows, D), lambda i: (i, 0)), square]
        + [ANY_SPEC] * len(deps),
        out_specs=[tok, square],
        out_shape=[sds(probs.shape, bf), sds((D, D), bf)],
        scratch_shapes=[pltpu.VMEM((D, D), f32)],
        compiler_params=params(),
        cost_estimate=cost(6 * items * rows * D * GROUP, 12 * items * rows * D),
        name="back_v",
    )(dbv, probs, dconv, x, gv, *deps)


def short_back_kernel(length, q, k, v, lq, lk, z, w, bv, up, dconv, x, dsf_out, dsb_out, dv_out, dlq_out, dlk_out, dw_out, gv_out):
    for gs in group_slices():
        dw, dsf_out[gs, :], dlk_out[:, gs] = back_f_group(lk[:, gs], w[:, gs], q[gs, :], up[gs, :])
        dw_out[:, gs] = dw
        z_g, bv_g = z[:, gs], bv[:, gs]
        dbvs = [mm(z_g[:, s], dw[:, s], 0, 0).astype(bf) for s in head_slices(4)]
        dots = jnp.concatenate(
            [jnp.sum(d.astype(f32) * bv_g[:, s], axis=1, keepdims=True) for d, s in zip(dbvs, head_slices(4))], axis=0
        )
        scores = mark_scores(lq[:, gs], k[gs, :], length[0])
        e = jnp.exp(scores - jnp.max(scores, axis=1, keepdims=True))
        probs = e / jnp.sum(e, axis=1, keepdims=True)
        wide = spread_heads(jnp.concatenate(dbvs, axis=1))
        dsb_out[gs, :], dlq_out[:, gs] = back_b_group(k[gs, :], v[gs, :], wide, dots, probs)
        dv_out[gs, :] = (dot(wide, probs.astype(bf), 0, 0) + dconv[gs, :]).astype(bf)
    gv_out[...] = dot(dv_out[...], x[...], 1, 0)


def short_back(length, q, k, v, lq, lk, z, w, bv, up, dconv, x, deps=()):
    mark = sds((LM, D), f32)
    return pl.pallas_call(
        after(short_back_kernel, 12, deps),
        in_specs=[SMEM_SPEC] + [VMEM_SPEC] * 11 + [ANY_SPEC] * len(deps),
        out_specs=[VMEM_SPEC] * 7,
        out_shape=[sds(q.shape, bf)] * 3 + [mark] * 3 + [sds((D, D), f32)],
        compiler_params=params(),
        cost_estimate=cost(24 * q.size * GROUP, 20 * q.size, 2 * q.size),
        name="short_back",
    )(length, q, k, v, lq, lk, z, w, bv, up, dconv, x, *deps)


def score_part(member, x, lq, lk, dsf, dsb, sq, sk, dq_out, dk_out, acc):
    member2 = jnp.concatenate([member, member], axis=0)
    for n, (marks, scores, sums, out) in enumerate(((lk, dsf, sq, dq_out), (lq, dsb, sk, dk_out))):
        hi, lo = split(sums)
        back = dot(jnp.concatenate([hi, lo], axis=0), member2, 0, 0)
        for gs in group_slices():
            part = (dot(spread_heads(marks[:, gs] * SCALE), scores[gs, :], 0, 0) + back[gs]).astype(bf)
            out[gs, :] = part
    both = jnp.concatenate([dq_out[...], dk_out[...]], axis=0)
    acc[...] += dot(both, x[...], 1, 0)


def score_grads_kernel(n_long, length, core, x_l, lq_l, lk_l, dsf_l, dsb_l, sq_l, sk_l,
                       x_s, lq_s, lk_s, dsf_s, dsb_s, sq_s, sk_s, sq_own, sk_own,
                       dq_l, dk_l, dq_s, dk_s, keep, send, acc, stage, sem):
    i = pl.program_id(0)

    @pl.when(i == 0)
    def _():
        acc[...] = jnp.zeros_like(acc)
        member = short_member(length[0], x_s.shape[0]).astype(bf)
        count = (length[0] // LM).astype(f32)
        sq, sk = (sq_s[...] + sq_own[...]) / count, (sk_s[...] + sk_own[...]) / count
        score_part(member, x_s, lq_s, lk_s, dsf_s, dsb_s, sq, sk, dq_s, dk_s, acc)

    @pl.when(i > 0)
    def _():
        count, rows = sq_l.shape[0], x_l.shape[0]
        member = (iota((count, rows), 1) // (LONG // LM) == iota((count, rows), 0)).astype(f32).astype(bf)
        score_part(member, x_l, lq_l, lk_l, dsf_l, dsb_l, sq_l[...], sk_l[...], dq_l, dk_l, acc)

    @pl.when(i == n_long)
    def _():
        jobs = [
            (lambda: acc[:D, :], lambda src, sem: to_side(src, keep, send, core[0] == 0, sem)),
            (lambda: acc[D:, :], lambda src, sem: to_side(src, keep, send, core[0] == 1, sem)),
        ]
        put_bf16(jobs, stage, sem)


def score_grads(length, core, long_args, short_args, items, deps=()):
    x_l, x_s = long_args[0], short_args[0]
    tl, ts = x_l.shape[0], x_s.shape[0]
    rows = tl // items
    marks_l = long_args[5].shape[0] // items
    at = lambda i: jnp.maximum(i - 1, 0)
    first = lambda i: 0

    def specs(r, marks, f):
        row = pl.BlockSpec((r, D), lambda i: (f(i), 0))
        mark = pl.BlockSpec((LM, D), lambda i: (f(i), 0))
        tok = pl.BlockSpec((D, r), lambda i: (0, f(i)))
        own = pl.BlockSpec((marks, D), lambda i: (f(i), 0))
        return [row, mark, mark, tok, tok, own, own]

    long_out = pl.BlockSpec((D, rows), lambda i: (0, at(i)))
    short_out = pl.BlockSpec((D, ts), lambda i: (0, 0))
    return pl.pallas_call(
        after(functools.partial(score_grads_kernel, items), 18, deps),
        grid=(items + 1,),
        in_specs=[SMEM_SPEC, SMEM_SPEC]
        + specs(rows, marks_l, at)
        + specs(ts, LM, first)
        + [const_spec((LM, D))] * 2
        + [ANY_SPEC] * len(deps),
        out_specs=[long_out] * 2 + [short_out] * 2 + [ANY_SPEC] * 2,
        out_shape=[sds((D, tl), bf)] * 2 + [sds((D, ts), bf)] * 2 + [sds((D, D), bf)] * 2,
        scratch_shapes=[
            pltpu.VMEM((2 * D, D), f32),
            pltpu.VMEM((2, D, D), bf),
            pltpu.SemaphoreType.DMA((2,)),
        ],
        compiler_params=params(),
        cost_estimate=cost(6 * (tl + ts) * D * D, 20 * (tl + ts) * D),
        name="score_grads",
    )(length, core, *long_args, *short_args, *deps)


def input_grad_kernel(n_long, dr_l, dq_l, dk_l, dv_l, dr_s, dq_s, dk_s, dv_s, wq, wk, wv, out_l, out_s, w_all):
    i = pl.program_id(0)
    is_long = i < n_long
    @pl.when(i == 0)
    def _():
        for j, w in enumerate((wq, wk, wv)):
            w_all[:, j * D : (j + 1) * D] = w[...]

    grad = jnp.concatenate(
        [jnp.where(is_long, a[...], b[...]) for a, b in ((dq_l, dq_s), (dk_l, dk_s), (dv_l, dv_s))], axis=0
    )
    total = jnp.where(is_long, dr_l[...], dr_s[...]) + dot(grad, w_all[...], 0, 1)
    total = total.astype(bf)

    @pl.when(is_long)
    def _():
        out_l[...] = total

    @pl.when(jnp.logical_not(is_long))
    def _():
        out_s[...] = total


def input_grad(long_args, short_args, weights, deps=()):
    tl, ts = long_args[0].shape[0], short_args[0].shape[0]
    nl = tl // ts
    at = lambda i: jnp.minimum(i, nl - 1)
    row = lambda f: pl.BlockSpec((ts, D), lambda i: (f(i), 0))
    col = lambda f: pl.BlockSpec((D, ts), lambda i: (0, f(i)))
    first = lambda i: 0
    return pl.pallas_call(
        after(functools.partial(input_grad_kernel, nl), 11, deps),
        grid=(nl + 1,),
        in_specs=[row(at)] + [col(at)] * 3 + [row(first)] + [col(first)] * 3 + [const_spec((D, D))] * 3
        + [ANY_SPEC] * len(deps),
        out_specs=[row(at), row(first)],
        out_shape=[sds((tl, D), bf), sds((ts, D), bf)],
        scratch_shapes=[pltpu.VMEM((D, 3 * D), bf)],
        compiler_params=params(),
        cost_estimate=cost(6 * (tl + ts) * D * D, 12 * (tl + ts) * D),
        name="input_grad",
    )(*long_args, *short_args, *weights, *deps)


def swap(values, axis, bit):
    count = lax.axis_size(axis)
    return lax.ppermute(values, axis, [(i, i ^ bit) for i in range(count)])


def side(axis, bit):
    return (lax.axis_index(axis) // bit) % 2


def exchange(values):
    return lax.all_to_all(values, "seq", 0, 0, tiled=True)


def gather(values):
    return exchange(jnp.broadcast_to(values[None], (lax.axis_size("seq"),) + values.shape))


def tied(values, dep):
    return lax.optimization_barrier(tuple(values) + (dep,))[:-1]


def is_small_mesh():
    return lax.axis_size("dp") == 4 and lax.axis_size("seq") == 8


def pair_sum(keep, send, axis, bit):
    return keep.astype(f32) + swap(send, axis, bit).astype(f32)


class Reduction:
    def __init__(self, keep, send, dim):
        self.dim, self.other = dim, 1 - dim
        self.core, self.x = side("dp", 1), side("dp", 2)
        v = pair_sum(keep, send, "dp", 1)
        if not is_small_mesh():
            self.theirs = v.astype(bf)
            return
        half = v.shape[self.other] // 2
        self.mine = lax.dynamic_slice_in_dim(v, self.x * half, half, self.other).astype(bf)
        self.theirs = lax.dynamic_slice_in_dim(v, (1 - self.x) * half, half, self.other).astype(bf)

    def wait_for(self, dep):
        if is_small_mesh():
            (self.mine,) = tied((self.mine,), dep)

    def over_x(self):
        if not is_small_mesh():
            self.value = self.theirs
            return self.value
        n_seq = lax.axis_size("seq")
        v = pair_sum(self.mine, self.theirs, "dp", 2).astype(bf)
        if self.dim == 0:
            v = v.reshape(n_seq, v.shape[0] // n_seq, v.shape[1])
        else:
            v = v.reshape(v.shape[0], n_seq, v.shape[1] // n_seq).transpose(1, 0, 2)
        self.value = v
        return v

    def over_seq(self):
        if not is_small_mesh():
            self.own = lax.psum_scatter(self.value, "seq", scatter_dimension=self.dim, tiled=True)
        else:
            self.own = jnp.sum(exchange(self.value).astype(f32), axis=0).astype(bf)
        return self.own

    def both(self):
        if not is_small_mesh():
            place = (jnp.arange(2) == self.core).astype(f32)[:, None, None]
            shares = lax.psum(self.own.astype(f32)[None] * place, "dp")
            return shares[0], shares[1]
        got = swap(self.own, "dp", 2)
        v = jnp.where(
            self.x == 0,
            jnp.concatenate([self.own, got], axis=self.other),
            jnp.concatenate([got, self.own], axis=self.other),
        )
        got = swap(v, "dp", 1)
        first = self.core == 0
        return jnp.where(first, v, got).astype(f32), jnp.where(first, got, v).astype(f32)


class Halving(Reduction):
    def __init__(self, keep, send, dim, order):
        if not is_small_mesh():
            super().__init__(keep, send, dim)
            return
        self.dim, self.other = dim, 1 - dim
        self.core, self.x = side("dp", 1), side("dp", 2)
        v = pair_sum(keep, send, "dp", 1)
        rows, n = v.shape
        if dim == 0:
            v = v.reshape(2, 2, 2, rows // 8, n)
        else:
            v = v.reshape(rows, 8, n // 8).transpose(1, 0, 2).reshape(2, 2, 2, rows, n // 8)
        self.left = ["z1", "z0", "y"]
        self.order = list(order)
        self.split(v)

    def split(self, v):
        step = self.order[0]
        if step == "x":
            dim = v.ndim - 1 if self.dim == 0 else v.ndim - 2
            bit = self.x
            size = v.shape[dim] // 2
        else:
            dim = self.left.index(step)
            self.left.pop(dim)
            bit = side("seq", {"y": 1, "z0": 2, "z1": 4}[step])
            size = 1
        take = lambda at: lax.dynamic_slice_in_dim(v, at * size, size, dim).astype(bf)
        self.mine, self.theirs = take(bit), take(1 - bit)
        if step != "x":
            self.mine, self.theirs = (lax.squeeze(u, (dim,)) for u in (self.mine, self.theirs))

    def step(self):
        if not is_small_mesh():
            self.value = self.theirs
            return self.theirs
        axis, bit = {"x": ("dp", 2), "y": ("seq", 1), "z0": ("seq", 2), "z1": ("seq", 4)}[self.order.pop(0)]
        v = pair_sum(self.mine, self.theirs, axis, bit)
        if self.order:
            self.split(v)
            return self.theirs
        self.own = v.astype(bf)
        return self.own

    def last(self):
        if not is_small_mesh():
            self.step()
            return self.over_seq()
        return self.step()


def hold(value, dep):
    return tied((value,), dep)[0]


class SumStages:
    def __init__(self, values):
        self.values = values
        self.steps = [("dp", 1), ("dp", 2), ("seq", 4), ("seq", 2), ("seq", 1)]

    def step(self, dep):
        if is_small_mesh():
            axis, bit = self.steps.pop(0)
            held = hold(self.values, dep)
            self.values = held + swap(held, axis, bit)
        elif len(self.steps) == 5:
            self.steps.pop(0)
            self.values = lax.psum(self.values, ("dp", "seq"))
        return self.values


def neighbours(first, last):
    count = lax.axis_size("seq")
    right = lax.ppermute(first, "seq", [((i + 1) % count, i) for i in range(count)])
    left = lax.ppermute(last, "seq", [(i, (i + 1) % count) for i in range(count)])
    return left, right


def pad_units(values, count):
    have = values.shape[0]
    if have == count:
        return values
    return jnp.concatenate([values, jnp.zeros((count - have,) + values.shape[1:], values.dtype)], axis=0)


def body(x_long, x_short, item_start, short_lengths, w_query, w_key, w_value, w_out, conv_taps, ln1_gain, ln1_bias,
         w_up, up_bias, w_down, down_bias, ln2_gain, ln2_bias, cot_long, cot_short):
    _, items, rows, _ = x_long.shape
    short_rows = x_short.shape[3]
    seg = LONG // LM
    own_marks = rows // seg
    n_seq = lax.axis_size("seq")
    me = lax.axis_index("seq")
    heads_each = next(h for h in (2, 4, 6, 12) if H % h == 0 and items * H // h <= n_seq)
    units = H // heads_each
    width = heads_each * HD
    owners = items * units

    x_l = x_long.reshape(items * rows, D)
    x_s = x_short.reshape(short_rows, D)
    length = short_lengths.reshape(1)
    core = side("dp", 1).astype(jnp.int32).reshape(1)
    mine = jnp.minimum(me, owners - 1).astype(jnp.int32)
    at = jnp.stack([mine // units, mine % units])

    x_mean = jnp.sum(x_long[0].reshape(items, own_marks, seg, D).astype(f32), axis=2) * (1.0 / seg)
    means = gather(x_mean.reshape(items * own_marks, D))
    means = means.reshape(n_seq, items, own_marks, D).transpose(1, 0, 2, 3).reshape(items * LM, D)
    mean_hi, mean_lo = split(means)

    def marks_of(w):
        return (
            jnp.dot(mean_hi, w, preferred_element_type=f32) + jnp.dot(mean_lo, w, preferred_element_type=f32)
        ).astype(bf)

    place = (me - item_start[0]) % n_seq
    open_left = (place > 0)[:, None, None]
    open_right = (place < n_seq - 1)[:, None, None]

    def rims(left, right):
        return jnp.concatenate(
            [jnp.where(open_left, left, jnp.zeros_like(left)), jnp.where(open_right, right, jnp.zeros_like(right))], axis=1
        ).reshape(items * 2 * HALF, D)

    x_rim = rims(*neighbours(x_long[0, :, :HALF], x_long[0, :, rows - HALF :]))
    v_rim = jnp.einsum("ke,nk->en", w_value, x_rim, preferred_element_type=f32).astype(bf)

    tap_rows = jnp.stack([conv_taps.T, conv_taps[::-1].T], axis=1)
    tap_rows = jnp.pad(tap_rows, ((0, 0), (0, 6), (0, 128 - TAPS)))

    q_l, k_l, v_l, q_s, k_s, v_s, lq_s, lk_s = qkv(length, x_l, x_s, w_query, w_key, w_value)
    c_l, c_s = conv(length, v_l, v_s, v_rim, tap_rows, items)
    lq_l, lk_l = marks_of(w_query), marks_of(w_key)

    msg_l = stats(lq_l, k_l, v_l, items, units)
    got_l = exchange(pad_units(msg_l, n_seq))
    z_own, z_s = inverse(at, lq_l, lk_l, lq_s, lk_s, width)
    w_own, bv_own = combine(got_l, z_own)
    w_l = exchange(w_own)[:owners]
    o_s, w_s, bv_s = short_attend(length, q_s, k_s, v_s, lq_s, lk_s, z_s, c_s)
    o_l = mix(lk_l, w_l, q_l, c_l, items, units)

    vecs = jnp.pad(jnp.stack([ln1_gain, ln1_bias, down_bias, ln2_gain, ln2_bias]), ((0, 3), (0, 0)))
    out_l, out_s, dr_l, dr_s, do_l, do_s, up_keep, up_send, dn_keep, dn_send, g_out, small, small_up = dense(
        core, x_l, x_s, o_l, o_s, cot_long.reshape(items * rows, D), cot_short.reshape(short_rows, D), w_out, w_up,
        w_down, vecs, up_bias.reshape(1, -1),
    )

    dw_l, dlk_part, dsf_l, edges = back_f(lk_l, w_l, q_l, do_l, items, units)
    got_dw = exchange(pad_units(dw_l, n_seq))
    up_keep, dn_keep = tied((up_keep, dn_keep), edges)
    up = Halving(up_keep, up_send, 0, ("x", "y", "z0", "z1"))
    down = Halving(dn_keep, dn_send, 1, ("y", "x", "z0", "z1"))
    do_rim = rims(*tied(neighbours(edges[:, :HALF], edges[:, HALF:]) + (up.theirs,), down.theirs)[:2]).T

    dc_l, dc_s, tap_g = conv_back(
        length, v_l, v_s, v_rim, do_l, do_s, do_rim, tap_rows, items, (up.theirs, down.theirs)
    )
    dsf_s, dsb_s, dv_s, dlq_s, dlk_s, dw_s, gv_s = short_back(
        length, q_s, k_s, v_s, lq_s, lk_s, z_s, w_s, bv_s, do_s, dc_s, x_s
    )
    packed = jnp.concatenate([small.reshape(-1), small_up.reshape(-1), tap_g[:, 0, :].reshape(-1)]).reshape(-1, 128)
    packed = SumStages(packed)
    dbv_own, dw_own = back_mix(got_dw, z_own, bv_own, (dv_s,))
    dbv_l = exchange(dbv_own)[:owners]
    dlq_own, dlk_own, dlq_own_s, dlk_own_s = back_inverse(
        at, lq_l, lk_l, lq_s, lk_s, dw_own, bv_own, dw_s, bv_s, (up.step(), down.step())
    )
    dsb_l, probs_l, dlq_part = back_b(
        lq_l, w_l, dbv_l, k_l, v_l, items, units, (up.step(), down.step(), packed.step(dw_own))
    )

    owned = (jnp.arange(owners) == me).astype(f32).reshape(items, units, 1, 1)

    def with_own(part, own):
        return part.reshape(items, LM, D) + (owned * own[None, None]).transpose(0, 2, 1, 3).reshape(items, LM, D)

    dl = jnp.stack([with_own(dlq_part, dlq_own), with_own(dlk_part, dlk_own)]).astype(bf)
    dl = dl.reshape(2 * items, n_seq, own_marks, D).transpose(1, 0, 2, 3)
    dv_l, g_v = back_v(dbv_l, probs_l, dc_l, x_l, gv_s, items, units, (dl,))
    dl = jnp.sum(exchange(dl).astype(f32), axis=0) * (1.0 / seg)
    dl = jnp.pad(dl.reshape(2, items, own_marks, D), ((0, 0), (0, 0), (0, 16 - own_marks), (0, 0)))
    dl = dl.reshape(2, items * 16, D)

    dq_l, dk_l, dq_s, dk_s, qk_keep, qk_send = score_grads(
        length,
        core,
        (x_l, lq_l, lk_l, dsf_l, dsb_l, dl[0], dl[1]),
        (x_s, lq_s, lk_s, dsf_s, dsb_s, dlq_s, dlk_s, dlq_own_s, dlk_own_s),
        items,
        (up.step(), down.step(), g_v, packed.step(dlq_part)),
    )
    query_key = Reduction(qk_keep, qk_send, 1)
    is_first = core[0] == 0
    vo_keep = hold(jnp.where(is_first, g_v, g_out), dq_l)
    value_out = Halving(vo_keep, jnp.where(is_first, g_out, g_v), 0, ("y", "z0", "z1", "x"))
    up.theirs, down.theirs = tied((up.theirs, down.theirs), dq_l)
    grad_l, grad_s = input_grad(
        (dr_l, dq_l, dk_l, dv_l),
        (dr_s, dq_s, dk_s, dv_s),
        (w_query, w_key, w_value),
        (query_key.theirs, value_out.theirs),
    )
    query_key.wait_for(grad_l)
    up.last()
    down.last()
    query_key.over_x()
    ready = query_key.value
    up.own, down.own = tied((up.own, down.own), ready)
    packed.step(ready)
    packed.step(ready)
    value_out.wait_for(ready)
    value_out.step()
    value_out.step()
    value_out.step()
    value_out.last()
    query_key.over_seq()
    up_a, up_b = up.both()
    down_a, down_b = down.both()
    v_a, v_b = value_out.both()
    q_g, k_g = query_key.both()

    packed = packed.step(ready).reshape(-1)
    small = packed[: 6 * D].reshape(6, D)
    small_up = packed[6 * D : 6 * D + FF]
    taps_g = packed[6 * D + FF :].reshape(H, 128)[:, :TAPS].T

    return (
        out_l.reshape(x_long.shape),
        out_s.reshape(x_short.shape),
        grad_l.reshape(x_long.shape),
        grad_s.reshape(x_short.shape),
        q_g.T,
        k_g.T,
        v_a,
        v_b,
        taps_g,
        small[0],
        small[1],
        jnp.concatenate([up_a, up_b], axis=1),
        small_up,
        jnp.concatenate([down_a, down_b], axis=0).T,
        small[2],
        small[4],
        small[5],
    )


def solution(mesh):
    tokens = P("dp", None, "seq", None)
    shorts = P("dp", "seq", None, None, None)
    rows = P("seq", None)
    return jax.shard_map(
        body,
        mesh=mesh,
        in_specs=(tokens, shorts, P("dp", None), P("dp", "seq", None)) + (P(),) * 13 + (tokens, shorts),
        out_specs=(tokens, shorts, tokens, shorts, rows, rows, rows, rows, P(), P(), P(), rows, P(), rows, P(), P(), P()),
        check_vma=False,
    )
```

```python
import functools

import jax
import jax.numpy as jnp
from jax import lax
from jax.experimental import pallas as pl
from jax.experimental.pallas import tpu as pltpu
from jax.sharding import PartitionSpec as P

D = 768
H = 12
HD = 64
FF = 3072
LM = 64
NS_STEPS = 6
HALF = 16
TAPS = 33
LONG = 4096
GROUP = 256
EPSILON = 1e-05
MASKED_SCORE = -1e30
SCALE = 0.125
VMEM_BYTES = 63 * 1024 * 1024

f32 = jnp.float32
bf = jnp.bfloat16
sds = jax.ShapeDtypeStruct


def dot(a, b, ca, cb):
    return lax.dot_general(a, b, (((ca,), (cb,)), ((), ())), preferred_element_type=f32)


def split(v):
    hi = v.astype(bf)
    return hi, (v - hi.astype(f32)).astype(bf)


def mm(a, b, ca=1, cb=0):
    ah, al = split(a)
    bh, bl = split(b)
    return dot(ah, bh, ca, cb) + (dot(ah, bl, ca, cb) + dot(al, bh, ca, cb))


def iota(shape, dim):
    return lax.broadcasted_iota(jnp.int32, shape, dim)


def spread_heads(block):
    tiled = jnp.concatenate([block.astype(f32)] * 4, axis=0)
    same = (iota((GROUP, GROUP), 0) // HD) == (iota((GROUP, GROUP), 1) // HD)
    return jnp.where(same, tiled, 0.0).astype(bf)


def pick_heads(full):
    head = iota((LM, GROUP), 1) // HD
    out = full[:LM]
    for h in range(1, 4):
        out = jnp.where(head == h, full[h * LM : (h + 1) * LM], out)
    return out


def lanes_of(columns):
    n = columns[0].shape[0]
    lane = iota((n, 128), 1)
    wide = jnp.zeros((n, 128), f32)
    for k, col in enumerate(columns):
        wide = jnp.where(lane == k, col, wide)
    return wide.T[:8]


def three_parts(row):
    hi = row.astype(bf).astype(f32)
    mid = (row - hi).astype(bf).astype(f32)
    low = row - hi - mid
    r = iota((16, row.shape[1]), 0)
    return jnp.where(r == 0, hi, jnp.where(r == 1, mid, jnp.where(r == 2, low, 0.0))).astype(bf)


def from_parts(rows):
    v = rows.astype(f32)
    total = v[0:1] + v[1:2] + v[2:3]
    return jnp.broadcast_to(total, (8, total.shape[1])).T[:, 0:1]


def head_softmax(scores):
    rows = scores.shape[1]
    s3 = scores.reshape(4, LM, rows)
    e = jnp.exp(s3 - jnp.max(s3, axis=1, keepdims=True))
    return (e / jnp.sum(e, axis=1, keepdims=True)).reshape(GROUP, rows)


def params(vmem=VMEM_BYTES):
    return pltpu.CompilerParams(vmem_limit_bytes=vmem)


def cost(flops, nbytes, trans=0):
    return pl.CostEstimate(flops=int(flops), bytes_accessed=int(nbytes), transcendentals=int(trans))


SMEM_SPEC = pl.BlockSpec(memory_space=pltpu.SMEM)
ANY_SPEC = pl.BlockSpec(memory_space=pl.ANY)


def after(kernel, count, deps):
    return lambda *refs: kernel(*refs[:count], *refs[count + len(deps) :])


def const_spec(shape):
    return pl.BlockSpec(shape, lambda i: tuple(0 for _ in shape), pipeline_mode=pl.Buffered(1))


def short_member(length, rows):
    seg = length // LM
    lm = iota((LM, rows), 0)
    pos = iota((LM, rows), 1)
    return ((pos >= lm * seg) & (pos < (lm + 1) * seg)).astype(f32)


def project_kernel(n_long, count, length, x_l, x_s, *refs):
    ws, out_l, out_s = refs[:count], refs[count : 2 * count], refs[2 * count : 3 * count]
    marks, w_t = refs[3 * count :]
    i = pl.program_id(0)

    @pl.when(i == 0)
    def _():
        for j, w in enumerate(ws):
            w_t[j * D : (j + 1) * D, :] = w[...].T

    x = jnp.where(i < n_long, x_l[...], x_s[...])
    made = dot(w_t[...], x, 1, 1).astype(bf)
    made = [made[j * D : (j + 1) * D] for j in range(count)]

    @pl.when(i < n_long)
    def _():
        for ref, v in zip(out_l, made):
            ref[...] = v

    @pl.when(i >= n_long)
    def _():
        for ref, v in zip(out_s, made):
            ref[...] = v
        member = short_member(length[0], made[0].shape[1]).astype(bf)
        marks[...] = (dot(member, made[0], 1, 1) / (length[0] // LM).astype(f32)).astype(bf)


def project(length, x_l, x_s, ws, deps=()):
    tile = x_s.shape[0]
    n = len(ws)
    nl = x_l.shape[0] // tile
    long_at = lambda i: jnp.minimum(i, nl - 1)
    row = lambda f: pl.BlockSpec((tile, D), lambda i: (f(i), 0))
    col = lambda f: pl.BlockSpec((D, tile), lambda i: (0, f(i)))
    first = lambda i: 0
    tl, ts = x_l.shape[0], x_s.shape[0]
    out = pl.pallas_call(
        after(functools.partial(project_kernel, nl, n), 3 + n, deps),
        grid=(nl + 1,),
        in_specs=[SMEM_SPEC, row(long_at), row(first)] + [const_spec((D, D))] * n + [ANY_SPEC] * len(deps),
        out_specs=[col(long_at)] * n + [col(first)] * n + [pl.BlockSpec((LM, D), lambda i: (0, 0))],
        out_shape=[sds((D, tl), bf)] * n + [sds((D, ts), bf)] * n + [sds((LM, D), bf)],
        scratch_shapes=[pltpu.VMEM((n * D, D), bf)],
        compiler_params=params(),
        cost_estimate=cost(2 * n * (tl + ts) * D * D, 4 * n * (tl + ts) * D),
        name="project",
    )(length, x_l, x_s, *ws, *deps)
    return out[:n], out[n : 2 * n], out[2 * n]


def mark_scores(lq_g, k_g, limit):
    scores = dot(spread_heads(lq_g * SCALE), k_g, 1, 0)
    if limit is not None:
        scores = jnp.where(iota(scores.shape, 1) < limit, scores, MASKED_SCORE)
    return scores


def group_slices():
    return [slice(g * GROUP, (g + 1) * GROUP) for g in range(3)]


def stats_kernel(units, lq, k, v, msg):
    sums, stats = [], []
    for gs in group_slices():
        scores = mark_scores(lq[:, gs], k[gs, :], None)
        most = jnp.max(scores, axis=1, keepdims=True)
        e = jnp.exp(scores - most)
        stats.append(lanes_of([most, jnp.sum(e, axis=1, keepdims=True)]))
        sums.append(pick_heads(dot(e.astype(bf), v[gs, :], 1, 1)))
    sums = jnp.concatenate(sums, axis=1)
    stats = jnp.concatenate(stats, axis=1)
    width = D // units
    for u in range(units):
        us = slice(u * width, (u + 1) * width)
        msg[u, :LM, :] = sums[:, us]
        msg[u, LM:, :] = stats[:, us]


def item_specs(rows):
    mark = pl.BlockSpec((LM, D), lambda i: (i, 0))
    tok = pl.BlockSpec((D, rows), lambda i: (0, i))
    return mark, tok


def stats(lq, k, v, items, units):
    rows = k.shape[1] // items
    mark, tok = item_specs(rows)
    return pl.pallas_call(
        functools.partial(stats_kernel, units),
        grid=(items,),
        in_specs=[mark, tok, tok],
        out_specs=pl.BlockSpec((units, LM + 8, D // units), lambda i: (i, 0, 0)),
        out_shape=sds((items * units, LM + 8, D // units), f32),
        compiler_params=params(),
        cost_estimate=cost(4 * items * rows * D * GROUP, 4 * items * rows * D, items * rows * D),
        name="stats",
    )(lq, k, v)


def eye():
    return jnp.where(iota((LM, LM), 0) == iota((LM, LM), 1), 1.0, 0.0).astype(f32)


def head_slices(count):
    return [slice(h * HD, (h + 1) * HD) for h in range(count)]


def mark_probs(q, k):
    s = SCALE * dot(q, k, 1, 1)
    e = jnp.exp(s - jnp.max(s, axis=-1, keepdims=True))
    return e / jnp.sum(e, axis=-1, keepdims=True)


def inverse_start(a):
    col = jnp.sum(a, axis=0, keepdims=True)
    row = jnp.sum(a, axis=1, keepdims=True)
    return col, row, jnp.max(col, axis=1, keepdims=True), jnp.max(row, axis=0, keepdims=True)


def inverse_steps(a_list, kept=None):
    ident = eye()
    z_list = []
    for a in a_list:
        _, _, cm, rm = inverse_start(a)
        z_list.append(a.T / (cm * rm))
    for _ in range(NS_STEPS):
        p_list = [mm(a, z) for a, z in zip(a_list, z_list)]
        t2 = [15.0 * ident - mm(p, 7.0 * ident - p) for p in p_list]
        t3 = [13.0 * ident - mm(p, t) for p, t in zip(p_list, t2)]
        if kept is not None:
            kept.append((z_list, p_list, t2, t3))
        z_list = [0.25 * mm(z, t) for z, t in zip(z_list, t3)]
    return z_list


def own_slices(*refs):
    return [(k, s) for k, ref in enumerate(refs) for s in head_slices(ref.shape[1] // HD)]


def inverse_kernel(at, lq_l, lk_l, lq_s, lk_s, z_l, z_s):
    qs, ks, zs = (lq_l, lq_s), (lk_l, lk_s), (z_l, z_s)
    heads = own_slices(lq_l, lq_s)
    a_list = [mark_probs(qs[n][:, s], ks[n][:, s]) for n, s in heads]
    for (n, s), z in zip(heads, inverse_steps(a_list)):
        zs[n][:, s] = z


def whole(shape):
    return pl.BlockSpec(shape, lambda i, at: tuple(0 for _ in shape))


def inverse(at, lq_l, lk_l, lq_s, lk_s, width):
    own = pl.BlockSpec((LM, width), lambda i, at: (at[0], at[1]))
    return pl.pallas_call(
        inverse_kernel,
        grid_spec=pltpu.PrefetchScalarGridSpec(
            num_scalar_prefetch=1,
            grid=(1,),
            in_specs=[own, own, whole((LM, D)), whole((LM, D))],
            out_specs=[whole((LM, width)), whole((LM, D))],
        ),
        out_shape=[sds((LM, width), f32), sds((LM, D), f32)],
        compiler_params=params(),
        cost_estimate=cost((width + D) // HD * 24 * 3 * 2 * 64**3 * 20, 1e6),
        name="inverse",
    )(at, lq_l, lk_l, lq_s, lk_s)


def put_all(out, marks, parts):
    for d in range(out.shape[0]):
        out[d, :LM, :] = marks
        out[d, LM:, :] = parts


def combine_kernel(senders, msg, z, out, bv_out):
    width = z.shape[1]
    most = jnp.concatenate([msg[d, LM : LM + 1, :] for d in range(senders)], axis=0)
    part = jnp.concatenate([msg[d, LM + 1 : LM + 2, :] for d in range(senders)], axis=0)
    top = jnp.max(most, axis=0, keepdims=True)
    e = jnp.exp(most - top)
    total = jnp.sum(part * e, axis=0, keepdims=True)
    weight = (e / total).T
    w_all = []
    for s in head_slices(width // HD):
        bv = jnp.zeros((LM, HD), f32)
        for d in range(senders):
            bv = bv + weight[s, d : d + 1] * msg[d, :LM, s]
        bv_out[:, s] = bv
        w_all.append(mm(z[:, s], bv))
    put_all(out, jnp.concatenate(w_all, axis=1).astype(bf), three_parts(top + jnp.log(total)))


VMEM_SPEC = pl.BlockSpec(memory_space=pltpu.VMEM)


def combine(msg, z):
    senders, _, width = msg.shape
    return pl.pallas_call(
        functools.partial(combine_kernel, senders),
        in_specs=[VMEM_SPEC] * 2,
        out_specs=[VMEM_SPEC] * 2,
        out_shape=[sds((senders, LM + 16, width), bf), sds((LM, width), f32)],
        compiler_params=params(),
        cost_estimate=cost(1e8, 4e6),
        name="combine",
    )(msg, z)


def joined(ref, units, rows):
    return jnp.concatenate([ref[u, rows, :] for u in range(units)], axis=1)


def mark_mix(lk_g, w_g, q_g, conv_g):
    probs = head_softmax(dot(spread_heads(lk_g * SCALE), q_g, 1, 0)).astype(bf)
    return (dot(spread_heads(w_g), probs, 0, 0) + conv_g).astype(bf)


def mix_kernel(units, lk, w, q, conv, out):
    w_all = joined(w, units, slice(0, LM))
    for gs in group_slices():
        out[gs, :] = mark_mix(lk[:, gs], w_all[:, gs], q[gs, :], conv[gs, :])


def short_kernel(length, q, k, v, lq, lk, z, conv, out, w_out, bv_out):
    for gs in group_slices():
        scores = mark_scores(lq[:, gs], k[gs, :], length[0])
        e = jnp.exp(scores - jnp.max(scores, axis=1, keepdims=True))
        probs = e / jnp.sum(e, axis=1, keepdims=True)
        bv = pick_heads(dot(probs.astype(bf), v[gs, :], 1, 1))
        bv_out[:, gs] = bv
        z_g = z[:, gs]
        w = jnp.concatenate([mm(z_g[:, s], bv[:, s]) for s in head_slices(4)], axis=1).astype(bf)
        w_out[:, gs] = w
        out[gs, :] = mark_mix(lk[:, gs], w, q[gs, :], conv[gs, :])


def short_attend(length, q, k, v, lq, lk, z, conv):
    return pl.pallas_call(
        short_kernel,
        in_specs=[SMEM_SPEC] + [VMEM_SPEC] * 7,
        out_specs=[VMEM_SPEC] * 3,
        out_shape=[sds(q.shape, bf), sds((LM, D), bf), sds((LM, D), f32)],
        compiler_params=params(),
        cost_estimate=cost(4 * q.size * GROUP * 2, 10 * q.size, 2 * q.size),
        name="short_attend",
    )(length, q, k, v, lq, lk, z, conv)


def unit_spec(units, rows, width):
    return pl.BlockSpec((units, rows, width), lambda i: (i, 0, 0))


def mix(lk, w, q, conv, items, units):
    rows = q.shape[1] // items
    mark, tok = item_specs(rows)
    return pl.pallas_call(
        functools.partial(mix_kernel, units),
        grid=(items,),
        in_specs=[mark, unit_spec(units, LM + 16, D // units), tok, tok],
        out_specs=tok,
        out_shape=sds(q.shape, bf),
        compiler_params=params(),
        cost_estimate=cost(4 * items * rows * D * GROUP, 8 * items * rows * D, items * rows * D),
        name="mix",
    )(lk, w, q, conv)


def windows(body, rim, items, rows, limit):
    out = []
    for j in range(items):
        own = body[:, j * rows : (j + 1) * rows]
        if limit is not None:
            own = jnp.where(iota(own.shape, 1) < limit, own.astype(f32), 0.0).astype(bf)
        wide = jnp.concatenate(
            [rim[:, 32 * j : 32 * j + HALF], own, rim[:, 32 * j + HALF : 32 * j + 2 * HALF]], axis=1
        )
        for t in range(rows // 128):
            out.append(wide[:, t * 128 : t * 128 + 128 + 2 * HALF])
    return jnp.concatenate(out, axis=0)


def band(row):
    wide = jnp.concatenate([row, jnp.zeros((1, 128), f32)], axis=1)
    rolled = pltpu.roll(jnp.broadcast_to(wide, (128, 256)), 0, 1, stride=1, stride_axis=0)
    return split(rolled[:, : 128 + 2 * HALF])


HEAD_STEP = 3


def unstack(stacked, out, at, items, rows, limit=None):
    k = 0
    for j in range(items):
        for t in range(rows // 128):
            v = stacked[k * HD : (k + 1) * HD]
            if limit is not None:
                v = jnp.where(iota(v.shape, 1) + t * 128 < limit, v, 0.0)
            out[at, j * rows + t * 128 : j * rows + (t + 1) * 128] = v
            k += 1


def both_windows(v_l, v_s, rim, at, items, limit):
    no_rim = jnp.zeros((HD, 2 * HALF), bf)
    rows, short_rows = v_l.shape[1] // items, v_s.shape[1]
    return jnp.concatenate(
        [
            windows(v_l[at, :], rim[at, :], items, rows, None),
            windows(v_s[at, :], no_rim, 1, short_rows, limit),
        ],
        axis=0,
    )


def banded(wins, row, out_l, out_s, at, items, limit):
    hi, lo = band(row)
    made = dot(wins, hi, 1, 1) + dot(wins, lo, 1, 1)
    cut = HD * out_l.shape[1] // 128
    unstack(made[:cut], out_l, at, items, out_l.shape[1] // items)
    unstack(made[cut:], out_s, at, 1, out_s.shape[1], limit)


def conv_kernel(items, length, v_l, v_s, rim, taps, out_l, out_s):
    for h in range(HEAD_STEP):
        at = slice(h * HD, (h + 1) * HD)
        wins = both_windows(v_l, v_s, rim, at, items, length[0])
        banded(wins, taps[h, 0:1, :], out_l, out_s, at, items, None)


def conv_specs(v_l, v_s, rim):
    n = HEAD_STEP * HD
    spec = lambda a: pl.BlockSpec((n, a.shape[1]), lambda h: (h, 0))
    return spec(v_l), spec(v_s), spec(rim), pl.BlockSpec((HEAD_STEP, 8, 128), lambda h: (h, 0, 0))


def conv(length, v_l, v_s, rim, taps, items):
    tok_l, tok_s, rims, tap = conv_specs(v_l, v_s, rim)
    return pl.pallas_call(
        functools.partial(conv_kernel, items),
        grid=(H // HEAD_STEP,),
        in_specs=[SMEM_SPEC, tok_l, tok_s, rims, tap],
        out_specs=[tok_l, tok_s],
        out_shape=[sds(v_l.shape, f32), sds(v_s.shape, f32)],
        compiler_params=params(),
        cost_estimate=cost(4 * 512 * v_l.size, 8 * v_l.size),
        name="conv",
    )(length, v_l, v_s, rim, taps)


def conv_back_kernel(items, length, v_l, v_s, rim, up_l, up_s, up_rim, taps, out_l, out_s, tap_grad):
    flip = (iota((128, 128), 0) + iota((128, 128), 1) == 127).astype(f32).astype(bf)
    for h in range(HEAD_STEP):
        at = slice(h * HD, (h + 1) * HD)
        wins = both_windows(v_l, v_s, rim, at, items, length[0])
        up_wins = both_windows(up_l, up_s, up_rim, at, items, None)
        banded(up_wins, taps[h, 1:2, :], out_l, out_s, at, items, length[0])
        ups = [up_l[at, t * 128 : (t + 1) * 128] for t in range(up_l.shape[1] // 128)]
        ups += [up_s[at, t * 128 : (t + 1) * 128] for t in range(up_s.shape[1] // 128)]
        gram = dot(jnp.concatenate(ups, axis=0), wins, 0, 0)
        hi, lo = split(gram)
        gram = dot(flip, hi, 1, 0) + dot(flip, lo, 1, 0)
        gram = jnp.concatenate([gram, jnp.zeros((128, 256 - gram.shape[1]), f32)], axis=1)
        skewed = pltpu.roll(gram, 129, 1, stride=1, stride_axis=0)
        tap_grad[h] = jnp.broadcast_to(jnp.sum(skewed, axis=0, keepdims=True)[:, :128], (8, 128))


def conv_back(length, v_l, v_s, rim, up_l, up_s, up_rim, taps, items, deps=()):
    tok_l, tok_s, rims, tap = conv_specs(v_l, v_s, rim)
    return pl.pallas_call(
        after(functools.partial(conv_back_kernel, items), 8, deps),
        grid=(H // HEAD_STEP,),
        in_specs=[SMEM_SPEC, tok_l, tok_s, rims, tok_l, tok_s, rims, tap] + [ANY_SPEC] * len(deps),
        out_specs=[tok_l, tok_s, tap],
        out_shape=[sds(v_l.shape, f32), sds(v_s.shape, f32), sds((H, 8, 128), f32)],
        compiler_params=params(),
        cost_estimate=cost(6 * 512 * v_l.size, 12 * v_l.size),
        name="conv_back",
    )(length, v_l, v_s, rim, up_l, up_s, up_rim, taps, *deps)


def fold_rows(v):
    return jnp.sum(v.reshape(v.shape[0] // 8, 8, v.shape[1]), axis=0)


def gelu_parts(x):
    e = jnp.exp(x * x * (-0.5))
    t = pl.reciprocal(1.0 + jnp.abs(x) * (0.3275911 * 0.7071067811865476), approx=False)
    poly = t * (
        0.127414796 + t * (-0.142248368 + t * (0.7107068705 + t * (-0.7265760135 + t * 0.5307027145)))
    )
    tail = poly * e
    phi = jnp.where(x >= 0, 1.0 - tail, tail)
    return x * phi, phi + x * e * 0.3989422804014327


def put_bf16(jobs, stage, sem):
    pend = []
    for k, (load, copies) in enumerate(jobs):
        slot = k % 2
        if k >= 2:
            for cp in pend[k - 2]:
                cp.wait()
        stage[slot] = load().astype(bf)
        pend.append(copies(stage.at[slot], sem.at[slot]))
    for group in pend[-2:]:
        for cp in group:
            cp.wait()


def to_side(src, keep, send, keeps, sem):
    copy = pltpu.make_async_copy(src, keep, sem)

    @pl.when(keeps)
    def _():
        copy.start()

    @pl.when(jnp.logical_not(keeps))
    def _():
        pltpu.make_async_copy(src, send, sem).start()

    return [copy]


def dense_kernel(n_long, tile, chunk, core, x_l, x_s, o_l, o_s, c_l, c_s, w_out, w_up, w_down, vecs, bu,
                 out_l, out_s, dr_l, dr_s, do_l, do_s, up_keep, up_send, dn_keep, dn_send, vo_keep, vo_send, small, small_up,
                 acc_up, acc_dn, acc_out, act, dact, accs, accu, x_b, o_b, c_b, out_b, dr_b, do_b,
                 in_sem, out_sem, end_sem):
    i = pl.program_id(0)
    last = pl.num_programs(0) - 1
    slot = lax.rem(i, 2)
    g1, b1, bd, g2, b2 = (vecs.at[k : k + 1] for k in range(5))

    def at(step):
        return pl.ds(pl.multiple_of(step * tile, tile), tile)

    def in_copies(step, to, refs):
        x, o, c = refs
        return [
            pltpu.make_async_copy(x.at[at(step), :], x_b.at[to], in_sem.at[0, to]),
            pltpu.make_async_copy(o.at[:, at(step)], o_b.at[to], in_sem.at[1, to]),
            pltpu.make_async_copy(c.at[at(step), :], c_b.at[to], in_sem.at[2, to]),
        ]

    def fetch(step, to):
        @pl.when(step < n_long)
        def _():
            for cp in in_copies(step, to, (x_l, o_l, c_l)):
                cp.start()

        @pl.when(step >= n_long)
        def _():
            for cp in in_copies(step - n_long, to, (x_s, o_s, c_s)):
                cp.start()

    def out_copies(step, refs):
        out, dr, do = refs
        return [
            pltpu.make_async_copy(out_b, out.at[at(step), :], out_sem.at[0]),
            pltpu.make_async_copy(dr_b, dr.at[at(step), :], out_sem.at[1]),
            pltpu.make_async_copy(do_b, do.at[:, at(step)], out_sem.at[2]),
        ]

    @pl.when(i == 0)
    def _():
        fetch(i, slot)
        for ref in (acc_up, acc_dn, acc_out, accs, accu):
            ref[...] = jnp.zeros_like(ref)

    @pl.when(i < last)
    def _():
        fetch(i + 1, 1 - slot)

    for cp in in_copies(0, slot, (x_s, o_s, c_s)):
        cp.wait()

    o_t = o_b[slot]
    r1 = x_b[slot].astype(f32) + dot(o_t, w_out[...], 0, 0)
    cen = r1 - jnp.mean(r1, axis=-1, keepdims=True)
    rstd1 = lax.rsqrt(jnp.mean(cen * cen, axis=-1, keepdims=True) + EPSILON)
    xh1 = cen * rstd1
    h1 = (xh1 * g1[...] + b1[...]).astype(bf)
    r2 = h1.astype(f32) + bd[...]
    for c in range(FF // chunk):
        cs = slice(c * chunk, (c + 1) * chunk)
        a, dg = gelu_parts(dot(h1, w_up[:, cs], 1, 0) + bu[:, cs])
        a = a.astype(bf)
        act[:, cs] = a
        dact[:, cs] = dg.astype(dact.dtype)
        r2 = r2 + dot(a, w_down[cs, :], 1, 0)
    cen2 = r2 - jnp.mean(r2, axis=-1, keepdims=True)
    rstd2 = lax.rsqrt(jnp.mean(cen2 * cen2, axis=-1, keepdims=True) + EPSILON)
    xh2 = cen2 * rstd2

    @pl.when(i > 0)
    def _():
        for cp in out_copies(0, (out_s, dr_s, do_s)):
            cp.wait()

    out_b[...] = (xh2 * g2[...] + b2[...]).astype(bf)
    g = c_b[slot].astype(f32)
    dxh = g * g2[...]
    dr2 = rstd2 * (
        dxh - jnp.mean(dxh, axis=-1, keepdims=True) - xh2 * jnp.mean(dxh * xh2, axis=-1, keepdims=True)
    )
    dz2 = dr2.astype(bf)
    accs[4] += fold_rows(g * xh2)
    accs[5] += fold_rows(g)
    accs[2] += fold_rows(dz2.astype(f32))
    dz2_t = dz2.T
    h1_t = h1.T
    dh1 = dr2
    for c in range(FF // chunk):
        cs = slice(c * chunk, (c + 1) * chunk)
        dp1 = (dot(dz2, w_down[cs, :], 1, 1) * dact[:, cs].astype(f32)).astype(bf)
        accu[:, cs] += fold_rows(dp1.astype(f32))
        dh1 = dh1 + dot(dp1, w_up[:, cs], 1, 1)
        acc_up[:, cs] += dot(h1_t, dp1, 1, 0)
        acc_dn[:, cs] += dot(dz2_t, act[:, cs], 1, 0)
    accs[0] += fold_rows(dh1 * xh1)
    accs[1] += fold_rows(dh1)
    dx = dh1 * g1[...]
    dr1 = rstd1 * (
        dx - jnp.mean(dx, axis=-1, keepdims=True) - xh1 * jnp.mean(dx * xh1, axis=-1, keepdims=True)
    )
    da1 = dr1.astype(bf)
    dr_b[...] = dr1
    acc_out[...] += dot(o_t, da1, 1, 0)
    do_b[...] = dot(w_out[...], da1, 1, 1).astype(bf)

    @pl.when(i < n_long)
    def _():
        for cp in out_copies(i, (out_l, dr_l, do_l)):
            cp.start()

    @pl.when(i >= n_long)
    def _():
        for cp in out_copies(i - n_long, (out_s, dr_s, do_s)):
            cp.start()

    @pl.when(i == last)
    def _():
        slots = tile // 128
        half = FF // 2
        pend = []

        def put(rows, copies):
            k = len(pend)
            if k >= slots:
                for cp in pend[k - slots]:
                    cp.wait()
            part = act.at[(k % slots) * 128 : (k % slots + 1) * 128]
            part[:, : rows.shape[1]] = rows.astype(bf)
            pend.append(copies(part, end_sem.at[k % slots]))

        def up_copies(part, sem, r):
            out = []
            for ref, which in ((up_keep, core[0]), (up_send, 1 - core[0])):
                start = pl.multiple_of(which * half, half)
                out.append(pltpu.make_async_copy(part.at[:, pl.ds(start, half)], ref.at[r : r + 128, :], sem))
                out[-1].start()
            return out

        for r in range(0, D, 128):
            put(acc_up[r : r + 128, :], lambda part, sem, r=r: up_copies(part, sem, r))
        for r in range(0, D, 128):
            into = r % (D // 2)
            put(
                acc_dn[r : r + 128, :],
                lambda part, sem, r=r, into=into: to_side(
                    part, dn_keep.at[into : into + 128, :], dn_send.at[into : into + 128, :], core[0] == r // (D // 2), sem
                ),
            )
        for r in range(0, D, 128):
            put(
                acc_out[r : r + 128, :],
                lambda part, sem, r=r: to_side(
                    part.at[:, :D], vo_keep.at[r : r + 128, :], vo_send.at[r : r + 128, :], core[0] == 1, sem
                ),
            )
        small[...] = jnp.sum(accs[...], axis=1)
        small_up[...] = jnp.sum(accu[...], axis=0, keepdims=True)
        for group in pend[-slots:]:
            for cp in group:
                cp.wait()
        for cp in out_copies(0, (out_s, dr_s, do_s)):
            cp.wait()


def dense(core, x_l, x_s, o_l, o_s, c_l, c_s, w_out, w_up, w_down, vecs, bu, tile=512, chunk=1536):
    nl, ns = x_l.shape[0] // tile, x_s.shape[0] // tile
    tl, ts = x_l.shape[0], x_s.shape[0]
    return pl.pallas_call(
        functools.partial(dense_kernel, nl, tile, chunk),
        grid=(nl + ns,),
        in_specs=[SMEM_SPEC]
        + [ANY_SPEC] * 6
        + [const_spec((D, D)), const_spec((D, FF)), const_spec((FF, D))]
        + [const_spec((8, D)), const_spec((1, FF))],
        out_specs=[ANY_SPEC] * 12 + [const_spec((6, D)), const_spec((1, FF))],
        out_shape=[sds((tl, D), bf), sds((ts, D), bf), sds((tl, D), f32), sds((ts, D), f32)]
        + [sds((D, tl), bf), sds((D, ts), bf), sds((D, FF // 2), bf), sds((D, FF // 2), bf)]
        + [sds((D // 2, FF), bf), sds((D // 2, FF), bf), sds((D, D), bf), sds((D, D), bf)]
        + [sds((6, D), f32), sds((1, FF), f32)],
        scratch_shapes=[
            pltpu.VMEM((D, FF), f32),
            pltpu.VMEM((D, FF), f32),
            pltpu.VMEM((D, D), f32),
            pltpu.VMEM((tile, FF), bf),
            pltpu.VMEM((tile, FF), f32),
            pltpu.VMEM((6, 8, D), f32),
            pltpu.VMEM((8, FF), f32),
            pltpu.VMEM((2, tile, D), bf),
            pltpu.VMEM((2, D, tile), bf),
            pltpu.VMEM((2, tile, D), bf),
            pltpu.VMEM((tile, D), bf),
            pltpu.VMEM((tile, D), f32),
            pltpu.VMEM((D, tile), bf),
            pltpu.SemaphoreType.DMA((3, 2)),
            pltpu.SemaphoreType.DMA((3,)),
            pltpu.SemaphoreType.DMA((tile // 128,)),
        ],
        compiler_params=params(),
        cost_estimate=cost(2 * (tl + ts) * (3 * D * D + 6 * D * FF), 60e6, (tl + ts) * FF),
        name="dense",
    )(core, x_l, x_s, o_l, o_s, c_l, c_s, w_out, w_up, w_down, vecs, bu)


def back_f_group(lk_g, w_g, q_g, up_g):
    rows = q_g.shape[1]
    probs = head_softmax(dot(spread_heads(lk_g * SCALE), q_g, 1, 0))
    dw = pick_heads(dot(probs.astype(bf), up_g, 1, 1))
    dprobs = dot(spread_heads(w_g), up_g, 1, 0)
    weighted = jnp.sum((probs * dprobs).reshape(4, LM, rows), axis=1, keepdims=True)
    dsf = (probs * (dprobs.reshape(4, LM, rows) - weighted).reshape(GROUP, rows)).astype(bf)
    return dw, dsf, SCALE * pick_heads(dot(dsf, q_g, 1, 1))


def back_f_kernel(units, lk, w, q, up, dw_out, dlk_out, dsf_out, edges):
    w_all = joined(w, units, slice(0, LM))
    rows = q.shape[1]
    edges[0] = jnp.concatenate([up[:, :HALF], up[:, rows - HALF :]], axis=1).T
    dws = []
    for gs in group_slices():
        dw, dsf_out[gs, :], dlk_out[:, gs] = back_f_group(lk[:, gs], w_all[:, gs], q[gs, :], up[gs, :])
        dws.append(dw)
    dws = jnp.concatenate(dws, axis=1)
    width = D // units
    for u in range(units):
        dw_out[u] = dws[:, u * width : (u + 1) * width]


def back_f(lk, w, q, up, items, units):
    rows = q.shape[1] // items
    mark, tok = item_specs(rows)
    width = D // units
    return pl.pallas_call(
        functools.partial(back_f_kernel, units),
        grid=(items,),
        in_specs=[mark, unit_spec(units, LM + 16, width), tok, tok],
        out_specs=[unit_spec(units, LM, width), mark, tok, pl.BlockSpec((1, 2 * HALF, D), lambda i: (i, 0, 0))],
        out_shape=[
            sds((items * units, LM, width), f32),
            sds((items * LM, D), f32),
            sds(q.shape, bf),
            sds((items, 2 * HALF, D), bf),
        ],
        compiler_params=params(),
        cost_estimate=cost(8 * items * rows * D * GROUP, 6 * items * rows * D, items * rows * D),
        name="back_f",
    )(lk, w, q, up)


def back_mix_kernel(senders, dw_in, z, bv, out, dw_out):
    width = z.shape[1]
    dw = dw_in[0]
    for d in range(1, senders):
        dw = dw + dw_in[d]
    dw_out[...] = dw
    dbvs, dots = [], []
    for s in head_slices(width // HD):
        dbv = mm(z[:, s], dw[:, s], 0, 0).astype(bf)
        dots.append(jnp.sum(dbv.astype(f32) * bv[:, s], axis=1, keepdims=True))
        dbvs.append(dbv)
    put_all(out, jnp.concatenate(dbvs, axis=1), three_parts(lanes_of([jnp.concatenate(dots, axis=0)])[:1]))


def back_mix(dw, z, bv, deps=()):
    senders, _, width = dw.shape
    return pl.pallas_call(
        after(functools.partial(back_mix_kernel, senders), 3, deps),
        in_specs=[VMEM_SPEC] * 3 + [ANY_SPEC] * len(deps),
        out_specs=[VMEM_SPEC] * 2,
        out_shape=[sds((senders, LM + 16, width), bf), sds((LM, width), f32)],
        compiler_params=params(),
        cost_estimate=cost(1e8, 4e6),
        name="back_mix",
    )(dw, z, bv, *deps)


def back_inverse_kernel(at, lq_l, lk_l, lq_s, lk_s, dw_l, bv_l, dw_s, bv_s, dlq_l, dlk_l, dlq_s, dlk_s):
    qs, ks, dws, bvs = (lq_l, lq_s), (lk_l, lk_s), (dw_l, dw_s), (bv_l, bv_s)
    heads = own_slices(lq_l, lq_s)
    a_list = [mark_probs(qs[n][:, s], ks[n][:, s]) for n, s in heads]
    kept = []
    inverse_steps(a_list, kept)
    ident = eye()
    dz = [mm(dws[n][:, s], bvs[n][:, s], 1, 1) for n, s in heads]
    da = [jnp.zeros((LM, LM), f32) for _ in heads]
    for z, p, t2, t3 in reversed(kept):
        dt3 = [0.25 * mm(zz, d, 0, 0) for zz, d in zip(z, dz)]
        dz = [0.25 * mm(d, t, 1, 1) for d, t in zip(dz, t3)]
        dp = [-mm(d, t, 1, 1) for d, t in zip(dt3, t2)]
        dt2 = [-mm(pp, d, 0, 0) for pp, d in zip(p, dt3)]
        dp = [x - mm(d, 7.0 * ident - pp, 1, 1) for x, d, pp in zip(dp, dt2, p)]
        dp = [x + mm(pp, d, 0, 0) for x, pp, d in zip(dp, p, dt2)]
        da = [x + mm(d, zz, 1, 1) for x, d, zz in zip(da, dp, z)]
        dz = [x + mm(a, d, 0, 0) for x, a, d in zip(dz, a_list, dp)]
    for (n, s), a, g, d in zip(heads, a_list, da, dz):
        col, row, cm, rm = inverse_start(a)
        norm = cm * rm
        g = g + d.T / norm
        dnorm = -jnp.sum(jnp.sum(d.T * a, axis=1, keepdims=True), axis=0, keepdims=True) / (norm * norm)
        at_col = (col == cm).astype(f32)
        at_row = (row == rm).astype(f32)
        g = g + dnorm * rm * at_col / jnp.sum(at_col, axis=1, keepdims=True)
        g = g + dnorm * cm * at_row / jnp.sum(at_row, axis=0, keepdims=True)
        ds = a * (g - jnp.sum(a * g, axis=1, keepdims=True))
        (dlq_l, dlq_s)[n][:, s] = SCALE * mm(ds, ks[n][:, s].astype(f32))
        (dlk_l, dlk_s)[n][:, s] = SCALE * mm(ds, qs[n][:, s].astype(f32), 0, 0)


def back_inverse(at, lq_l, lk_l, lq_s, lk_s, dw_l, bv_l, dw_s, bv_s, deps=()):
    width = dw_l.shape[1]
    own = pl.BlockSpec((LM, width), lambda i, at: (at[0], at[1]))
    one, all_heads = whole((LM, width)), whole((LM, D))
    return pl.pallas_call(
        after(back_inverse_kernel, 9, deps),
        grid_spec=pltpu.PrefetchScalarGridSpec(
            num_scalar_prefetch=1,
            grid=(1,),
            in_specs=[own, own, all_heads, all_heads, one, one, all_heads, all_heads] + [ANY_SPEC] * len(deps),
            out_specs=[one, one, all_heads, all_heads],
        ),
        out_shape=[sds((LM, width), f32)] * 2 + [sds((LM, D), f32)] * 2,
        compiler_params=params(),
        cost_estimate=cost((width + D) // HD * 72 * 3 * 2 * 64**3 * 20, 2e6),
        name="back_inverse",
    )(at, lq_l, lk_l, lq_s, lk_s, dw_l, bv_l, dw_s, bv_s, *deps)


def back_b_group(k_g, v_g, wide, dots, probs):
    dsb = (probs * (dot(wide, v_g, 1, 0) - dots)).astype(bf)
    return dsb, SCALE * pick_heads(dot(dsb, k_g, 1, 1))


def back_b_kernel(units, lq, w, dbv, k, v, dsb_out, probs_out, dlq_out):
    level = from_parts(joined(w, units, slice(LM, LM + 16)))
    dots = from_parts(joined(dbv, units, slice(LM, LM + 16)))
    dbv_all = joined(dbv, units, slice(0, LM))
    for gs in group_slices():
        probs = jnp.exp(mark_scores(lq[:, gs], k[gs, :], None) - level[gs])
        probs_out[gs, :] = probs.astype(bf)
        dsb_out[gs, :], dlq_out[:, gs] = back_b_group(
            k[gs, :], v[gs, :], spread_heads(dbv_all[:, gs]), dots[gs], probs
        )


def back_b(lq, w, dbv, k, v, items, units, deps=()):
    rows = k.shape[1] // items
    mark, tok = item_specs(rows)
    unit = unit_spec(units, LM + 16, D // units)
    return pl.pallas_call(
        after(functools.partial(back_b_kernel, units), 5, deps),
        grid=(items,),
        in_specs=[mark, unit, unit, tok, tok] + [ANY_SPEC] * len(deps),
        out_specs=[tok, tok, mark],
        out_shape=[sds(k.shape, bf), sds(k.shape, bf), sds((items * LM, D), f32)],
        compiler_params=params(),
        cost_estimate=cost(8 * items * rows * D * GROUP, 10 * items * rows * D, items * rows * D),
        name="back_b",
    )(lq, w, dbv, k, v, *deps)


def back_v_kernel(units, core, dbv, probs, dconv, x, gv_in, keep_in, send_in, dv_out, keep, send, acc, stage, sem):
    i = pl.program_id(0)

    @pl.when(i == 0)
    def _():
        acc[...] = gv_in[...]

    dbv_all = joined(dbv, units, slice(0, LM))
    for gs in group_slices():
        dv_out[gs, :] = (dot(spread_heads(dbv_all[:, gs]), probs[gs, :], 0, 0) + dconv[gs, :]).astype(bf)
    acc[...] += dot(dv_out[...], x[...], 1, 0)

    @pl.when(i == pl.num_programs(0) - 1)
    def _():
        stage[...] = acc[...].T.astype(bf)
        for cp in to_side(stage, keep, send, core[0] == 0, sem.at[0]):
            cp.wait()


def back_v(core, dbv, probs, dconv, x, gv, keep, send, items, units, deps=()):
    rows = probs.shape[1] // items
    _, tok = item_specs(rows)
    square = const_spec((D, D))
    return pl.pallas_call(
        after(functools.partial(back_v_kernel, units), 8, deps),
        grid=(items,),
        in_specs=[SMEM_SPEC, unit_spec(units, LM + 16, D // units), tok, tok]
        + [pl.BlockSpec((rows, D), lambda i: (i, 0)), square, ANY_SPEC, ANY_SPEC]
        + [ANY_SPEC] * len(deps),
        out_specs=[tok, ANY_SPEC, ANY_SPEC],
        out_shape=[sds(probs.shape, bf), sds((D, D), bf), sds((D, D), bf)],
        input_output_aliases={6: 1, 7: 2},
        scratch_shapes=[pltpu.VMEM((D, D), f32), pltpu.VMEM((D, D), bf), pltpu.SemaphoreType.DMA((1,))],
        compiler_params=params(),
        cost_estimate=cost(6 * items * rows * D * GROUP, 12 * items * rows * D),
        name="back_v",
    )(core, dbv, probs, dconv, x, gv, keep, send, *deps)


def short_back_kernel(length, q, k, v, lq, lk, z, w, bv, up, dconv, x, dsf_out, dsb_out, dv_out, dlq_out, dlk_out, dw_out, gv_out):
    for gs in group_slices():
        dw, dsf_out[gs, :], dlk_out[:, gs] = back_f_group(lk[:, gs], w[:, gs], q[gs, :], up[gs, :])
        dw_out[:, gs] = dw
        z_g, bv_g = z[:, gs], bv[:, gs]
        dbvs = [mm(z_g[:, s], dw[:, s], 0, 0).astype(bf) for s in head_slices(4)]
        dots = jnp.concatenate(
            [jnp.sum(d.astype(f32) * bv_g[:, s], axis=1, keepdims=True) for d, s in zip(dbvs, head_slices(4))], axis=0
        )
        scores = mark_scores(lq[:, gs], k[gs, :], length[0])
        e = jnp.exp(scores - jnp.max(scores, axis=1, keepdims=True))
        probs = e / jnp.sum(e, axis=1, keepdims=True)
        wide = spread_heads(jnp.concatenate(dbvs, axis=1))
        dsb_out[gs, :], dlq_out[:, gs] = back_b_group(k[gs, :], v[gs, :], wide, dots, probs)
        dv_out[gs, :] = (dot(wide, probs.astype(bf), 0, 0) + dconv[gs, :]).astype(bf)
    gv_out[...] = dot(dv_out[...], x[...], 1, 0)


def short_back(length, q, k, v, lq, lk, z, w, bv, up, dconv, x, deps=()):
    mark = sds((LM, D), f32)
    return pl.pallas_call(
        after(short_back_kernel, 12, deps),
        in_specs=[SMEM_SPEC] + [VMEM_SPEC] * 11 + [ANY_SPEC] * len(deps),
        out_specs=[VMEM_SPEC] * 7,
        out_shape=[sds(q.shape, bf)] * 3 + [mark] * 3 + [sds((D, D), f32)],
        compiler_params=params(),
        cost_estimate=cost(24 * q.size * GROUP, 20 * q.size, 2 * q.size),
        name="short_back",
    )(length, q, k, v, lq, lk, z, w, bv, up, dconv, x, *deps)


def score_part(member, x, lq, lk, dsf, dsb, sq, sk, dq_out, dk_out, acc):
    member2 = jnp.concatenate([member, member], axis=0)
    for n, (marks, scores, sums, out) in enumerate(((lk, dsf, sq, dq_out), (lq, dsb, sk, dk_out))):
        hi, lo = split(sums)
        back = dot(jnp.concatenate([hi, lo], axis=0), member2, 0, 0)
        for gs in group_slices():
            part = (dot(spread_heads(marks[:, gs] * SCALE), scores[gs, :], 0, 0) + back[gs]).astype(bf)
            out[gs, :] = part
    both = jnp.concatenate([dq_out[...], dk_out[...]], axis=0)
    acc[...] += dot(both, x[...], 1, 0)


def score_grads_kernel(n_long, length, core, x_l, lq_l, lk_l, dsf_l, dsb_l, sq_l, sk_l,
                       x_s, lq_s, lk_s, dsf_s, dsb_s, sq_s, sk_s, sq_own, sk_own,
                       dq_l, dk_l, dq_s, dk_s, keep, send, acc, stage, sem):
    i = pl.program_id(0)

    @pl.when(i == 0)
    def _():
        acc[...] = jnp.zeros_like(acc)
        member = short_member(length[0], x_s.shape[0]).astype(bf)
        count = (length[0] // LM).astype(f32)
        sq, sk = (sq_s[...] + sq_own[...]) / count, (sk_s[...] + sk_own[...]) / count
        score_part(member, x_s, lq_s, lk_s, dsf_s, dsb_s, sq, sk, dq_s, dk_s, acc)

    @pl.when(i > 0)
    def _():
        count, rows = sq_l.shape[0], x_l.shape[0]
        member = (iota((count, rows), 1) // (LONG // LM) == iota((count, rows), 0)).astype(f32).astype(bf)
        score_part(member, x_l, lq_l, lk_l, dsf_l, dsb_l, sq_l[...], sk_l[...], dq_l, dk_l, acc)

    @pl.when(i == n_long)
    def _():
        jobs = [
            (lambda: acc[:D, :], lambda src, sem: to_side(src, keep, send, core[0] == 0, sem)),
            (lambda: acc[D:, :], lambda src, sem: to_side(src, keep, send, core[0] == 1, sem)),
        ]
        put_bf16(jobs, stage, sem)


def score_grads(length, core, long_args, short_args, items, deps=()):
    x_l, x_s = long_args[0], short_args[0]
    tl, ts = x_l.shape[0], x_s.shape[0]
    rows = tl // items
    marks_l = long_args[5].shape[0] // items
    at = lambda i: jnp.maximum(i - 1, 0)
    first = lambda i: 0

    def specs(r, marks, f):
        row = pl.BlockSpec((r, D), lambda i: (f(i), 0))
        mark = pl.BlockSpec((LM, D), lambda i: (f(i), 0))
        tok = pl.BlockSpec((D, r), lambda i: (0, f(i)))
        own = pl.BlockSpec((marks, D), lambda i: (f(i), 0))
        return [row, mark, mark, tok, tok, own, own]

    long_out = pl.BlockSpec((D, rows), lambda i: (0, at(i)))
    short_out = pl.BlockSpec((D, ts), lambda i: (0, 0))
    return pl.pallas_call(
        after(functools.partial(score_grads_kernel, items), 18, deps),
        grid=(items + 1,),
        in_specs=[SMEM_SPEC, SMEM_SPEC]
        + specs(rows, marks_l, at)
        + specs(ts, LM, first)
        + [const_spec((LM, D))] * 2
        + [ANY_SPEC] * len(deps),
        out_specs=[long_out] * 2 + [short_out] * 2 + [ANY_SPEC] * 2,
        out_shape=[sds((D, tl), bf)] * 2 + [sds((D, ts), bf)] * 2 + [sds((D, D), bf)] * 2,
        scratch_shapes=[
            pltpu.VMEM((2 * D, D), f32),
            pltpu.VMEM((2, D, D), bf),
            pltpu.SemaphoreType.DMA((2,)),
        ],
        compiler_params=params(),
        cost_estimate=cost(6 * (tl + ts) * D * D, 20 * (tl + ts) * D),
        name="score_grads",
    )(length, core, *long_args, *short_args, *deps)


def input_grad_kernel(n_long, dr_l, dq_l, dk_l, dv_l, dr_s, dq_s, dk_s, dv_s, wq, wk, wv, out_l, out_s, w_all):
    i = pl.program_id(0)
    is_long = i < n_long
    @pl.when(i == 0)
    def _():
        for j, w in enumerate((wq, wk, wv)):
            w_all[:, j * D : (j + 1) * D] = w[...]

    grad = jnp.concatenate(
        [jnp.where(is_long, a[...], b[...]) for a, b in ((dq_l, dq_s), (dk_l, dk_s), (dv_l, dv_s))], axis=0
    )
    total = jnp.where(is_long, dr_l[...], dr_s[...]) + dot(grad, w_all[...], 0, 1)
    total = total.astype(bf)

    @pl.when(is_long)
    def _():
        out_l[...] = total

    @pl.when(jnp.logical_not(is_long))
    def _():
        out_s[...] = total


def input_grad(long_args, short_args, weights, deps=()):
    tl, ts = long_args[0].shape[0], short_args[0].shape[0]
    nl = tl // ts
    at = lambda i: jnp.minimum(i, nl - 1)
    row = lambda f: pl.BlockSpec((ts, D), lambda i: (f(i), 0))
    col = lambda f: pl.BlockSpec((D, ts), lambda i: (0, f(i)))
    first = lambda i: 0
    return pl.pallas_call(
        after(functools.partial(input_grad_kernel, nl), 11, deps),
        grid=(nl + 1,),
        in_specs=[row(at)] + [col(at)] * 3 + [row(first)] + [col(first)] * 3 + [const_spec((D, D))] * 3
        + [ANY_SPEC] * len(deps),
        out_specs=[row(at), row(first)],
        out_shape=[sds((tl, D), bf), sds((ts, D), bf)],
        scratch_shapes=[pltpu.VMEM((D, 3 * D), bf)],
        compiler_params=params(),
        cost_estimate=cost(6 * (tl + ts) * D * D, 12 * (tl + ts) * D),
        name="input_grad",
    )(*long_args, *short_args, *weights, *deps)


def swap(values, axis, bit):
    count = lax.axis_size(axis)
    return lax.ppermute(values, axis, [(i, i ^ bit) for i in range(count)])


def side(axis, bit):
    return (lax.axis_index(axis) // bit) % 2


def exchange(values):
    return lax.all_to_all(values, "seq", 0, 0, tiled=True)


def gather(values):
    return exchange(jnp.broadcast_to(values[None], (lax.axis_size("seq"),) + values.shape))


def tied(values, dep):
    return lax.optimization_barrier(tuple(values) + (dep,))[:-1]


def is_small_mesh():
    return lax.axis_size("dp") == 4 and lax.axis_size("seq") == 8


def pair_sum(keep, send, axis, bit):
    return keep.astype(f32) + swap(send, axis, bit).astype(f32)


class Reduction:
    def __init__(self, keep, send, dim):
        self.dim, self.other = dim, 1 - dim
        self.core, self.x = side("dp", 1), side("dp", 2)
        v = pair_sum(keep, send, "dp", 1)
        if not is_small_mesh():
            self.theirs = v.astype(bf)
            return
        half = v.shape[self.other] // 2
        self.mine = lax.dynamic_slice_in_dim(v, self.x * half, half, self.other).astype(bf)
        self.theirs = lax.dynamic_slice_in_dim(v, (1 - self.x) * half, half, self.other).astype(bf)

    def wait_for(self, dep):
        if is_small_mesh():
            (self.mine,) = tied((self.mine,), dep)

    def over_x(self):
        if not is_small_mesh():
            self.value = self.theirs
            return self.value
        n_seq = lax.axis_size("seq")
        v = pair_sum(self.mine, self.theirs, "dp", 2).astype(bf)
        if self.dim == 0:
            v = v.reshape(n_seq, v.shape[0] // n_seq, v.shape[1])
        else:
            v = v.reshape(v.shape[0], n_seq, v.shape[1] // n_seq).transpose(1, 0, 2)
        self.value = v
        return v

    def over_seq(self):
        if not is_small_mesh():
            self.own = lax.psum_scatter(self.value, "seq", scatter_dimension=self.dim, tiled=True)
        else:
            self.own = jnp.sum(exchange(self.value).astype(f32), axis=0).astype(bf)
        return self.own

    def both(self):
        if not is_small_mesh():
            place = (jnp.arange(2) == self.core).astype(f32)[:, None, None]
            shares = lax.psum(self.own.astype(f32)[None] * place, "dp")
            return shares[0], shares[1]
        got = swap(self.own, "dp", 2)
        v = jnp.where(
            self.x == 0,
            jnp.concatenate([self.own, got], axis=self.other),
            jnp.concatenate([got, self.own], axis=self.other),
        )
        got = swap(v, "dp", 1)
        first = self.core == 0
        return jnp.where(first, v, got).astype(f32), jnp.where(first, got, v).astype(f32)


class Halving(Reduction):
    def __init__(self, keep, send, dim, order):
        if not is_small_mesh():
            super().__init__(keep, send, dim)
            return
        self.dim, self.other = dim, 1 - dim
        self.core, self.x = side("dp", 1), side("dp", 2)
        v = pair_sum(keep, send, "dp", 1)
        rows, n = v.shape
        if dim == 0:
            v = v.reshape(2, 2, 2, rows // 8, n)
        else:
            v = v.reshape(rows, 8, n // 8).transpose(1, 0, 2).reshape(2, 2, 2, rows, n // 8)
        self.left = ["z1", "z0", "y"]
        self.order = list(order)
        self.split(v)

    def split(self, v):
        step = self.order[0]
        if step == "x":
            dim = v.ndim - 1 if self.dim == 0 else v.ndim - 2
            bit = self.x
            size = v.shape[dim] // 2
        else:
            dim = self.left.index(step)
            self.left.pop(dim)
            bit = side("seq", {"y": 1, "z0": 2, "z1": 4}[step])
            size = 1
        take = lambda at: lax.dynamic_slice_in_dim(v, at * size, size, dim).astype(bf)
        self.mine, self.theirs = take(bit), take(1 - bit)
        if step != "x":
            self.mine, self.theirs = (lax.squeeze(u, (dim,)) for u in (self.mine, self.theirs))

    def step(self):
        if not is_small_mesh():
            self.value = self.theirs
            return self.theirs
        axis, bit = {"x": ("dp", 2), "y": ("seq", 1), "z0": ("seq", 2), "z1": ("seq", 4)}[self.order.pop(0)]
        v = pair_sum(self.mine, self.theirs, axis, bit)
        if self.order:
            self.split(v)
            return self.theirs
        self.own = v.astype(bf)
        return self.own

    def last(self):
        if not is_small_mesh():
            self.step()
            return self.over_seq()
        return self.step()


def hold(value, dep):
    return tied((value,), dep)[0]


class SumStages:
    def __init__(self, values):
        self.values = values
        self.steps = [("dp", 1), ("dp", 2), ("seq", 4), ("seq", 2), ("seq", 1)]

    def step(self, dep):
        if is_small_mesh():
            axis, bit = self.steps.pop(0)
            held = hold(self.values, dep)
            self.values = held + swap(held, axis, bit)
        elif len(self.steps) == 5:
            self.steps.pop(0)
            self.values = lax.psum(self.values, ("dp", "seq"))
        return self.values


def neighbours(first, last):
    count = lax.axis_size("seq")
    right = lax.ppermute(first, "seq", [((i + 1) % count, i) for i in range(count)])
    left = lax.ppermute(last, "seq", [(i, (i + 1) % count) for i in range(count)])
    return left, right


def pad_units(values, count):
    have = values.shape[0]
    if have == count:
        return values
    return jnp.concatenate([values, jnp.zeros((count - have,) + values.shape[1:], values.dtype)], axis=0)


def body(x_long, x_short, item_start, short_lengths, w_query, w_key, w_value, w_out, conv_taps, ln1_gain, ln1_bias,
         w_up, up_bias, w_down, down_bias, ln2_gain, ln2_bias, cot_long, cot_short):
    _, items, rows, _ = x_long.shape
    short_rows = x_short.shape[3]
    seg = LONG // LM
    own_marks = rows // seg
    n_seq = lax.axis_size("seq")
    me = lax.axis_index("seq")
    heads_each = next(h for h in (2, 4, 6, 12) if H % h == 0 and items * H // h <= n_seq)
    units = H // heads_each
    width = heads_each * HD
    owners = items * units

    x_l = x_long.reshape(items * rows, D)
    x_s = x_short.reshape(short_rows, D)
    length = short_lengths.reshape(1)
    core = side("dp", 1).astype(jnp.int32).reshape(1)
    mine = jnp.minimum(me, owners - 1).astype(jnp.int32)
    at = jnp.stack([mine // units, mine % units])

    x_mean = jnp.sum(x_long[0].reshape(items, own_marks, seg, D).astype(f32), axis=2) * (1.0 / seg)
    means = gather(x_mean.reshape(items * own_marks, D))
    means = means.reshape(n_seq, items, own_marks, D).transpose(1, 0, 2, 3).reshape(items * LM, D)
    mean_hi, mean_lo = split(means)

    def marks_of(w):
        return (
            jnp.dot(mean_hi, w, preferred_element_type=f32) + jnp.dot(mean_lo, w, preferred_element_type=f32)
        ).astype(bf)

    place = (me - item_start[0]) % n_seq
    open_left = (place > 0)[:, None, None]
    open_right = (place < n_seq - 1)[:, None, None]

    def rims(left, right):
        return jnp.concatenate(
            [jnp.where(open_left, left, jnp.zeros_like(left)), jnp.where(open_right, right, jnp.zeros_like(right))], axis=1
        ).reshape(items * 2 * HALF, D)

    x_rim = rims(*neighbours(x_long[0, :, :HALF], x_long[0, :, rows - HALF :]))
    v_rim = jnp.einsum("ke,nk->en", w_value, x_rim, preferred_element_type=f32).astype(bf)

    tap_rows = jnp.stack([conv_taps.T, conv_taps[::-1].T], axis=1)
    tap_rows = jnp.pad(tap_rows, ((0, 0), (0, 6), (0, 128 - TAPS)))

    (k_l, v_l), (k_s, v_s), lk_s = project(length, x_l, x_s, (w_key, w_value))
    c_l, c_s = conv(length, v_l, v_s, v_rim, tap_rows, items)
    lq_l, lk_l = marks_of(w_query), marks_of(w_key)

    msg_l = stats(lq_l, k_l, v_l, items, units)
    (q_l,), (q_s,), lq_s = project(length, x_l, x_s, (w_query,), (msg_l,))
    got_l = exchange(pad_units(msg_l, n_seq))
    z_own, z_s = inverse(at, lq_l, lk_l, lq_s, lk_s, width)
    w_own, bv_own = combine(got_l, z_own)
    w_l = exchange(w_own)[:owners]
    o_s, w_s, bv_s = short_attend(length, q_s, k_s, v_s, lq_s, lk_s, z_s, c_s)
    o_l = mix(lk_l, w_l, q_l, c_l, items, units)

    vecs = jnp.pad(jnp.stack([ln1_gain, ln1_bias, down_bias, ln2_gain, ln2_bias]), ((0, 3), (0, 0)))
    out_l, out_s, dr_l, dr_s, do_l, do_s, up_keep, up_send, dn_keep, dn_send, vo_keep, vo_send, small, small_up = dense(
        core, x_l, x_s, o_l, o_s, cot_long.reshape(items * rows, D), cot_short.reshape(short_rows, D), w_out, w_up,
        w_down, vecs, up_bias.reshape(1, -1),
    )

    dw_l, dlk_part, dsf_l, edges = back_f(lk_l, w_l, q_l, do_l, items, units)
    got_dw = exchange(pad_units(dw_l, n_seq))
    up_keep, dn_keep = tied((up_keep, dn_keep), edges)
    up = Halving(up_keep, up_send, 0, ("x", "y", "z0", "z1"))
    down = Halving(dn_keep, dn_send, 1, ("y", "x", "z0", "z1"))
    do_rim = rims(*tied(neighbours(edges[:, :HALF], edges[:, HALF:]) + (up.theirs,), down.theirs)[:2]).T

    dc_l, dc_s, tap_g = conv_back(
        length, v_l, v_s, v_rim, do_l, do_s, do_rim, tap_rows, items, (up.theirs, down.theirs)
    )
    dsf_s, dsb_s, dv_s, dlq_s, dlk_s, dw_s, gv_s = short_back(
        length, q_s, k_s, v_s, lq_s, lk_s, z_s, w_s, bv_s, do_s, dc_s, x_s
    )
    packed = jnp.concatenate([small.reshape(-1), small_up.reshape(-1), tap_g[:, 0, :].reshape(-1)]).reshape(-1, 128)
    packed = SumStages(packed)
    dbv_own, dw_own = back_mix(got_dw, z_own, bv_own, (dv_s,))
    dbv_l = exchange(dbv_own)[:owners]
    dlq_own, dlk_own, dlq_own_s, dlk_own_s = back_inverse(
        at, lq_l, lk_l, lq_s, lk_s, dw_own, bv_own, dw_s, bv_s, (up.step(), down.step())
    )
    dsb_l, probs_l, dlq_part = back_b(
        lq_l, w_l, dbv_l, k_l, v_l, items, units, (up.step(), down.step(), packed.step(dw_own))
    )

    owned = (jnp.arange(owners) == me).astype(f32).reshape(items, units, 1, 1)

    def with_own(part, own):
        return part.reshape(items, LM, D) + (owned * own[None, None]).transpose(0, 2, 1, 3).reshape(items, LM, D)

    dl = jnp.stack([with_own(dlq_part, dlq_own), with_own(dlk_part, dlk_own)]).astype(bf)
    dl = dl.reshape(2 * items, n_seq, own_marks, D).transpose(1, 0, 2, 3)
    dv_l, vo_keep, vo_send = back_v(core, dbv_l, probs_l, dc_l, x_l, gv_s, vo_keep, vo_send, items, units, (dl,))
    dl = jnp.sum(exchange(dl).astype(f32), axis=0) * (1.0 / seg)
    dl = jnp.pad(dl.reshape(2, items, own_marks, D), ((0, 0), (0, 0), (0, 16 - own_marks), (0, 0)))
    dl = dl.reshape(2, items * 16, D)

    dq_l, dk_l, dq_s, dk_s, qk_keep, qk_send = score_grads(
        length,
        core,
        (x_l, lq_l, lk_l, dsf_l, dsb_l, dl[0], dl[1]),
        (x_s, lq_s, lk_s, dsf_s, dsb_s, dlq_s, dlk_s, dlq_own_s, dlk_own_s),
        items,
        (packed.step(dlq_part), dv_l),
    )
    query_key = Reduction(qk_keep, qk_send, 1)
    value_out = Halving(hold(vo_keep, dq_l), vo_send, 0, ("y", "z0", "z1", "x"))
    up.step()
    down.step()
    up.theirs, down.theirs = tied((up.theirs, down.theirs), dq_l)
    grad_l, grad_s = input_grad(
        (dr_l, dq_l, dk_l, dv_l),
        (dr_s, dq_s, dk_s, dv_s),
        (w_query, w_key, w_value),
        (query_key.theirs, value_out.theirs),
    )
    query_key.wait_for(grad_l)
    up.last()
    down.last()
    query_key.over_x()
    ready = query_key.value
    up.own, down.own = tied((up.own, down.own), ready)
    packed.step(ready)
    packed.step(ready)
    value_out.wait_for(ready)
    value_out.step()
    value_out.step()
    value_out.step()
    value_out.last()
    query_key.over_seq()
    up_a, up_b = up.both()
    down_a, down_b = down.both()
    v_a, v_b = value_out.both()
    q_g, k_g = query_key.both()

    packed = packed.step(ready).reshape(-1)
    small = packed[: 6 * D].reshape(6, D)
    small_up = packed[6 * D : 6 * D + FF]
    taps_g = packed[6 * D + FF :].reshape(H, 128)[:, :TAPS].T

    return (
        out_l.reshape(x_long.shape),
        out_s.reshape(x_short.shape),
        grad_l.reshape(x_long.shape),
        grad_s.reshape(x_short.shape),
        q_g.T,
        k_g.T,
        v_a,
        v_b,
        taps_g,
        small[0],
        small[1],
        jnp.concatenate([up_a, up_b], axis=1),
        small_up,
        jnp.concatenate([down_a, down_b], axis=0).T,
        small[2],
        small[4],
        small[5],
    )


def solution(mesh):
    tokens = P("dp", None, "seq", None)
    shorts = P("dp", "seq", None, None, None)
    rows = P("seq", None)
    return jax.shard_map(
        body,
        mesh=mesh,
        in_specs=(tokens, shorts, P("dp", None), P("dp", "seq", None)) + (P(),) * 13 + (tokens, shorts),
        out_specs=(tokens, shorts, tokens, shorts, rows, rows, rows, rows, P(), P(), P(), rows, P(), rows, P(), P(), P()),
        check_vma=False,
    )
```

```python
import functools

import jax
import jax.numpy as jnp
from jax import lax
from jax.experimental import pallas as pl
from jax.experimental.pallas import tpu as pltpu
from jax.sharding import PartitionSpec as P

D = 768
H = 12
HD = 64
FF = 3072
LM = 64
NS_STEPS = 6
HALF = 16
TAPS = 33
LONG = 4096
GROUP = 256
EPSILON = 1e-05
MASKED_SCORE = -1e30
SCALE = 0.125
VMEM_BYTES = 63 * 1024 * 1024

f32 = jnp.float32
bf = jnp.bfloat16
sds = jax.ShapeDtypeStruct


def dot(a, b, ca, cb):
    return lax.dot_general(a, b, (((ca,), (cb,)), ((), ())), preferred_element_type=f32)


def split(v):
    hi = v.astype(bf)
    return hi, (v - hi.astype(f32)).astype(bf)


def mm(a, b, ca=1, cb=0):
    ah, al = split(a)
    bh, bl = split(b)
    return dot(ah, bh, ca, cb) + (dot(ah, bl, ca, cb) + dot(al, bh, ca, cb))


def iota(shape, dim):
    return lax.broadcasted_iota(jnp.int32, shape, dim)


def spread_heads(block):
    tiled = jnp.concatenate([block.astype(f32)] * 4, axis=0)
    same = (iota((GROUP, GROUP), 0) // HD) == (iota((GROUP, GROUP), 1) // HD)
    return jnp.where(same, tiled, 0.0).astype(bf)


def pick_heads(full):
    head = iota((LM, GROUP), 1) // HD
    out = full[:LM]
    for h in range(1, 4):
        out = jnp.where(head == h, full[h * LM : (h + 1) * LM], out)
    return out


def lanes_of(columns):
    n = columns[0].shape[0]
    lane = iota((n, 128), 1)
    wide = jnp.zeros((n, 128), f32)
    for k, col in enumerate(columns):
        wide = jnp.where(lane == k, col, wide)
    return wide.T[:8]


def three_parts(row):
    hi = row.astype(bf).astype(f32)
    mid = (row - hi).astype(bf).astype(f32)
    low = row - hi - mid
    r = iota((16, row.shape[1]), 0)
    return jnp.where(r == 0, hi, jnp.where(r == 1, mid, jnp.where(r == 2, low, 0.0))).astype(bf)


def from_parts(rows):
    v = rows.astype(f32)
    total = v[0:1] + v[1:2] + v[2:3]
    return jnp.broadcast_to(total, (8, total.shape[1])).T[:, 0:1]


def head_softmax(scores):
    rows = scores.shape[1]
    s3 = scores.reshape(4, LM, rows)
    e = jnp.exp(s3 - jnp.max(s3, axis=1, keepdims=True))
    return (e / jnp.sum(e, axis=1, keepdims=True)).reshape(GROUP, rows)


def params(vmem=VMEM_BYTES):
    return pltpu.CompilerParams(vmem_limit_bytes=vmem)


def cost(flops, nbytes, trans=0):
    return pl.CostEstimate(flops=int(flops), bytes_accessed=int(nbytes), transcendentals=int(trans))


SMEM_SPEC = pl.BlockSpec(memory_space=pltpu.SMEM)
ANY_SPEC = pl.BlockSpec(memory_space=pl.ANY)


def after(kernel, count, deps):
    return lambda *refs: kernel(*refs[:count], *refs[count + len(deps) :])


def const_spec(shape):
    return pl.BlockSpec(shape, lambda i: tuple(0 for _ in shape), pipeline_mode=pl.Buffered(1))


def short_member(length, rows):
    seg = length // LM
    lm = iota((LM, rows), 0)
    pos = iota((LM, rows), 1)
    return ((pos >= lm * seg) & (pos < (lm + 1) * seg)).astype(f32)


def project_kernel(n_long, count, length, x_l, x_s, *refs):
    ws, out_l, out_s = refs[:count], refs[count : 2 * count], refs[2 * count : 3 * count]
    marks, w_t = refs[3 * count :]
    i = pl.program_id(0)

    @pl.when(i == 0)
    def _():
        for j, w in enumerate(ws):
            w_t[j * D : (j + 1) * D, :] = w[...].T

    x = jnp.where(i < n_long, x_l[...], x_s[...])
    made = dot(w_t[...], x, 1, 1).astype(bf)
    made = [made[j * D : (j + 1) * D] for j in range(count)]

    @pl.when(i < n_long)
    def _():
        for ref, v in zip(out_l, made):
            ref[...] = v

    @pl.when(i >= n_long)
    def _():
        for ref, v in zip(out_s, made):
            ref[...] = v
        member = short_member(length[0], made[0].shape[1]).astype(bf)
        marks[...] = (dot(member, made[0], 1, 1) / (length[0] // LM).astype(f32)).astype(bf)


def project(length, x_l, x_s, ws, deps=()):
    tile = x_s.shape[0]
    n = len(ws)
    nl = x_l.shape[0] // tile
    long_at = lambda i: jnp.minimum(i, nl - 1)
    row = lambda f: pl.BlockSpec((tile, D), lambda i: (f(i), 0))
    col = lambda f: pl.BlockSpec((D, tile), lambda i: (0, f(i)))
    first = lambda i: 0
    tl, ts = x_l.shape[0], x_s.shape[0]
    out = pl.pallas_call(
        after(functools.partial(project_kernel, nl, n), 3 + n, deps),
        grid=(nl + 1,),
        in_specs=[SMEM_SPEC, row(long_at), row(first)] + [const_spec((D, D))] * n + [ANY_SPEC] * len(deps),
        out_specs=[col(long_at)] * n + [col(first)] * n + [pl.BlockSpec((LM, D), lambda i: (0, 0))],
        out_shape=[sds((D, tl), bf)] * n + [sds((D, ts), bf)] * n + [sds((LM, D), bf)],
        scratch_shapes=[pltpu.VMEM((n * D, D), bf)],
        compiler_params=params(),
        cost_estimate=cost(2 * n * (tl + ts) * D * D, 4 * n * (tl + ts) * D),
        name="project",
    )(length, x_l, x_s, *ws, *deps)
    return out[:n], out[n : 2 * n], out[2 * n]


def mark_scores(lq_g, k_g, limit):
    scores = dot(spread_heads(lq_g * SCALE), k_g, 1, 0)
    if limit is not None:
        scores = jnp.where(iota(scores.shape, 1) < limit, scores, MASKED_SCORE)
    return scores


def group_slices():
    return [slice(g * GROUP, (g + 1) * GROUP) for g in range(3)]


def stats_kernel(units, lq, k, v, msg):
    sums, stats = [], []
    for gs in group_slices():
        scores = mark_scores(lq[:, gs], k[gs, :], None)
        most = jnp.max(scores, axis=1, keepdims=True)
        e = jnp.exp(scores - most)
        stats.append(lanes_of([most, jnp.sum(e, axis=1, keepdims=True)]))
        sums.append(pick_heads(dot(e.astype(bf), v[gs, :], 1, 1)))
    sums = jnp.concatenate(sums, axis=1)
    stats = jnp.concatenate(stats, axis=1)
    width = D // units
    for u in range(units):
        us = slice(u * width, (u + 1) * width)
        msg[u, :LM, :] = sums[:, us]
        msg[u, LM:, :] = stats[:, us]


def item_specs(rows):
    mark = pl.BlockSpec((LM, D), lambda i: (i, 0))
    tok = pl.BlockSpec((D, rows), lambda i: (0, i))
    return mark, tok


def stats(lq, k, v, items, units):
    rows = k.shape[1] // items
    mark, tok = item_specs(rows)
    return pl.pallas_call(
        functools.partial(stats_kernel, units),
        grid=(items,),
        in_specs=[mark, tok, tok],
        out_specs=pl.BlockSpec((units, LM + 8, D // units), lambda i: (i, 0, 0)),
        out_shape=sds((items * units, LM + 8, D // units), f32),
        compiler_params=params(),
        cost_estimate=cost(4 * items * rows * D * GROUP, 4 * items * rows * D, items * rows * D),
        name="stats",
    )(lq, k, v)


def eye():
    return jnp.where(iota((LM, LM), 0) == iota((LM, LM), 1), 1.0, 0.0).astype(f32)


def head_slices(count):
    return [slice(h * HD, (h + 1) * HD) for h in range(count)]


def mark_probs(q, k):
    s = SCALE * dot(q, k, 1, 1)
    e = jnp.exp(s - jnp.max(s, axis=-1, keepdims=True))
    return e / jnp.sum(e, axis=-1, keepdims=True)


def inverse_start(a):
    col = jnp.sum(a, axis=0, keepdims=True)
    row = jnp.sum(a, axis=1, keepdims=True)
    return col, row, jnp.max(col, axis=1, keepdims=True), jnp.max(row, axis=0, keepdims=True)


def inverse_steps(a_list, kept=None):
    ident = eye()
    z_list = []
    for a in a_list:
        _, _, cm, rm = inverse_start(a)
        z_list.append(a.T / (cm * rm))
    for _ in range(NS_STEPS):
        p_list = [mm(a, z) for a, z in zip(a_list, z_list)]
        t2 = [15.0 * ident - mm(p, 7.0 * ident - p) for p in p_list]
        t3 = [13.0 * ident - mm(p, t) for p, t in zip(p_list, t2)]
        if kept is not None:
            kept.append((z_list, p_list, t2, t3))
        z_list = [0.25 * mm(z, t) for z, t in zip(z_list, t3)]
    return z_list


def own_slices(*refs):
    return [(k, s) for k, ref in enumerate(refs) for s in head_slices(ref.shape[1] // HD)]


def inverse_kernel(at, lq_l, lk_l, lq_s, lk_s, z_l, z_s):
    qs, ks, zs = (lq_l, lq_s), (lk_l, lk_s), (z_l, z_s)
    heads = own_slices(lq_l, lq_s)
    a_list = [mark_probs(qs[n][:, s], ks[n][:, s]) for n, s in heads]
    for (n, s), z in zip(heads, inverse_steps(a_list)):
        zs[n][:, s] = z


def whole(shape):
    return pl.BlockSpec(shape, lambda i, at: tuple(0 for _ in shape))


def inverse(at, lq_l, lk_l, lq_s, lk_s, width):
    own = pl.BlockSpec((LM, width), lambda i, at: (at[0], at[1]))
    return pl.pallas_call(
        inverse_kernel,
        grid_spec=pltpu.PrefetchScalarGridSpec(
            num_scalar_prefetch=1,
            grid=(1,),
            in_specs=[own, own, whole((LM, D)), whole((LM, D))],
            out_specs=[whole((LM, width)), whole((LM, D))],
        ),
        out_shape=[sds((LM, width), f32), sds((LM, D), f32)],
        compiler_params=params(),
        cost_estimate=cost((width + D) // HD * 24 * 3 * 2 * 64**3 * 20, 1e6),
        name="inverse",
    )(at, lq_l, lk_l, lq_s, lk_s)


def put_all(out, marks, parts):
    for d in range(out.shape[0]):
        out[d, :LM, :] = marks
        out[d, LM:, :] = parts


def combine_kernel(senders, msg, z, out, bv_out):
    width = z.shape[1]
    most = jnp.concatenate([msg[d, LM : LM + 1, :] for d in range(senders)], axis=0)
    part = jnp.concatenate([msg[d, LM + 1 : LM + 2, :] for d in range(senders)], axis=0)
    top = jnp.max(most, axis=0, keepdims=True)
    e = jnp.exp(most - top)
    total = jnp.sum(part * e, axis=0, keepdims=True)
    weight = (e / total).T
    w_all = []
    for s in head_slices(width // HD):
        bv = jnp.zeros((LM, HD), f32)
        for d in range(senders):
            bv = bv + weight[s, d : d + 1] * msg[d, :LM, s]
        bv_out[:, s] = bv
        w_all.append(mm(z[:, s], bv))
    put_all(out, jnp.concatenate(w_all, axis=1).astype(bf), three_parts(top + jnp.log(total)))


VMEM_SPEC = pl.BlockSpec(memory_space=pltpu.VMEM)


def combine(msg, z):
    senders, _, width = msg.shape
    return pl.pallas_call(
        functools.partial(combine_kernel, senders),
        in_specs=[VMEM_SPEC] * 2,
        out_specs=[VMEM_SPEC] * 2,
        out_shape=[sds((senders, LM + 16, width), bf), sds((LM, width), f32)],
        compiler_params=params(),
        cost_estimate=cost(1e8, 4e6),
        name="combine",
    )(msg, z)


def joined(ref, units, rows):
    return jnp.concatenate([ref[u, rows, :] for u in range(units)], axis=1)


def mark_mix(lk_g, w_g, q_g, conv_g):
    probs = head_softmax(dot(spread_heads(lk_g * SCALE), q_g, 1, 0)).astype(bf)
    return (dot(spread_heads(w_g), probs, 0, 0) + conv_g).astype(bf)


def mix_kernel(units, lk, w, q, conv, out):
    w_all = joined(w, units, slice(0, LM))
    for gs in group_slices():
        out[gs, :] = mark_mix(lk[:, gs], w_all[:, gs], q[gs, :], conv[gs, :])


def short_kernel(length, q, k, v, lq, lk, z, conv, out, w_out, bv_out):
    for gs in group_slices():
        scores = mark_scores(lq[:, gs], k[gs, :], length[0])
        e = jnp.exp(scores - jnp.max(scores, axis=1, keepdims=True))
        probs = e / jnp.sum(e, axis=1, keepdims=True)
        bv = pick_heads(dot(probs.astype(bf), v[gs, :], 1, 1))
        bv_out[:, gs] = bv
        z_g = z[:, gs]
        w = jnp.concatenate([mm(z_g[:, s], bv[:, s]) for s in head_slices(4)], axis=1).astype(bf)
        w_out[:, gs] = w
        out[gs, :] = mark_mix(lk[:, gs], w, q[gs, :], conv[gs, :])


def short_attend(length, q, k, v, lq, lk, z, conv):
    return pl.pallas_call(
        short_kernel,
        in_specs=[SMEM_SPEC] + [VMEM_SPEC] * 7,
        out_specs=[VMEM_SPEC] * 3,
        out_shape=[sds(q.shape, bf), sds((LM, D), bf), sds((LM, D), f32)],
        compiler_params=params(),
        cost_estimate=cost(4 * q.size * GROUP * 2, 10 * q.size, 2 * q.size),
        name="short_attend",
    )(length, q, k, v, lq, lk, z, conv)


def unit_spec(units, rows, width):
    return pl.BlockSpec((units, rows, width), lambda i: (i, 0, 0))


def mix(lk, w, q, conv, items, units):
    rows = q.shape[1] // items
    mark, tok = item_specs(rows)
    return pl.pallas_call(
        functools.partial(mix_kernel, units),
        grid=(items,),
        in_specs=[mark, unit_spec(units, LM + 16, D // units), tok, tok],
        out_specs=tok,
        out_shape=sds(q.shape, bf),
        compiler_params=params(),
        cost_estimate=cost(4 * items * rows * D * GROUP, 8 * items * rows * D, items * rows * D),
        name="mix",
    )(lk, w, q, conv)


def windows(body, rim, items, rows, limit):
    out = []
    for j in range(items):
        own = body[:, j * rows : (j + 1) * rows]
        if limit is not None:
            own = jnp.where(iota(own.shape, 1) < limit, own.astype(f32), 0.0).astype(bf)
        wide = jnp.concatenate(
            [rim[:, 32 * j : 32 * j + HALF], own, rim[:, 32 * j + HALF : 32 * j + 2 * HALF]], axis=1
        )
        for t in range(rows // 128):
            out.append(wide[:, t * 128 : t * 128 + 128 + 2 * HALF])
    return jnp.concatenate(out, axis=0)


def band(row):
    wide = jnp.concatenate([row, jnp.zeros((1, 128), f32)], axis=1)
    rolled = pltpu.roll(jnp.broadcast_to(wide, (128, 256)), 0, 1, stride=1, stride_axis=0)
    return split(rolled[:, : 128 + 2 * HALF])


HEAD_STEP = 3


def unstack(stacked, out, at, items, rows, limit=None):
    k = 0
    for j in range(items):
        for t in range(rows // 128):
            v = stacked[k * HD : (k + 1) * HD]
            if limit is not None:
                v = jnp.where(iota(v.shape, 1) + t * 128 < limit, v, 0.0)
            out[at, j * rows + t * 128 : j * rows + (t + 1) * 128] = v
            k += 1


def both_windows(v_l, v_s, rim, at, items, limit):
    no_rim = jnp.zeros((HD, 2 * HALF), bf)
    rows, short_rows = v_l.shape[1] // items, v_s.shape[1]
    return jnp.concatenate(
        [
            windows(v_l[at, :], rim[at, :], items, rows, None),
            windows(v_s[at, :], no_rim, 1, short_rows, limit),
        ],
        axis=0,
    )


def banded(wins, row, out_l, out_s, at, items, limit):
    hi, lo = band(row)
    made = dot(wins, hi, 1, 1) + dot(wins, lo, 1, 1)
    cut = HD * out_l.shape[1] // 128
    unstack(made[:cut], out_l, at, items, out_l.shape[1] // items)
    unstack(made[cut:], out_s, at, 1, out_s.shape[1], limit)


def conv_kernel(items, length, v_l, v_s, rim, taps, out_l, out_s):
    for h in range(HEAD_STEP):
        at = slice(h * HD, (h + 1) * HD)
        wins = both_windows(v_l, v_s, rim, at, items, length[0])
        banded(wins, taps[h, 0:1, :], out_l, out_s, at, items, None)


def conv_specs(v_l, v_s, rim):
    n = HEAD_STEP * HD
    spec = lambda a: pl.BlockSpec((n, a.shape[1]), lambda h: (h, 0))
    return spec(v_l), spec(v_s), spec(rim), pl.BlockSpec((HEAD_STEP, 8, 128), lambda h: (h, 0, 0))


def conv(length, v_l, v_s, rim, taps, items):
    tok_l, tok_s, rims, tap = conv_specs(v_l, v_s, rim)
    return pl.pallas_call(
        functools.partial(conv_kernel, items),
        grid=(H // HEAD_STEP,),
        in_specs=[SMEM_SPEC, tok_l, tok_s, rims, tap],
        out_specs=[tok_l, tok_s],
        out_shape=[sds(v_l.shape, f32), sds(v_s.shape, f32)],
        compiler_params=params(),
        cost_estimate=cost(4 * 512 * v_l.size, 8 * v_l.size),
        name="conv",
    )(length, v_l, v_s, rim, taps)


def conv_back_kernel(items, length, v_l, v_s, rim, up_l, up_s, up_rim, taps, out_l, out_s, tap_grad):
    flip = (iota((128, 128), 0) + iota((128, 128), 1) == 127).astype(f32).astype(bf)
    for h in range(HEAD_STEP):
        at = slice(h * HD, (h + 1) * HD)
        wins = both_windows(v_l, v_s, rim, at, items, length[0])
        up_wins = both_windows(up_l, up_s, up_rim, at, items, None)
        banded(up_wins, taps[h, 1:2, :], out_l, out_s, at, items, length[0])
        ups = [up_l[at, t * 128 : (t + 1) * 128] for t in range(up_l.shape[1] // 128)]
        ups += [up_s[at, t * 128 : (t + 1) * 128] for t in range(up_s.shape[1] // 128)]
        gram = dot(jnp.concatenate(ups, axis=0), wins, 0, 0)
        hi, lo = split(gram)
        gram = dot(flip, hi, 1, 0) + dot(flip, lo, 1, 0)
        gram = jnp.concatenate([gram, jnp.zeros((128, 256 - gram.shape[1]), f32)], axis=1)
        skewed = pltpu.roll(gram, 129, 1, stride=1, stride_axis=0)
        tap_grad[h] = jnp.broadcast_to(jnp.sum(skewed, axis=0, keepdims=True)[:, :128], (8, 128))


def conv_back(length, v_l, v_s, rim, up_l, up_s, up_rim, taps, items, deps=()):
    tok_l, tok_s, rims, tap = conv_specs(v_l, v_s, rim)
    return pl.pallas_call(
        after(functools.partial(conv_back_kernel, items), 8, deps),
        grid=(H // HEAD_STEP,),
        in_specs=[SMEM_SPEC, tok_l, tok_s, rims, tok_l, tok_s, rims, tap] + [ANY_SPEC] * len(deps),
        out_specs=[tok_l, tok_s, tap],
        out_shape=[sds(v_l.shape, f32), sds(v_s.shape, f32), sds((H, 8, 128), f32)],
        compiler_params=params(),
        cost_estimate=cost(6 * 512 * v_l.size, 12 * v_l.size),
        name="conv_back",
    )(length, v_l, v_s, rim, up_l, up_s, up_rim, taps, *deps)


def fold_rows(v):
    return jnp.sum(v.reshape(v.shape[0] // 8, 8, v.shape[1]), axis=0)


def gelu_parts(x):
    e = jnp.exp(x * x * (-0.5))
    t = pl.reciprocal(1.0 + jnp.abs(x) * (0.3275911 * 0.7071067811865476), approx=False)
    poly = t * (
        0.127414796 + t * (-0.142248368 + t * (0.7107068705 + t * (-0.7265760135 + t * 0.5307027145)))
    )
    tail = poly * e
    phi = jnp.where(x >= 0, 1.0 - tail, tail)
    return x * phi, phi + x * e * 0.3989422804014327


def put_bf16(jobs, stage, sem):
    pend = []
    for k, (load, copies) in enumerate(jobs):
        slot = k % 2
        if k >= 2:
            for cp in pend[k - 2]:
                cp.wait()
        stage[slot] = load().astype(bf)
        pend.append(copies(stage.at[slot], sem.at[slot]))
    for group in pend[-2:]:
        for cp in group:
            cp.wait()


def to_side(src, keep, send, keeps, sem):
    copy = pltpu.make_async_copy(src, keep, sem)

    @pl.when(keeps)
    def _():
        copy.start()

    @pl.when(jnp.logical_not(keeps))
    def _():
        pltpu.make_async_copy(src, send, sem).start()

    return [copy]


def dense_kernel(n_long, tile, chunk, core, x_l, x_s, o_l, o_s, c_l, c_s, w_out, w_up, w_down, vecs, bu,
                 out_l, out_s, dr_l, dr_s, do_l, do_s, up_keep, up_send, dn_keep, dn_send, vo_keep, vo_send, small, small_up,
                 acc_up, acc_dn, acc_out, act, dact, accs, accu, x_b, o_b, c_b, out_b, dr_b, do_b,
                 in_sem, out_sem, end_sem):
    i = pl.program_id(0)
    last = pl.num_programs(0) - 1
    slot = lax.rem(i, 2)
    g1, b1, bd, g2, b2 = (vecs.at[k : k + 1] for k in range(5))

    def at(step):
        return pl.ds(pl.multiple_of(step * tile, tile), tile)

    def in_copies(step, to, refs):
        x, o, c = refs
        return [
            pltpu.make_async_copy(x.at[at(step), :], x_b.at[to], in_sem.at[0, to]),
            pltpu.make_async_copy(o.at[:, at(step)], o_b.at[to], in_sem.at[1, to]),
            pltpu.make_async_copy(c.at[at(step), :], c_b.at[to], in_sem.at[2, to]),
        ]

    def fetch(step, to):
        @pl.when(step < n_long)
        def _():
            for cp in in_copies(step, to, (x_l, o_l, c_l)):
                cp.start()

        @pl.when(step >= n_long)
        def _():
            for cp in in_copies(step - n_long, to, (x_s, o_s, c_s)):
                cp.start()

    def out_copies(step, refs):
        out, dr, do = refs
        return [
            pltpu.make_async_copy(out_b, out.at[at(step), :], out_sem.at[0]),
            pltpu.make_async_copy(dr_b, dr.at[at(step), :], out_sem.at[1]),
            pltpu.make_async_copy(do_b, do.at[:, at(step)], out_sem.at[2]),
        ]

    @pl.when(i == 0)
    def _():
        fetch(i, slot)
        for ref in (acc_up, acc_dn, acc_out, accs, accu):
            ref[...] = jnp.zeros_like(ref)

    @pl.when(i < last)
    def _():
        fetch(i + 1, 1 - slot)

    for cp in in_copies(0, slot, (x_s, o_s, c_s)):
        cp.wait()

    o_t = o_b[slot]
    r1 = x_b[slot].astype(f32) + dot(o_t, w_out[...], 0, 0)
    cen = r1 - jnp.mean(r1, axis=-1, keepdims=True)
    rstd1 = lax.rsqrt(jnp.mean(cen * cen, axis=-1, keepdims=True) + EPSILON)
    xh1 = cen * rstd1
    h1 = (xh1 * g1[...] + b1[...]).astype(bf)
    r2 = h1.astype(f32) + bd[...]
    for c in range(FF // chunk):
        cs = slice(c * chunk, (c + 1) * chunk)
        a, dg = gelu_parts(dot(h1, w_up[:, cs], 1, 0) + bu[:, cs])
        a = a.astype(bf)
        act[:, cs] = a
        dact[:, cs] = dg.astype(dact.dtype)
        r2 = r2 + dot(a, w_down[cs, :], 1, 0)
    cen2 = r2 - jnp.mean(r2, axis=-1, keepdims=True)
    rstd2 = lax.rsqrt(jnp.mean(cen2 * cen2, axis=-1, keepdims=True) + EPSILON)
    xh2 = cen2 * rstd2

    @pl.when(i > 0)
    def _():
        for cp in out_copies(0, (out_s, dr_s, do_s)):
            cp.wait()

    out_b[...] = (xh2 * g2[...] + b2[...]).astype(bf)
    g = c_b[slot].astype(f32)
    dxh = g * g2[...]
    dr2 = rstd2 * (
        dxh - jnp.mean(dxh, axis=-1, keepdims=True) - xh2 * jnp.mean(dxh * xh2, axis=-1, keepdims=True)
    )
    dz2 = dr2.astype(bf)
    accs[4] += fold_rows(g * xh2)
    accs[5] += fold_rows(g)
    accs[2] += fold_rows(dz2.astype(f32))
    dz2_t = dz2.T
    h1_t = h1.T
    dh1 = dr2
    for c in range(FF // chunk):
        cs = slice(c * chunk, (c + 1) * chunk)
        dp1 = (dot(dz2, w_down[cs, :], 1, 1) * dact[:, cs].astype(f32)).astype(bf)
        accu[:, cs] += fold_rows(dp1.astype(f32))
        dh1 = dh1 + dot(dp1, w_up[:, cs], 1, 1)
        acc_up[:, cs] += dot(h1_t, dp1, 1, 0)
        acc_dn[:, cs] += dot(dz2_t, act[:, cs], 1, 0)
    accs[0] += fold_rows(dh1 * xh1)
    accs[1] += fold_rows(dh1)
    dx = dh1 * g1[...]
    dr1 = rstd1 * (
        dx - jnp.mean(dx, axis=-1, keepdims=True) - xh1 * jnp.mean(dx * xh1, axis=-1, keepdims=True)
    )
    da1 = dr1.astype(bf)
    dr_b[...] = dr1
    acc_out[...] += dot(o_t, da1, 1, 0)
    do_b[...] = dot(w_out[...], da1, 1, 1).astype(bf)

    @pl.when(i < n_long)
    def _():
        for cp in out_copies(i, (out_l, dr_l, do_l)):
            cp.start()

    @pl.when(i >= n_long)
    def _():
        for cp in out_copies(i - n_long, (out_s, dr_s, do_s)):
            cp.start()

    @pl.when(i == last)
    def _():
        slots = tile // 128
        half = FF // 2
        pend = []

        def put(rows, copies):
            k = len(pend)
            if k >= slots:
                for cp in pend[k - slots]:
                    cp.wait()
            part = act.at[(k % slots) * 128 : (k % slots + 1) * 128]
            part[:, : rows.shape[1]] = rows.astype(bf)
            pend.append(copies(part, end_sem.at[k % slots]))

        def up_copies(part, sem, r):
            out = []
            for ref, which in ((up_keep, core[0]), (up_send, 1 - core[0])):
                start = pl.multiple_of(which * half, half)
                out.append(pltpu.make_async_copy(part.at[:, pl.ds(start, half)], ref.at[r : r + 128, :], sem))
                out[-1].start()
            return out

        for r in range(0, D, 128):
            put(acc_up[r : r + 128, :], lambda part, sem, r=r: up_copies(part, sem, r))
        for r in range(0, D, 128):
            into = r % (D // 2)
            put(
                acc_dn[r : r + 128, :],
                lambda part, sem, r=r, into=into: to_side(
                    part, dn_keep.at[into : into + 128, :], dn_send.at[into : into + 128, :], core[0] == r // (D // 2), sem
                ),
            )
        for r in range(0, D, 128):
            put(
                acc_out[r : r + 128, :],
                lambda part, sem, r=r: to_side(
                    part.at[:, :D], vo_keep.at[r : r + 128, :], vo_send.at[r : r + 128, :], core[0] == 1, sem
                ),
            )
        small[...] = jnp.sum(accs[...], axis=1)
        small_up[...] = jnp.sum(accu[...], axis=0, keepdims=True)
        for group in pend[-slots:]:
            for cp in group:
                cp.wait()
        for cp in out_copies(0, (out_s, dr_s, do_s)):
            cp.wait()


def dense(core, x_l, x_s, o_l, o_s, c_l, c_s, w_out, w_up, w_down, vecs, bu, tile=512, chunk=1536):
    nl, ns = x_l.shape[0] // tile, x_s.shape[0] // tile
    tl, ts = x_l.shape[0], x_s.shape[0]
    return pl.pallas_call(
        functools.partial(dense_kernel, nl, tile, chunk),
        grid=(nl + ns,),
        in_specs=[SMEM_SPEC]
        + [ANY_SPEC] * 6
        + [const_spec((D, D)), const_spec((D, FF)), const_spec((FF, D))]
        + [const_spec((8, D)), const_spec((1, FF))],
        out_specs=[ANY_SPEC] * 12 + [const_spec((6, D)), const_spec((1, FF))],
        out_shape=[sds((tl, D), bf), sds((ts, D), bf), sds((tl, D), f32), sds((ts, D), f32)]
        + [sds((D, tl), bf), sds((D, ts), bf), sds((D, FF // 2), bf), sds((D, FF // 2), bf)]
        + [sds((D // 2, FF), bf), sds((D // 2, FF), bf), sds((D, D), bf), sds((D, D), bf)]
        + [sds((6, D), f32), sds((1, FF), f32)],
        scratch_shapes=[
            pltpu.VMEM((D, FF), f32),
            pltpu.VMEM((D, FF), f32),
            pltpu.VMEM((D, D), f32),
            pltpu.VMEM((tile, FF), bf),
            pltpu.VMEM((tile, FF), f32),
            pltpu.VMEM((6, 8, D), f32),
            pltpu.VMEM((8, FF), f32),
            pltpu.VMEM((2, tile, D), bf),
            pltpu.VMEM((2, D, tile), bf),
            pltpu.VMEM((2, tile, D), bf),
            pltpu.VMEM((tile, D), bf),
            pltpu.VMEM((tile, D), f32),
            pltpu.VMEM((D, tile), bf),
            pltpu.SemaphoreType.DMA((3, 2)),
            pltpu.SemaphoreType.DMA((3,)),
            pltpu.SemaphoreType.DMA((tile // 128,)),
        ],
        compiler_params=params(),
        cost_estimate=cost(2 * (tl + ts) * (3 * D * D + 6 * D * FF), 60e6, (tl + ts) * FF),
        name="dense",
    )(core, x_l, x_s, o_l, o_s, c_l, c_s, w_out, w_up, w_down, vecs, bu)


def back_f_group(lk_g, w_g, q_g, up_g):
    rows = q_g.shape[1]
    probs = head_softmax(dot(spread_heads(lk_g * SCALE), q_g, 1, 0))
    dw = pick_heads(dot(probs.astype(bf), up_g, 1, 1))
    dprobs = dot(spread_heads(w_g), up_g, 1, 0)
    weighted = jnp.sum((probs * dprobs).reshape(4, LM, rows), axis=1, keepdims=True)
    dsf = (probs * (dprobs.reshape(4, LM, rows) - weighted).reshape(GROUP, rows)).astype(bf)
    return dw, dsf, SCALE * pick_heads(dot(dsf, q_g, 1, 1))


def back_f_kernel(units, lk, w, q, up, dw_out, dlk_out, dsf_out, edges):
    w_all = joined(w, units, slice(0, LM))
    rows = q.shape[1]
    edges[0] = jnp.concatenate([up[:, :HALF], up[:, rows - HALF :]], axis=1).T
    dws = []
    for gs in group_slices():
        dw, dsf_out[gs, :], dlk_out[:, gs] = back_f_group(lk[:, gs], w_all[:, gs], q[gs, :], up[gs, :])
        dws.append(dw)
    dws = jnp.concatenate(dws, axis=1)
    width = D // units
    for u in range(units):
        dw_out[u] = dws[:, u * width : (u + 1) * width]


def back_f(lk, w, q, up, items, units):
    rows = q.shape[1] // items
    mark, tok = item_specs(rows)
    width = D // units
    return pl.pallas_call(
        functools.partial(back_f_kernel, units),
        grid=(items,),
        in_specs=[mark, unit_spec(units, LM + 16, width), tok, tok],
        out_specs=[unit_spec(units, LM, width), mark, tok, pl.BlockSpec((1, 2 * HALF, D), lambda i: (i, 0, 0))],
        out_shape=[
            sds((items * units, LM, width), f32),
            sds((items * LM, D), f32),
            sds(q.shape, bf),
            sds((items, 2 * HALF, D), bf),
        ],
        compiler_params=params(),
        cost_estimate=cost(8 * items * rows * D * GROUP, 6 * items * rows * D, items * rows * D),
        name="back_f",
    )(lk, w, q, up)


def back_mix_kernel(senders, dw_in, z, bv, out, dw_out):
    width = z.shape[1]
    dw = dw_in[0]
    for d in range(1, senders):
        dw = dw + dw_in[d]
    dw_out[...] = dw
    dbvs, dots = [], []
    for s in head_slices(width // HD):
        dbv = mm(z[:, s], dw[:, s], 0, 0).astype(bf)
        dots.append(jnp.sum(dbv.astype(f32) * bv[:, s], axis=1, keepdims=True))
        dbvs.append(dbv)
    put_all(out, jnp.concatenate(dbvs, axis=1), three_parts(lanes_of([jnp.concatenate(dots, axis=0)])[:1]))


def back_mix(dw, z, bv, deps=()):
    senders, _, width = dw.shape
    return pl.pallas_call(
        after(functools.partial(back_mix_kernel, senders), 3, deps),
        in_specs=[VMEM_SPEC] * 3 + [ANY_SPEC] * len(deps),
        out_specs=[VMEM_SPEC] * 2,
        out_shape=[sds((senders, LM + 16, width), bf), sds((LM, width), f32)],
        compiler_params=params(),
        cost_estimate=cost(1e8, 4e6),
        name="back_mix",
    )(dw, z, bv, *deps)


def back_inverse_kernel(at, lq_l, lk_l, lq_s, lk_s, dw_l, bv_l, dw_s, bv_s, dlq_l, dlk_l, dlq_s, dlk_s):
    qs, ks, dws, bvs = (lq_l, lq_s), (lk_l, lk_s), (dw_l, dw_s), (bv_l, bv_s)
    heads = own_slices(lq_l, lq_s)
    a_list = [mark_probs(qs[n][:, s], ks[n][:, s]) for n, s in heads]
    kept = []
    inverse_steps(a_list, kept)
    ident = eye()
    dz = [mm(dws[n][:, s], bvs[n][:, s], 1, 1) for n, s in heads]
    da = [jnp.zeros((LM, LM), f32) for _ in heads]
    for z, p, t2, t3 in reversed(kept):
        dt3 = [0.25 * mm(zz, d, 0, 0) for zz, d in zip(z, dz)]
        dz = [0.25 * mm(d, t, 1, 1) for d, t in zip(dz, t3)]
        dp = [-mm(d, t, 1, 1) for d, t in zip(dt3, t2)]
        dt2 = [-mm(pp, d, 0, 0) for pp, d in zip(p, dt3)]
        dp = [x - mm(d, 7.0 * ident - pp, 1, 1) for x, d, pp in zip(dp, dt2, p)]
        dp = [x + mm(pp, d, 0, 0) for x, pp, d in zip(dp, p, dt2)]
        da = [x + mm(d, zz, 1, 1) for x, d, zz in zip(da, dp, z)]
        dz = [x + mm(a, d, 0, 0) for x, a, d in zip(dz, a_list, dp)]
    for (n, s), a, g, d in zip(heads, a_list, da, dz):
        col, row, cm, rm = inverse_start(a)
        norm = cm * rm
        g = g + d.T / norm
        dnorm = -jnp.sum(jnp.sum(d.T * a, axis=1, keepdims=True), axis=0, keepdims=True) / (norm * norm)
        at_col = (col == cm).astype(f32)
        at_row = (row == rm).astype(f32)
        g = g + dnorm * rm * at_col / jnp.sum(at_col, axis=1, keepdims=True)
        g = g + dnorm * cm * at_row / jnp.sum(at_row, axis=0, keepdims=True)
        ds = a * (g - jnp.sum(a * g, axis=1, keepdims=True))
        (dlq_l, dlq_s)[n][:, s] = SCALE * mm(ds, ks[n][:, s].astype(f32))
        (dlk_l, dlk_s)[n][:, s] = SCALE * mm(ds, qs[n][:, s].astype(f32), 0, 0)


def back_inverse(at, lq_l, lk_l, lq_s, lk_s, dw_l, bv_l, dw_s, bv_s, deps=()):
    width = dw_l.shape[1]
    own = pl.BlockSpec((LM, width), lambda i, at: (at[0], at[1]))
    one, all_heads = whole((LM, width)), whole((LM, D))
    return pl.pallas_call(
        after(back_inverse_kernel, 9, deps),
        grid_spec=pltpu.PrefetchScalarGridSpec(
            num_scalar_prefetch=1,
            grid=(1,),
            in_specs=[own, own, all_heads, all_heads, one, one, all_heads, all_heads] + [ANY_SPEC] * len(deps),
            out_specs=[one, one, all_heads, all_heads],
        ),
        out_shape=[sds((LM, width), f32)] * 2 + [sds((LM, D), f32)] * 2,
        compiler_params=params(),
        cost_estimate=cost((width + D) // HD * 72 * 3 * 2 * 64**3 * 20, 2e6),
        name="back_inverse",
    )(at, lq_l, lk_l, lq_s, lk_s, dw_l, bv_l, dw_s, bv_s, *deps)


def back_b_group(k_g, v_g, wide, dots, probs):
    dsb = (probs * (dot(wide, v_g, 1, 0) - dots)).astype(bf)
    return dsb, SCALE * pick_heads(dot(dsb, k_g, 1, 1))


def back_b_kernel(units, lq, w, dbv, k, v, dsb_out, probs_out, dlq_out):
    level = from_parts(joined(w, units, slice(LM, LM + 16)))
    dots = from_parts(joined(dbv, units, slice(LM, LM + 16)))
    dbv_all = joined(dbv, units, slice(0, LM))
    for gs in group_slices():
        probs = jnp.exp(mark_scores(lq[:, gs], k[gs, :], None) - level[gs])
        probs_out[gs, :] = probs.astype(bf)
        dsb_out[gs, :], dlq_out[:, gs] = back_b_group(
            k[gs, :], v[gs, :], spread_heads(dbv_all[:, gs]), dots[gs], probs
        )


def back_b(lq, w, dbv, k, v, items, units, deps=()):
    rows = k.shape[1] // items
    mark, tok = item_specs(rows)
    unit = unit_spec(units, LM + 16, D // units)
    return pl.pallas_call(
        after(functools.partial(back_b_kernel, units), 5, deps),
        grid=(items,),
        in_specs=[mark, unit, unit, tok, tok] + [ANY_SPEC] * len(deps),
        out_specs=[tok, tok, mark],
        out_shape=[sds(k.shape, bf), sds(k.shape, bf), sds((items * LM, D), f32)],
        compiler_params=params(),
        cost_estimate=cost(8 * items * rows * D * GROUP, 10 * items * rows * D, items * rows * D),
        name="back_b",
    )(lq, w, dbv, k, v, *deps)


def back_v_kernel(units, core, dbv, probs, dconv, x, gv_in, keep_in, send_in, dv_out, keep, send, acc, stage, sem):
    i = pl.program_id(0)

    @pl.when(i == 0)
    def _():
        acc[...] = gv_in[...]

    dbv_all = joined(dbv, units, slice(0, LM))
    for gs in group_slices():
        dv_out[gs, :] = (dot(spread_heads(dbv_all[:, gs]), probs[gs, :], 0, 0) + dconv[gs, :]).astype(bf)
    acc[...] += dot(dv_out[...], x[...], 1, 0)

    @pl.when(i == pl.num_programs(0) - 1)
    def _():
        stage[...] = acc[...].T.astype(bf)
        for cp in to_side(stage, keep, send, core[0] == 0, sem.at[0]):
            cp.wait()


def back_v(core, dbv, probs, dconv, x, gv, keep, send, items, units, deps=()):
    rows = probs.shape[1] // items
    _, tok = item_specs(rows)
    square = const_spec((D, D))
    return pl.pallas_call(
        after(functools.partial(back_v_kernel, units), 8, deps),
        grid=(items,),
        in_specs=[SMEM_SPEC, unit_spec(units, LM + 16, D // units), tok, tok]
        + [pl.BlockSpec((rows, D), lambda i: (i, 0)), square, ANY_SPEC, ANY_SPEC]
        + [ANY_SPEC] * len(deps),
        out_specs=[tok, ANY_SPEC, ANY_SPEC],
        out_shape=[sds(probs.shape, bf), sds((D, D), bf), sds((D, D), bf)],
        input_output_aliases={6: 1, 7: 2},
        scratch_shapes=[pltpu.VMEM((D, D), f32), pltpu.VMEM((D, D), bf), pltpu.SemaphoreType.DMA((1,))],
        compiler_params=params(),
        cost_estimate=cost(6 * items * rows * D * GROUP, 12 * items * rows * D),
        name="back_v",
    )(core, dbv, probs, dconv, x, gv, keep, send, *deps)


def short_back_kernel(length, q, k, v, lq, lk, z, w, bv, up, dconv, x, dsf_out, dsb_out, dv_out, dlq_out, dlk_out, dw_out, gv_out):
    for gs in group_slices():
        dw, dsf_out[gs, :], dlk_out[:, gs] = back_f_group(lk[:, gs], w[:, gs], q[gs, :], up[gs, :])
        dw_out[:, gs] = dw
        z_g, bv_g = z[:, gs], bv[:, gs]
        dbvs = [mm(z_g[:, s], dw[:, s], 0, 0).astype(bf) for s in head_slices(4)]
        dots = jnp.concatenate(
            [jnp.sum(d.astype(f32) * bv_g[:, s], axis=1, keepdims=True) for d, s in zip(dbvs, head_slices(4))], axis=0
        )
        scores = mark_scores(lq[:, gs], k[gs, :], length[0])
        e = jnp.exp(scores - jnp.max(scores, axis=1, keepdims=True))
        probs = e / jnp.sum(e, axis=1, keepdims=True)
        wide = spread_heads(jnp.concatenate(dbvs, axis=1))
        dsb_out[gs, :], dlq_out[:, gs] = back_b_group(k[gs, :], v[gs, :], wide, dots, probs)
        dv_out[gs, :] = (dot(wide, probs.astype(bf), 0, 0) + dconv[gs, :]).astype(bf)
    gv_out[...] = dot(dv_out[...], x[...], 1, 0)


def short_back(length, q, k, v, lq, lk, z, w, bv, up, dconv, x, deps=()):
    mark = sds((LM, D), f32)
    return pl.pallas_call(
        after(short_back_kernel, 12, deps),
        in_specs=[SMEM_SPEC] + [VMEM_SPEC] * 11 + [ANY_SPEC] * len(deps),
        out_specs=[VMEM_SPEC] * 7,
        out_shape=[sds(q.shape, bf)] * 3 + [mark] * 3 + [sds((D, D), f32)],
        compiler_params=params(),
        cost_estimate=cost(24 * q.size * GROUP, 20 * q.size, 2 * q.size),
        name="short_back",
    )(length, q, k, v, lq, lk, z, w, bv, up, dconv, x, *deps)


def score_part(member, x, lq, lk, dsf, dsb, sq, sk, dq_out, dk_out, acc):
    member2 = jnp.concatenate([member, member], axis=0)
    for n, (marks, scores, sums, out) in enumerate(((lk, dsf, sq, dq_out), (lq, dsb, sk, dk_out))):
        hi, lo = split(sums)
        back = dot(jnp.concatenate([hi, lo], axis=0), member2, 0, 0)
        for gs in group_slices():
            part = (dot(spread_heads(marks[:, gs] * SCALE), scores[gs, :], 0, 0) + back[gs]).astype(bf)
            out[gs, :] = part
    both = jnp.concatenate([dq_out[...], dk_out[...]], axis=0)
    acc[...] += dot(both, x[...], 1, 0)


def score_grads_kernel(n_long, length, core, x_l, lq_l, lk_l, dsf_l, dsb_l, sq_l, sk_l,
                       x_s, lq_s, lk_s, dsf_s, dsb_s, sq_s, sk_s, sq_own, sk_own,
                       dq_l, dk_l, dq_s, dk_s, keep, send, acc, stage, sem):
    i = pl.program_id(0)

    @pl.when(i == 0)
    def _():
        acc[...] = jnp.zeros_like(acc)
        member = short_member(length[0], x_s.shape[0]).astype(bf)
        count = (length[0] // LM).astype(f32)
        sq, sk = (sq_s[...] + sq_own[...]) / count, (sk_s[...] + sk_own[...]) / count
        score_part(member, x_s, lq_s, lk_s, dsf_s, dsb_s, sq, sk, dq_s, dk_s, acc)

    @pl.when(i > 0)
    def _():
        count, rows = sq_l.shape[0], x_l.shape[0]
        member = (iota((count, rows), 1) // (LONG // LM) == iota((count, rows), 0)).astype(f32).astype(bf)
        score_part(member, x_l, lq_l, lk_l, dsf_l, dsb_l, sq_l[...], sk_l[...], dq_l, dk_l, acc)

    @pl.when(i == n_long)
    def _():
        jobs = [
            (lambda: acc[:D, :], lambda src, sem: to_side(src, keep, send, core[0] == 0, sem)),
            (lambda: acc[D:, :], lambda src, sem: to_side(src, keep, send, core[0] == 1, sem)),
        ]
        put_bf16(jobs, stage, sem)


def score_grads(length, core, long_args, short_args, items, deps=()):
    x_l, x_s = long_args[0], short_args[0]
    tl, ts = x_l.shape[0], x_s.shape[0]
    rows = tl // items
    marks_l = long_args[5].shape[0] // items
    at = lambda i: jnp.maximum(i - 1, 0)
    first = lambda i: 0

    def specs(r, marks, f):
        row = pl.BlockSpec((r, D), lambda i: (f(i), 0))
        mark = pl.BlockSpec((LM, D), lambda i: (f(i), 0))
        tok = pl.BlockSpec((D, r), lambda i: (0, f(i)))
        own = pl.BlockSpec((marks, D), lambda i: (f(i), 0))
        return [row, mark, mark, tok, tok, own, own]

    long_out = pl.BlockSpec((D, rows), lambda i: (0, at(i)))
    short_out = pl.BlockSpec((D, ts), lambda i: (0, 0))
    return pl.pallas_call(
        after(functools.partial(score_grads_kernel, items), 18, deps),
        grid=(items + 1,),
        in_specs=[SMEM_SPEC, SMEM_SPEC]
        + specs(rows, marks_l, at)
        + specs(ts, LM, first)
        + [const_spec((LM, D))] * 2
        + [ANY_SPEC] * len(deps),
        out_specs=[long_out] * 2 + [short_out] * 2 + [ANY_SPEC] * 2,
        out_shape=[sds((D, tl), bf)] * 2 + [sds((D, ts), bf)] * 2 + [sds((D, D), bf)] * 2,
        scratch_shapes=[
            pltpu.VMEM((2 * D, D), f32),
            pltpu.VMEM((2, D, D), bf),
            pltpu.SemaphoreType.DMA((2,)),
        ],
        compiler_params=params(),
        cost_estimate=cost(6 * (tl + ts) * D * D, 20 * (tl + ts) * D),
        name="score_grads",
    )(length, core, *long_args, *short_args, *deps)


def input_grad_kernel(n_long, dr_l, dq_l, dk_l, dv_l, dr_s, dq_s, dk_s, dv_s, wq, wk, wv, out_l, out_s, w_all):
    i = pl.program_id(0)
    is_long = i < n_long
    @pl.when(i == 0)
    def _():
        for j, w in enumerate((wq, wk, wv)):
            w_all[:, j * D : (j + 1) * D] = w[...]

    grad = jnp.concatenate(
        [jnp.where(is_long, a[...], b[...]) for a, b in ((dq_l, dq_s), (dk_l, dk_s), (dv_l, dv_s))], axis=0
    )
    total = jnp.where(is_long, dr_l[...], dr_s[...]) + dot(grad, w_all[...], 0, 1)
    total = total.astype(bf)

    @pl.when(is_long)
    def _():
        out_l[...] = total

    @pl.when(jnp.logical_not(is_long))
    def _():
        out_s[...] = total


def input_grad(long_args, short_args, weights, deps=()):
    tl, ts = long_args[0].shape[0], short_args[0].shape[0]
    nl = tl // ts
    at = lambda i: jnp.minimum(i, nl - 1)
    row = lambda f: pl.BlockSpec((ts, D), lambda i: (f(i), 0))
    col = lambda f: pl.BlockSpec((D, ts), lambda i: (0, f(i)))
    first = lambda i: 0
    return pl.pallas_call(
        after(functools.partial(input_grad_kernel, nl), 11, deps),
        grid=(nl + 1,),
        in_specs=[row(at)] + [col(at)] * 3 + [row(first)] + [col(first)] * 3 + [const_spec((D, D))] * 3
        + [ANY_SPEC] * len(deps),
        out_specs=[row(at), row(first)],
        out_shape=[sds((tl, D), bf), sds((ts, D), bf)],
        scratch_shapes=[pltpu.VMEM((D, 3 * D), bf)],
        compiler_params=params(),
        cost_estimate=cost(6 * (tl + ts) * D * D, 12 * (tl + ts) * D),
        name="input_grad",
    )(*long_args, *short_args, *weights, *deps)


def swap(values, axis, bit):
    count = lax.axis_size(axis)
    return lax.ppermute(values, axis, [(i, i ^ bit) for i in range(count)])


def side(axis, bit):
    return (lax.axis_index(axis) // bit) % 2


def exchange(values):
    return lax.all_to_all(values, "seq", 0, 0, tiled=True)


def gather(values):
    return exchange(jnp.broadcast_to(values[None], (lax.axis_size("seq"),) + values.shape))


def tied(values, dep):
    return lax.optimization_barrier(tuple(values) + (dep,))[:-1]


def is_small_mesh():
    return lax.axis_size("dp") == 4 and lax.axis_size("seq") == 8


def pair_sum(keep, send, axis, bit):
    return keep.astype(f32) + swap(send, axis, bit).astype(f32)


class Reduction:
    def __init__(self, keep, send, dim):
        self.dim, self.other = dim, 1 - dim
        self.core, self.x = side("dp", 1), side("dp", 2)
        v = pair_sum(keep, send, "dp", 1)
        if not is_small_mesh():
            self.theirs = v.astype(bf)
            return
        half = v.shape[self.other] // 2
        self.mine = lax.dynamic_slice_in_dim(v, self.x * half, half, self.other).astype(bf)
        self.theirs = lax.dynamic_slice_in_dim(v, (1 - self.x) * half, half, self.other).astype(bf)

    def wait_for(self, dep):
        if is_small_mesh():
            (self.mine,) = tied((self.mine,), dep)

    def over_x(self):
        if not is_small_mesh():
            self.value = self.theirs
            return self.value
        n_seq = lax.axis_size("seq")
        v = pair_sum(self.mine, self.theirs, "dp", 2).astype(bf)
        if self.dim == 0:
            v = v.reshape(n_seq, v.shape[0] // n_seq, v.shape[1])
        else:
            v = v.reshape(v.shape[0], n_seq, v.shape[1] // n_seq).transpose(1, 0, 2)
        self.value = v
        return v

    def over_seq(self):
        if not is_small_mesh():
            self.own = lax.psum_scatter(self.value, "seq", scatter_dimension=self.dim, tiled=True)
        else:
            self.own = jnp.sum(exchange(self.value).astype(f32), axis=0).astype(bf)
        return self.own

    def both(self):
        if not is_small_mesh():
            place = (jnp.arange(2) == self.core).astype(f32)[:, None, None]
            shares = lax.psum(self.own.astype(f32)[None] * place, "dp")
            return shares[0], shares[1]
        got = swap(self.own, "dp", 2)
        v = jnp.where(
            self.x == 0,
            jnp.concatenate([self.own, got], axis=self.other),
            jnp.concatenate([got, self.own], axis=self.other),
        )
        got = swap(v, "dp", 1)
        first = self.core == 0
        return jnp.where(first, v, got).astype(f32), jnp.where(first, got, v).astype(f32)


class Halving(Reduction):
    def __init__(self, keep, send, dim, order):
        if not is_small_mesh():
            super().__init__(keep, send, dim)
            return
        self.dim, self.other = dim, 1 - dim
        self.core, self.x = side("dp", 1), side("dp", 2)
        v = pair_sum(keep, send, "dp", 1)
        rows, n = v.shape
        if dim == 0:
            v = v.reshape(2, 2, 2, rows // 8, n)
        else:
            v = v.reshape(rows, 8, n // 8).transpose(1, 0, 2).reshape(2, 2, 2, rows, n // 8)
        self.left = ["z1", "z0", "y"]
        self.order = list(order)
        self.split(v)

    def split(self, v):
        step = self.order[0]
        if step == "x":
            dim = v.ndim - 1 if self.dim == 0 else v.ndim - 2
            bit = self.x
            size = v.shape[dim] // 2
        else:
            dim = self.left.index(step)
            self.left.pop(dim)
            bit = side("seq", {"y": 1, "z0": 2, "z1": 4}[step])
            size = 1
        take = lambda at: lax.dynamic_slice_in_dim(v, at * size, size, dim).astype(bf)
        self.mine, self.theirs = take(bit), take(1 - bit)
        if step != "x":
            self.mine, self.theirs = (lax.squeeze(u, (dim,)) for u in (self.mine, self.theirs))

    def step(self):
        if not is_small_mesh():
            self.value = self.theirs
            return self.theirs
        axis, bit = {"x": ("dp", 2), "y": ("seq", 1), "z0": ("seq", 2), "z1": ("seq", 4)}[self.order.pop(0)]
        v = pair_sum(self.mine, self.theirs, axis, bit)
        if self.order:
            self.split(v)
            return self.theirs
        self.own = v.astype(bf)
        return self.own

    def last(self):
        if not is_small_mesh():
            self.step()
            return self.over_seq()
        return self.step()


def hold(value, dep):
    return tied((value,), dep)[0]


class SumStages:
    def __init__(self, values):
        self.values = values
        self.steps = [("dp", 1), ("dp", 2), ("seq", 4), ("seq", 2), ("seq", 1)]

    def step(self, dep):
        if is_small_mesh():
            axis, bit = self.steps.pop(0)
            held = hold(self.values, dep)
            self.values = held + swap(held, axis, bit)
        elif len(self.steps) == 5:
            self.steps.pop(0)
            self.values = lax.psum(self.values, ("dp", "seq"))
        return self.values


def neighbours(first, last):
    count = lax.axis_size("seq")
    right = lax.ppermute(first, "seq", [((i + 1) % count, i) for i in range(count)])
    left = lax.ppermute(last, "seq", [(i, (i + 1) % count) for i in range(count)])
    return left, right


def pad_units(values, count):
    have = values.shape[0]
    if have == count:
        return values
    return jnp.concatenate([values, jnp.zeros((count - have,) + values.shape[1:], values.dtype)], axis=0)


def body(x_long, x_short, item_start, short_lengths, w_query, w_key, w_value, w_out, conv_taps, ln1_gain, ln1_bias,
         w_up, up_bias, w_down, down_bias, ln2_gain, ln2_bias, cot_long, cot_short):
    _, items, rows, _ = x_long.shape
    short_rows = x_short.shape[3]
    seg = LONG // LM
    own_marks = rows // seg
    n_seq = lax.axis_size("seq")
    me = lax.axis_index("seq")
    heads_each = next(h for h in (2, 4, 6, 12) if H % h == 0 and items * H // h <= n_seq)
    units = H // heads_each
    width = heads_each * HD
    owners = items * units

    x_l = x_long.reshape(items * rows, D)
    x_s = x_short.reshape(short_rows, D)
    length = short_lengths.reshape(1)
    core = side("dp", 1).astype(jnp.int32).reshape(1)
    mine = jnp.minimum(me, owners - 1).astype(jnp.int32)
    at = jnp.stack([mine // units, mine % units])

    x_mean = jnp.sum(x_long[0].reshape(items, own_marks, seg, D).astype(f32), axis=2) * (1.0 / seg)
    means = gather(x_mean.reshape(items * own_marks, D))
    means = means.reshape(n_seq, items, own_marks, D).transpose(1, 0, 2, 3).reshape(items * LM, D)
    mean_hi, mean_lo = split(means)

    def marks_of(w):
        return (
            jnp.dot(mean_hi, w, preferred_element_type=f32) + jnp.dot(mean_lo, w, preferred_element_type=f32)
        ).astype(bf)

    place = (me - item_start[0]) % n_seq
    open_left = (place > 0)[:, None, None]
    open_right = (place < n_seq - 1)[:, None, None]

    def rims(left, right):
        return jnp.concatenate(
            [jnp.where(open_left, left, jnp.zeros_like(left)), jnp.where(open_right, right, jnp.zeros_like(right))], axis=1
        ).reshape(items * 2 * HALF, D)

    x_rim = rims(*neighbours(x_long[0, :, :HALF], x_long[0, :, rows - HALF :]))
    v_rim = jnp.einsum("ke,nk->en", w_value, x_rim, preferred_element_type=f32).astype(bf)

    tap_rows = jnp.stack([conv_taps.T, conv_taps[::-1].T], axis=1)
    tap_rows = jnp.pad(tap_rows, ((0, 0), (0, 6), (0, 128 - TAPS)))

    (k_l, v_l), (k_s, v_s), lk_s = project(length, x_l, x_s, (w_key, w_value))
    c_l, c_s = conv(length, v_l, v_s, v_rim, tap_rows, items)
    lq_l, lk_l = marks_of(w_query), marks_of(w_key)

    msg_l = stats(lq_l, k_l, v_l, items, units)
    (q_l,), (q_s,), lq_s = project(length, x_l, x_s, (w_query,), (msg_l,))
    got_l = exchange(pad_units(msg_l, n_seq))
    z_own, z_s = inverse(at, lq_l, lk_l, lq_s, lk_s, width)
    w_own, bv_own = combine(got_l, z_own)
    w_l = exchange(w_own)[:owners]
    o_s, w_s, bv_s = short_attend(length, q_s, k_s, v_s, lq_s, lk_s, z_s, c_s)
    o_l = mix(lk_l, w_l, q_l, c_l, items, units)

    vecs = jnp.pad(jnp.stack([ln1_gain, ln1_bias, down_bias, ln2_gain, ln2_bias]), ((0, 3), (0, 0)))
    out_l, out_s, dr_l, dr_s, do_l, do_s, up_keep, up_send, dn_keep, dn_send, vo_keep, vo_send, small, small_up = dense(
        core, x_l, x_s, o_l, o_s, cot_long.reshape(items * rows, D), cot_short.reshape(short_rows, D), w_out, w_up,
        w_down, vecs, up_bias.reshape(1, -1),
    )

    dw_l, dlk_part, dsf_l, edges = back_f(lk_l, w_l, q_l, do_l, items, units)
    got_dw = exchange(pad_units(dw_l, n_seq))
    up_keep, dn_keep = tied((up_keep, dn_keep), edges)
    up = Halving(up_keep, up_send, 0, ("x", "y", "z0", "z1"))
    down = Halving(dn_keep, dn_send, 1, ("y", "x", "z0", "z1"))
    do_rim = rims(*tied(neighbours(edges[:, :HALF], edges[:, HALF:]) + (up.theirs,), down.theirs)[:2]).T

    dc_l, dc_s, tap_g = conv_back(
        length, v_l, v_s, v_rim, do_l, do_s, do_rim, tap_rows, items, (up.theirs, down.theirs)
    )
    dsf_s, dsb_s, dv_s, dlq_s, dlk_s, dw_s, gv_s = short_back(
        length, q_s, k_s, v_s, lq_s, lk_s, z_s, w_s, bv_s, do_s, dc_s, x_s
    )
    packed = jnp.concatenate([small.reshape(-1), small_up.reshape(-1), tap_g[:, 0, :].reshape(-1)]).reshape(-1, 128)
    packed = SumStages(packed)
    dbv_own, dw_own = back_mix(got_dw, z_own, bv_own, (dv_s,))
    dbv_l = exchange(dbv_own)[:owners]
    dlq_own, dlk_own, dlq_own_s, dlk_own_s = back_inverse(
        at, lq_l, lk_l, lq_s, lk_s, dw_own, bv_own, dw_s, bv_s, (up.step(), down.step())
    )
    dsb_l, probs_l, dlq_part = back_b(
        lq_l, w_l, dbv_l, k_l, v_l, items, units, (up.step(), down.step(), packed.step(dw_own))
    )

    owned = (jnp.arange(owners) == me).astype(f32).reshape(items, units, 1, 1)

    def with_own(part, own):
        return part.reshape(items, LM, D) + (owned * own[None, None]).transpose(0, 2, 1, 3).reshape(items, LM, D)

    dl = jnp.stack([with_own(dlq_part, dlq_own), with_own(dlk_part, dlk_own)]).astype(bf)
    dl = dl.reshape(2 * items, n_seq, own_marks, D).transpose(1, 0, 2, 3)
    dv_l, vo_keep, vo_send = back_v(core, dbv_l, probs_l, dc_l, x_l, gv_s, vo_keep, vo_send, items, units, (dl,))
    dl = jnp.sum(exchange(dl).astype(f32), axis=0) * (1.0 / seg)
    dl = jnp.pad(dl.reshape(2, items, own_marks, D), ((0, 0), (0, 0), (0, 16 - own_marks), (0, 0)))
    dl = dl.reshape(2, items * 16, D)

    dq_l, dk_l, dq_s, dk_s, qk_keep, qk_send = score_grads(
        length,
        core,
        (x_l, lq_l, lk_l, dsf_l, dsb_l, dl[0], dl[1]),
        (x_s, lq_s, lk_s, dsf_s, dsb_s, dlq_s, dlk_s, dlq_own_s, dlk_own_s),
        items,
        (packed.step(dlq_part), dv_l),
    )
    query_key = Reduction(qk_keep, qk_send, 1)
    value_out = Halving(hold(vo_keep, dq_l), vo_send, 0, ("y", "z0", "z1", "x"))
    up.step()
    down.step()
    up.theirs, down.theirs = tied((up.theirs, down.theirs), dq_l)
    grad_l, grad_s = input_grad(
        (dr_l, dq_l, dk_l, dv_l),
        (dr_s, dq_s, dk_s, dv_s),
        (w_query, w_key, w_value),
        (query_key.theirs, value_out.theirs),
    )
    query_key.wait_for(grad_l)
    up.last()
    down.last()
    query_key.over_x()
    ready = query_key.value
    up.own, down.own = tied((up.own, down.own), ready)
    value_out.wait_for(ready)
    for _ in range(3):
        value_out.step()
        packed.step(value_out.theirs)
    value_out.last()
    query_key.over_seq()
    up_a, up_b = up.both()
    down_a, down_b = down.both()
    v_a, v_b = value_out.both()
    q_g, k_g = query_key.both()

    packed = packed.values.reshape(-1)
    small = packed[: 6 * D].reshape(6, D)
    small_up = packed[6 * D : 6 * D + FF]
    taps_g = packed[6 * D + FF :].reshape(H, 128)[:, :TAPS].T

    return (
        out_l.reshape(x_long.shape),
        out_s.reshape(x_short.shape),
        grad_l.reshape(x_long.shape),
        grad_s.reshape(x_short.shape),
        q_g.T,
        k_g.T,
        v_a,
        v_b,
        taps_g,
        small[0],
        small[1],
        jnp.concatenate([up_a, up_b], axis=1),
        small_up,
        jnp.concatenate([down_a, down_b], axis=0).T,
        small[2],
        small[4],
        small[5],
    )


def solution(mesh):
    tokens = P("dp", None, "seq", None)
    shorts = P("dp", "seq", None, None, None)
    rows = P("seq", None)
    return jax.shard_map(
        body,
        mesh=mesh,
        in_specs=(tokens, shorts, P("dp", None), P("dp", "seq", None)) + (P(),) * 13 + (tokens, shorts),
        out_specs=(tokens, shorts, tokens, shorts, rows, rows, rows, rows, P(), P(), P(), rows, P(), rows, P(), P(), P()),
        check_vma=False,
    )
```
